128 devices in a mesh: dp: 16 (over y, x_hi, core), seq: 8 (over x_lo, z).
Axes of the slice: x: 4 (x_hi: 2, x_lo: 2; x = x_hi * 2 + x_lo), y: 4, z: 4, core: 2. Of those that a mesh axis runs over, the one named last changes fastest.
Arguments:
- residual_input: bfloat16 [16, 32768, 512], P('dp', 'seq'), may hold values from -6 to 6
- mel_input_frames: bfloat16 [16, 128, 80], P('dp', 'seq'), may hold values from -6 to 6
- starts: int32 [16, 3], P('dp'), may hold values from 1 to 32767, as said below
- resets: int32 [16, 32768], P('dp', 'seq'), may hold values 0 or 1
- residual_gradient: bfloat16 [16, 32768, 512], P('dp', 'seq'), may hold values from -6 to 6
- skip_gradient: bfloat16 [16, 32768, 512], P('dp', 'seq'), may hold values from -6 to 6
- first_upsample_weight: bfloat16 [80, 2560], P(None, ('dp', 'seq')), may hold values from -0.5 to 0.5
- second_upsample_weight: bfloat16 [80, 2560], P(None, ('dp', 'seq')), may hold values from -0.5 to 0.5
- conditioning_weight: bfloat16 [80, 1024], P(None, ('dp', 'seq')), may hold values from -0.625 to 0.625
- dilated_weight: bfloat16 [1024, 1024], P(('dp', 'seq')), may hold values from -0.1875 to 0.1875
- gate_bias_vector: bfloat16 [1024], P(('dp', 'seq')), may hold values from -3 to 3
- output_weight: bfloat16 [512, 1024], P(None, ('dp', 'seq')), may hold values from -0.5 to 0.5
- output_bias_vector: bfloat16 [1024], P(('dp', 'seq')), may hold values from -2 to 2
Outputs:
- res_out: bfloat16 [16, 32768, 512], P('dp', 'seq')
- skip_out: bfloat16 [16, 32768, 512], P('dp', 'seq')
- res_grad: bfloat16 [16, 32768, 512], P('dp', 'seq')
- mel_grad: bfloat16 [16, 128, 80], P('dp', 'seq')
- up_first_grad: float32 [80, 2560], P(None, ('dp', 'seq'))
- up_second_grad: float32 [80, 2560], P(None, ('dp', 'seq'))
- cond_w_grad: float32 [80, 1024], P(None, ('dp', 'seq'))
- dil_w_grad: float32 [1024, 1024], P(('dp', 'seq'))
- gate_b_grad: float32 [1024], P(('dp', 'seq'))
- out_w_grad: float32 [512, 1024], P(None, ('dp', 'seq'))
- out_b_grad: float32 [1024], P(('dp', 'seq'))
The draws below stay inside these ranges and needn't reach their ends.
Inputs may be any that keep to these rules, and one draw needn't show every extreme that they name: In each row the starts rise strictly.
All inputs are finite; a program needn't handle non-finite values. No bound on the sum of `resets` on one device may be relied on, other than what follows from the above.
Results may differ from the reference program's by a relative error of at most 0.019.
Values may be sent and summed in bfloat16 or wider, within the bound.
No kernel may reach another device: no remote copies, remote signals or barrier semaphores. Data moves between devices by JAX's collectives and lax.ppermute only.
A program may use at most 192 MiB of HBM per device.

```python
import jax
import jax.numpy as jnp
from jax import lax

RESIDUAL_WIDTH = 512
GATE_CHANNELS = 1024
SK = 512
CM = 80
KUP = 32
DILATION_STEP = 64
UTTS = 4
HALF = 512
S_DEV = 4096
ROWS = 16
ROW_LEN = 32768
FRAMES = 128


def draw_starts(key, part):
    key = jax.random.fold_in(key, 11)

    def one_row(row_key):
        key_long, key_head, key_tail = jax.random.split(row_key, 3)
        long_index = jax.random.randint(key_long, (), 0, UTTS)
        head = 1 + jnp.sort(jax.random.permutation(key_head, S_DEV // 2 - 1)[:UTTS - 1])
        tail_rows = ROW_LEN - S_DEV // 2 + jnp.sort(jax.random.permutation(key_tail, S_DEV // 2)[:UTTS - 1])
        slots = jnp.arange(UTTS - 1)
        return jnp.where(slots < long_index, head, tail_rows).astype(jnp.int32)
    return jax.vmap(one_row)(jax.random.split(key, ROWS))


def touch_ends(array, stream_key, smallest, largest):
    longest = array.shape.index(max(array.shape))
    spots = []
    for shift in (0, 1):
        where = [jax.random.randint(jax.random.fold_in(stream_key, axis), (), 0, length) for axis, length in enumerate(array.shape)]
        where[longest] = (where[longest] + shift) % array.shape[longest]
        spots.append(tuple(where))
    return array.at[spots[0]].set(smallest).at[spots[1]].set(largest)


def level_of(own_key, dims, shards, low, largest):
    def one(axis_at, parts):
        steps = jax.random.uniform(jax.random.fold_in(jax.random.fold_in(own_key, 6), axis_at), (parts,), jnp.float32, low / len(shards), largest / len(shards))
        return jnp.repeat(jnp.exp(steps), dims[axis_at] // parts).reshape((-1,) + (1,) * (len(dims) - axis_at - 1))

    loudness = one(*shards[0])
    for cut in shards[1:]:
        loudness = loudness * one(*cut)
    return loudness


def gaussian(own_key, shape, spread, limit, cuts=(), kind=jnp.bfloat16):
    factor_of = level_of(own_key, shape, cuts, -0.22, 0.18) if cuts else 1.0
    result = jax.random.normal(own_key, shape, jnp.float32) * spread * factor_of
    return jnp.minimum(jnp.maximum(result, -limit), limit).astype(kind)


def setup_inputs(seed: int = 0) -> dict:
    keys = jax.random.split(jax.random.key(seed), 14)
    return {
        "residual_input": gaussian(keys[0], (ROWS, ROW_LEN, RESIDUAL_WIDTH), 1.0, 6.0, ((0, 16), (1, 8))),
        "mel_input_frames": gaussian(keys[1], (ROWS, FRAMES, CM), 1.0, 6.0, ((0, 16), (1, 8))),
        "starts": draw_starts(jax.random.fold_in(keys[13], 71), 0),
        "resets": touch_ends((jax.random.randint(keys[3], (ROWS, ROW_LEN), 0, 8) < 7).astype(jnp.int32), jax.random.fold_in(keys[3], 1), 0, 1),
        "residual_gradient": gaussian(keys[4], (ROWS, ROW_LEN, RESIDUAL_WIDTH), 1.0, 6.0, ((0, 16), (1, 8))),
        "skip_gradient": gaussian(keys[5], (ROWS, ROW_LEN, SK), 1.0, 6.0, ((0, 16), (1, 8))),
        "first_upsample_weight": gaussian(keys[6], (CM, KUP * CM), (2 * CM) ** -0.5, 0.5, ((1, 128),)),
        "second_upsample_weight": gaussian(keys[7], (CM, KUP * CM), (2 * CM) ** -0.5, 0.5, ((1, 128),)),
        "conditioning_weight": gaussian(keys[8], (CM, GATE_CHANNELS), CM ** -0.5, 0.625, ((1, 128),)),
        "dilated_weight": gaussian(keys[9], (2 * RESIDUAL_WIDTH, GATE_CHANNELS), (2 * RESIDUAL_WIDTH) ** -0.5, 0.1875, ((0, 128),)),
        "gate_bias_vector": gaussian(keys[10], (GATE_CHANNELS,), 0.5, 3.0, ((0, 128),)),
        "output_weight": gaussian(keys[11], (HALF, RESIDUAL_WIDTH + SK), (HALF // 4) ** -0.5, 0.5, ((1, 128),)),
        "output_bias_vector": gaussian(keys[12], (RESIDUAL_WIDTH + SK,), 0.3, 2.0, ((0, 128),)),
    }


@jax.custom_vjp
def low(v):
    return lax.optimization_barrier(v.astype(jnp.bfloat16)).astype(jnp.float32)

@jax.custom_vjp
def low_back(v):
    return v

def low_keep(v):
    return (low(v), None)

def low_pass(kept, grad):
    return (grad,)

def back_keep(v):
    return (v, None)

def back_low(kept, grad):
    return (low(grad),)
low.defvjp(low_keep, low_pass)
low_back.defvjp(back_keep, back_low)

def matrix_product(left, right):
    return jnp.dot(left, right, precision=lax.Precision.HIGHEST, preferred_element_type=jnp.float32)

def upsample(rows, weight_tuple):
    half = KUP // 2
    width = weight_tuple.shape[1] // KUP
    extended = jnp.concatenate([jnp.zeros((1, rows.shape[1]), jnp.float32), rows], 0)
    product = matrix_product(extended, weight_tuple).reshape(extended.shape[0], KUP, width)
    return (product[1:, :half] + product[:-1, half:]).reshape(-1, width)

def row_forward(layer_parameters, audio_samples, mel_rows, row_start_flag, reset_row_flag):
    first_upsample_matrix, second_upsample_matrix, conditioning_matrix, dilated_matrix, gate_bias_term, output_matrix, output_bias_term = layer_parameters
    inter = low_back(low(upsample(mel_rows, first_upsample_matrix)))
    conditioning_upsampled = low_back(low(upsample(inter, second_upsample_matrix)))
    sample_positions = jnp.arange(ROW_LEN, dtype=jnp.int32)
    crossed_boundary = jnp.any((row_start_flag[None, :] > sample_positions[:, None] - DILATION_STEP) & (row_start_flag[None, :] <= sample_positions[:, None]), axis=1)
    keep_mask = jnp.where(crossed_boundary | (sample_positions < DILATION_STEP), jnp.float32(0.0), reset_row_flag.astype(jnp.float32))
    shifted_samples = jnp.concatenate([jnp.zeros((DILATION_STEP, RESIDUAL_WIDTH), jnp.float32), audio_samples[:-DILATION_STEP]], 0)
    past_samples = low_back(shifted_samples * keep_mask[:, None])
    gate_preactivation = matrix_product(past_samples, dilated_matrix[:RESIDUAL_WIDTH]) + matrix_product(audio_samples, dilated_matrix[RESIDUAL_WIDTH:]) + matrix_product(conditioning_upsampled, conditioning_matrix) + gate_bias_term
    gate_preactivation = low_back(gate_preactivation)
    gated = low(jnp.tanh(gate_preactivation[:, :HALF]) * jax.nn.sigmoid(gate_preactivation[:, HALF:]))
    out = matrix_product(gated, output_matrix) + output_bias_term
    return (audio_samples + out[:, :RESIDUAL_WIDTH], out[:, RESIDUAL_WIDTH:])

def reference(residual_input, mel_input_frames, starts, resets, residual_gradient, skip_gradient, first_upsample_weight, second_upsample_weight, conditioning_weight, dilated_weight, gate_bias_vector, output_weight, output_bias_vector):
    layer_parameters = tuple((parameter_entry.astype(jnp.float32) for parameter_entry in (first_upsample_weight, second_upsample_weight, conditioning_weight, dilated_weight, gate_bias_vector, output_weight, output_bias_vector)))
    checked_row = jax.checkpoint(row_forward)

    def forward(audio_all, mel_all, weight_tuple):

        def step(carry, item):
            return (carry, checked_row(weight_tuple, item[0], item[1], item[2], item[3]))
        unused, outputs = lax.scan(step, jnp.float32(0.0), (audio_all, mel_all, starts, resets))
        return outputs
    outputs, pull = jax.vjp(forward, residual_input.astype(jnp.float32), mel_input_frames.astype(jnp.float32), layer_parameters)
    d_audio, d_mel, d_params = pull((residual_gradient.astype(jnp.float32), skip_gradient.astype(jnp.float32)))
    return (outputs[0].astype(jnp.bfloat16), outputs[1].astype(jnp.bfloat16), d_audio.astype(jnp.bfloat16), d_mel.astype(jnp.bfloat16), d_params[0], d_params[1], d_params[2], d_params[3], d_params[4], d_params[5], d_params[6])
```

```python
import jax
import jax.numpy as jnp
from jax import lax
from jax.experimental import pallas as pl
from jax.experimental.pallas import tpu as pltpu
from jax.sharding import Mesh, PartitionSpec as P

STEP = 64
SEQ = ("xl", "z")
CHIPS = ("y", "xh", "xl", "z")
BF16 = jnp.bfloat16
F32 = jnp.float32
LANES = 128
TAPS = 32
HALF_TAPS = 16
CM = 80
SHARE = 20
LINES = 144
VMEM_BYTES = 60 * 1024 * 1024


def dot(a, b):
    return jnp.dot(a, b, preferred_element_type=F32)


def dot_nt(a, b):
    return lax.dot_general(a, b, (((1,), (1,)), ((), ())), preferred_element_type=F32)


def dot_tn(a, b):
    return lax.dot_general(a, b, (((0,), (0,)), ((), ())), preferred_element_type=F32)


def lane_mask(rows):
    return lax.broadcasted_iota(jnp.int32, (rows, LANES), 1) < CM


def turn_kernel(past, audio, res_grad, skip_grad, xt, gt):
    half = past.shape[1]
    xt[:half, :] = past[...].T
    xt[half:, :] = audio[...].T
    gt[:half, :] = res_grad[...].T
    gt[half:, :] = skip_grad[...].T


def turn(past, audio, res_grad, skip_grad, tile):
    samples, width = past.shape
    rows = pl.BlockSpec((tile, width), lambda i: (i, 0))
    cols = pl.BlockSpec((2 * width, tile), lambda i: (0, i))
    shape = jax.ShapeDtypeStruct((2 * width, samples), BF16)
    return pl.pallas_call(
        turn_kernel,
        grid=(samples // tile,),
        in_specs=[rows] * 4,
        out_specs=[cols, cols],
        out_shape=[shape, shape],
        compiler_params=pltpu.CompilerParams(vmem_limit_bytes=VMEM_BYTES),
        cost_estimate=pl.CostEstimate(flops=0, bytes_accessed=16 * samples * width, transcendentals=0),
    )(past, audio, res_grad, skip_grad)


def main_kernel(
    core, mel_a, mel_b, past, audio, g_res, g_skip, xt, gt, head_mask, g_sum, wd, wot, wct, u1t, u2t,
    dp_out, gated_out, stay, send, halo, mel_here,
    wc, inter, cond_all, dcond_all, dinter, dwg, owg, cwg, du,
):
    step = pl.program_id(0)
    tile = audio.shape[0]
    half = audio.shape[1]
    frames = cond_all.shape[0] // HALF_TAPS
    first_rows = mel_a.shape[0]

    @pl.when(step == 0)
    def _():
        wc[...] = wct[...].T
        keep = lane_mask(first_rows)
        for r in range(HALF_TAPS):
            here = dot_nt(mel_a[...], u1t[pl.ds(CM * r, LANES), :])
            before = dot_nt(mel_b[...], u1t[pl.ds(CM * (r + HALF_TAPS), LANES), :])
            rounded = jnp.where(keep, here + before, 0.0).astype(BF16).astype(F32)
            inter[pl.ds(r, first_rows, stride=HALF_TAPS), :] = rounded
        rows_a = inter[pl.ds(HALF_TAPS, frames), :].astype(BF16)
        rows_b = inter[pl.ds(HALF_TAPS - 1, frames), :].astype(BF16)
        lane = lax.broadcasted_iota(jnp.int32, (frames, LANES), 1)
        one = jnp.where(lane == CM, 1.0, 0.0)
        for r in range(HALF_TAPS):
            here = dot_nt(rows_a, u2t[pl.ds(CM * r, LANES), :])
            before = dot_nt(rows_b, u2t[pl.ds(CM * (r + HALF_TAPS), LANES), :])
            cond_all[pl.ds(r, frames, stride=HALF_TAPS), :] = jnp.where(lane < CM, here + before, one)
        dwg[...] = jnp.zeros_like(dwg)
        owg[...] = jnp.zeros_like(owg)
        cwg[...] = jnp.zeros_like(cwg)
        cwg[CM + 1 : CM + 2, :] = g_sum[...]

    at = pl.multiple_of(step * tile, tile)
    cond = cond_all[pl.ds(at, tile), :].astype(BF16)
    pre = dot(past[...], wd[:half, :]) + dot(audio[...], wd[half:, :]) + dot(cond, wc[...])
    th = jnp.tanh(pre[:, :half])
    sg = 0.5 * jnp.tanh(0.5 * pre[:, half:]) + 0.5
    gated = (th * sg).astype(BF16)
    gated_out[...] = gated
    dg = dot(g_res[...], wot[:half, :]) + dot(g_skip[...], wot[half:, :])
    dgs = dg * sg
    dp = jnp.concatenate([dgs * (1.0 - th * th), dgs * th * (1.0 - sg)], 1).astype(BF16)
    dp_out[...] = dp
    dcond_all[pl.ds(at, tile), :] = dot(dp, wct[...])
    owg[...] += dot(gt[...], gated)
    dwg[...] += dot(xt[...], dp)
    cwg[...] += dot_tn(cond, dp)

    @pl.when(step == 0)
    def _():
        halo[:STEP, :] = (dp[:STEP, :].astype(F32) * head_mask[...]).astype(BF16)

    @pl.when(step == pl.num_programs(0) - 1)
    def _():
        rows_a = inter[pl.ds(HALF_TAPS, frames), :].astype(BF16)
        rows_b = inter[pl.ds(HALF_TAPS - 1, frames), :].astype(BF16)
        both = jnp.concatenate([rows_a, rows_b], 1)
        keep = lane_mask(frames)
        sum_a = jnp.zeros((frames, LANES), F32)
        sum_b = jnp.zeros((frames, LANES), F32)

        def put(grads, tap, first):
            for q in range(CM // SHARE):
                du[pl.ds((CM // SHARE * tap + q) * 2 * SHARE + first, SHARE), :] = grads[SHARE * q : SHARE * (q + 1)]

        for r in range(HALF_TAPS):
            e = jnp.where(keep, dcond_all[pl.ds(r, frames, stride=HALF_TAPS), :], 0.0).astype(BF16)
            grads = dot_tn(e, both)
            put(grads[:, :LANES], r, SHARE)
            put(grads[:, LANES:], r + HALF_TAPS, SHARE)
            sum_a += dot(e, u2t[pl.ds(CM * r, LANES), :])
            sum_b += dot(e, u2t[pl.ds(CM * (r + HALF_TAPS), LANES), :])
        dinter[...] = jnp.zeros_like(dinter)
        dinter[pl.ds(HALF_TAPS, frames), :] = sum_a
        dinter[pl.ds(HALF_TAPS - 1, frames), :] += sum_b
        mels = jnp.concatenate([mel_a[...], mel_b[...]], 1)
        keep = lane_mask(first_rows)
        mel_sum_a = jnp.zeros((first_rows, LANES), F32)
        mel_sum_b = jnp.zeros((first_rows, LANES), F32)
        for r in range(HALF_TAPS):
            f = jnp.where(keep, dinter[pl.ds(r, first_rows, stride=HALF_TAPS), :], 0.0).astype(BF16)
            grads = dot_tn(f, mels)
            put(grads[:, :LANES], r, 0)
            put(grads[:, LANES:], r + HALF_TAPS, 0)
            mel_sum_a += dot(f, u1t[pl.ds(CM * r, LANES), :])
            mel_sum_b += dot(f, u1t[pl.ds(CM * (r + HALF_TAPS), LANES), :])
        zero = jnp.zeros((1, LANES), F32)
        mel_sum = jnp.concatenate([zero, mel_sum_a], 0) + jnp.concatenate([mel_sum_b, zero], 0)
        real = mel_here.shape[0]
        mel_here[...] = mel_sum[2 : 2 + real]
        halo[STEP:, :] = jnp.zeros_like(halo[STEP:, :])
        halo[STEP:, :LANES] = jnp.concatenate([mel_sum[:2], jnp.zeros((14, LANES), F32)], 0).astype(BF16)
        cwgt = cwg[...].T
        dcond_all[: cwgt.shape[0], :] = cwgt

        def pack(a, _):
            for b in range(8):
                for out, side in ((stay, core[0]), (send, 1 - core[0])):
                    at_row = pl.multiple_of(a * 128 + side * 64 + b * 8, 8)
                    rows = pl.ds(at_row, 8)
                    place = a * 8 + b
                    for m in range(4):
                        two = [dwg[rows, pl.ds(256 * m, 128)], dwg[rows, pl.ds(256 * m + 128, 128)]]
                        out[place, pl.ds(16 * m, 16), :] = jnp.concatenate(two, 0).astype(BF16)
                    for m in range(2):
                        two = [owg[rows, pl.ds(256 * m, 128)], owg[rows, pl.ds(256 * m + 128, 128)]]
                        out[place, pl.ds(64 + 16 * m, 16), :] = jnp.concatenate(two, 0).astype(BF16)
                    du_row = pl.multiple_of(at_row * 5, 8)
                    rest = [dcond_all[rows, :], du[pl.ds(du_row, 2 * SHARE), :]]
                    out[place, pl.ds(96, 48), :] = jnp.concatenate(rest, 0).astype(BF16)
            return _

        lax.fori_loop(0, 8, pack, 0)


def main_pass(core, mel_a, mel_b, past, audio, g_res, g_skip, xt, gt, head_mask, g_sum, wd, wot, wct, u1t, u2t, tile):
    samples, width = audio.shape
    first_rows = mel_a.shape[0]
    rows = pl.BlockSpec((tile, width), lambda i: (i, 0))
    cols = pl.BlockSpec((2 * width, tile), lambda i: (0, i))

    def whole(shape):
        return pl.BlockSpec(shape, lambda i: (0,) * len(shape))

    fixed = [head_mask, g_sum, wd, wot, wct, u1t, u2t]
    packed = (64, LINES, LANES)
    outs = [
        ((samples, 2 * width), BF16),
        ((samples, width), BF16),
        (packed, BF16),
        (packed, BF16),
        ((STEP + 16, 2 * width), BF16),
        ((samples // (HALF_TAPS * HALF_TAPS), LANES), F32),
    ]
    return pl.pallas_call(
        main_kernel,
        grid=(samples // tile,),
        in_specs=[pl.BlockSpec(memory_space=pltpu.SMEM)]
        + [whole(mel_a.shape), whole(mel_b.shape), rows, rows, rows, rows, cols, cols]
        + [whole(a.shape) for a in fixed],
        out_specs=[
            pl.BlockSpec((tile, 2 * width), lambda i: (i, 0)),
            pl.BlockSpec((tile, width), lambda i: (i, 0)),
        ]
        + [whole(s) for s, _ in outs[2:]],
        out_shape=[jax.ShapeDtypeStruct(s, d) for s, d in outs],
        scratch_shapes=[
            pltpu.VMEM((LANES, 2 * width), BF16),
            pltpu.VMEM((first_rows * HALF_TAPS, LANES), F32),
            pltpu.VMEM((samples, LANES), F32),
            pltpu.VMEM((samples, LANES), F32),
            pltpu.VMEM((first_rows * HALF_TAPS, LANES), F32),
            pltpu.VMEM((2 * width, 2 * width), F32),
            pltpu.VMEM((2 * width, width), F32),
            pltpu.VMEM((LANES, 2 * width), F32),
            pltpu.VMEM((2 * TAPS * CM, LANES), F32),
        ],
        compiler_params=pltpu.CompilerParams(vmem_limit_bytes=VMEM_BYTES),
        cost_estimate=pl.CostEstimate(
            flops=28_000_000_000, bytes_accessed=48 * samples * width, transcendentals=0
        ),
    )(core, mel_a, mel_b, past, audio, g_res, g_skip, xt, gt, *fixed)


def add_kernel(a, b, after, out):
    out[...] = (a[...].astype(F32) + b[...].astype(F32)).astype(BF16)


def add_pair(a, b, after):
    block = pl.BlockSpec((8,) + a.shape[1:], lambda i: (i, 0, 0))
    return pl.pallas_call(
        add_kernel,
        grid=(a.shape[0] // 8,),
        in_specs=[block, block, pl.BlockSpec(memory_space=pl.ANY)],
        out_specs=block,
        out_shape=jax.ShapeDtypeStruct(a.shape, BF16),
    )(a, b, after)


def after_kernel(a, *rest):
    pass


def after(a, *others):
    anywhere = pl.BlockSpec(memory_space=pl.ANY)
    return pl.pallas_call(
        after_kernel,
        in_specs=[anywhere] * (1 + len(others)),
        out_specs=anywhere,
        out_shape=jax.ShapeDtypeStruct(a.shape, a.dtype),
        input_output_aliases={0: 0},
    )(a, *others)


def tail_kernel(dp, dp_next, dp_halo, gated, audio, g_res, mask, wd, wot, ob, res_out, skip_out, res_grad, wdt, wo):
    step = pl.program_id(0)
    tile, half = audio.shape

    @pl.when(step == 0)
    def _():
        wdt[...] = wd[...].T
        wo[...] = wot[...].T

    out = dot(gated[...], wo[...]) + ob[...]
    res_out[...] = (audio[...].astype(F32) + out[:, :half]).astype(BF16)
    skip_out[...] = out[:, half:].astype(BF16)
    last = step == pl.num_programs(0) - 1
    after = jnp.where(last, dp_halo[...], dp_next[...])
    ahead = jnp.concatenate([dp[STEP:, :], after], 0)
    d_past = dot(ahead, wdt[:, :half])
    kept = mask[...].astype(F32)
    kept = jnp.concatenate([kept] * (half // LANES), 1)
    d_now = dot(dp[...], wdt[:, half:])
    res_grad[...] = (g_res[...].astype(F32) + d_now + d_past * kept).astype(BF16)


def tail_pass(dp, dp_halo, gated, audio, g_res, mask, wd, wot, ob, tile):
    samples, width = audio.shape
    rows = pl.BlockSpec((tile, width), lambda i: (i, 0))
    step_blocks = tile // STEP
    final = samples // STEP - 1

    def whole(shape):
        return pl.BlockSpec(shape, lambda i: (0,) * len(shape))

    shape = jax.ShapeDtypeStruct((samples, width), BF16)
    return pl.pallas_call(
        tail_kernel,
        grid=(samples // tile,),
        in_specs=[
            pl.BlockSpec((tile, 2 * width), lambda i: (i, 0)),
            pl.BlockSpec((STEP, 2 * width), lambda i: (jnp.minimum((i + 1) * step_blocks, final), 0)),
            whole(dp_halo.shape),
            rows,
            rows,
            rows,
            pl.BlockSpec((tile, LANES), lambda i: (i, 0)),
            whole(wd.shape),
            whole(wot.shape),
            whole(ob.shape),
        ],
        out_specs=[rows] * 3,
        out_shape=[shape] * 3,
        scratch_shapes=[
            pltpu.VMEM((2 * width, 2 * width), BF16),
            pltpu.VMEM((width, 2 * width), BF16),
        ],
        compiler_params=pltpu.CompilerParams(vmem_limit_bytes=VMEM_BYTES),
        cost_estimate=pl.CostEstimate(
            flops=13_000_000_000, bytes_accessed=20 * samples * width, transcendentals=0
        ),
    )(dp, dp, dp_halo, gated, audio, g_res, mask, wd, wot, ob)


def shifted(value, steps, count=8):
    first, last = max(0, -steps), min(count, count - steps)
    return lax.ppermute(value, SEQ, [(s, s + steps) for s in range(first, last)])


def swap(value):
    return lax.ppermute(value, "c", [(0, 1), (1, 0)])


def lane_tiles(a):
    rows, width = a.shape
    return a.reshape(rows, width // LANES, LANES).transpose(1, 0, 2).reshape(-1, LANES)


def from_lane_tiles(a, tiles):
    return a.reshape(-1, tiles, 8, LANES).transpose(0, 2, 1, 3).reshape(-1, tiles * LANES)


def pad_lanes(a):
    return jnp.pad(a, ((0, 0), (0, LANES - a.shape[1])))


def on_device(
    residual_input, mel_input_frames, starts, resets, residual_gradient, skip_gradient,
    first_upsample_weight, second_upsample_weight, conditioning_weight, dilated_weight,
    gate_bias_vector, output_weight, output_bias_vector,
):
    core = lax.axis_index("c")
    audio, mel = residual_input[0], mel_input_frames[0]
    g_res, g_skip = residual_gradient[0], skip_gradient[0]
    samples, width = audio.shape
    frames = mel.shape[0]

    tails = jnp.concatenate([audio[-STEP:], jnp.pad(mel[-2:], ((0, 14), (0, width - CM)))], 0)
    tails = shifted(tails, 1)
    audio_tail, mel_tail = tails[:STEP], tails[STEP : STEP + 2, :CM]

    shard = jnp.concatenate(
        [
            lane_tiles(dilated_weight),
            lane_tiles(output_weight.T),
            pad_lanes(
                jnp.concatenate(
                    [conditioning_weight.T, gate_bias_vector[:, None], output_bias_vector[:, None]], 1
                )
            ),
            pad_lanes(first_upsample_weight.T),
            pad_lanes(second_upsample_weight.T),
        ],
        0,
    )
    own = lax.all_to_all(jnp.broadcast_to(shard[None], (64, LINES, LANES)), CHIPS, 0, 0)

    mel_ext = pad_lanes(jnp.concatenate([mel_tail, mel, jnp.zeros((14, CM), BF16)], 0))
    mel_b, mel_a = mel_ext[: 2 * frames - 8], mel_ext[1 : 2 * frames - 7]
    seq_at = lax.axis_index(SEQ)
    position = seq_at * samples + jnp.arange(samples, dtype=jnp.int32)
    crossed = jnp.any(
        (starts[0][None, :] > position[:, None] - STEP) & (starts[0][None, :] <= position[:, None]), axis=1
    )
    keep = jnp.where(crossed | (position < STEP), 0, resets[0]).astype(BF16)
    past = jnp.concatenate([audio_tail, audio[:-STEP]], 0) * keep[:, None]
    mask = jnp.broadcast_to(
        jnp.concatenate([keep[STEP:], jnp.ones((STEP,), BF16)])[:, None], (samples, LANES)
    )
    head_mask = jnp.broadcast_to(keep[:STEP, None].astype(F32), (STEP, 2 * width))
    xt, gt = turn(past, audio, g_res, g_skip, 512)
    g_sum = jnp.concatenate([jnp.sum(g_res.astype(F32), 0), jnp.sum(g_skip.astype(F32), 0)])[None]

    own = after(own, xt, gt, g_sum, mask, head_mask)
    other = swap(own)
    own = own.reshape(8, 8, LINES, LANES)
    other = other.reshape(8, 8, LINES, LANES)
    low, high = jnp.where(core == 0, own, other), jnp.where(core == 0, other, own)
    weights = jnp.stack([low, high], 1).reshape(128, LINES, LANES)
    wd = from_lane_tiles(weights[:, :64], 8)
    wot = from_lane_tiles(weights[:, 64:96], 4)
    wct = weights[:, 96:104].reshape(-1, LANES)
    u1t = jnp.pad(weights[:, 104:124].reshape(-1, LANES), ((0, 48), (0, 0)))
    u2t = jnp.pad(weights[:, 124:144].reshape(-1, LANES), ((0, 48), (0, 0)))

    dp, gated, stay, send, halo, mel_here = main_pass(
        core.astype(jnp.int32)[None],
        mel_a, mel_b, past, audio, g_res, g_skip, xt, gt, head_mask, g_sum, wd, wot, wct, u1t, u2t, 512,
    )

    came = swap(send)
    halo_next = shifted(halo, -1)
    pair = add_pair(stay, came, halo_next)
    all_parts = lax.all_to_all(pair, CHIPS, 0, 0)

    mel_back = halo_next[STEP : STEP + 2, :CM].astype(F32)
    mel_grad = mel_here[:, :CM] + jnp.pad(mel_back, ((frames - 2, 0), (0, 0)))
    ob = wct[:, CM + 1].astype(F32)[None]
    res_out, skip_out, res_grad = tail_pass(
        dp, halo_next[:STEP], gated, audio, g_res, mask, wd, wot, ob, 512
    )

    total = jnp.sum(all_parts.astype(F32), 0)
    return (
        res_out[None],
        skip_out[None],
        res_grad[None],
        mel_grad.astype(BF16)[None],
        total[104:124, :CM].T,
        total[124:144, :CM].T,
        total[96:104, :CM].T,
        total[:64].reshape(8, 8, LANES).transpose(1, 0, 2).reshape(8, 1024),
        total[96:104, CM],
        total[64:96].reshape(4, 8, LANES).transpose(1, 0, 2).reshape(8, 512).T,
        total[96:104, CM + 1],
    )


def solution(mesh):
    fine = Mesh(mesh.devices.reshape(4, 2, 2, 2, 4), ("y", "xh", "c", "xl", "z"))
    dp, seq = ("y", "xh", "c"), ("xl", "z")
    every = dp + seq
    return jax.shard_map(
        on_device,
        mesh=fine,
        in_specs=(
            P(dp, seq, None),
            P(dp, seq, None),
            P(dp, None),
            P(dp, seq),
            P(dp, seq, None),
            P(dp, seq, None),
            P(None, every),
            P(None, every),
            P(None, every),
            P(every, None),
            P(every),
            P(None, every),
            P(every),
        ),
        out_specs=(
            P(dp, seq, None),
            P(dp, seq, None),
            P(dp, seq, None),
            P(dp, seq, None),
            P(None, every),
            P(None, every),
            P(None, every),
            P(every, None),
            P(every),
            P(None, every),
            P(every),
        ),
        check_vma=False,
    )
```

```python
import jax
import jax.numpy as jnp
from jax import lax
from jax.experimental import pallas as pl
from jax.experimental.pallas import tpu as pltpu
from jax.sharding import Mesh, PartitionSpec as P

STEP = 64
SEQ = ("xl", "z")
CHIPS = ("y", "xh", "xl", "z")
BF16 = jnp.bfloat16
F32 = jnp.float32
LANES = 128
TAPS = 32
HALF_TAPS = 16
CM = 80
SHARE = 20
LINES = 144
VMEM_BYTES = 50 * 1024 * 1024
SIDE_VMEM_BYTES = 40 * 1024 * 1024


def dot(a, b):
    return jnp.dot(a, b, preferred_element_type=F32)


def dot_nt(a, b):
    return lax.dot_general(a, b, (((1,), (1,)), ((), ())), preferred_element_type=F32)


def dot_tn(a, b):
    return lax.dot_general(a, b, (((0,), (0,)), ((), ())), preferred_element_type=F32)


def lane_mask(rows):
    return lax.broadcasted_iota(jnp.int32, (rows, LANES), 1) < CM


def spread_kernel(wd, wot, wct, u1t, u2t, gb, ob, out, lines):
    lines[...] = jnp.zeros_like(lines)
    for j in range(8):
        lines[8 * j : 8 * j + 8, :] = wd[:, LANES * j : LANES * (j + 1)].astype(F32)
    for j in range(4):
        lines[64 + 8 * j : 72 + 8 * j, :] = wot[:, LANES * j : LANES * (j + 1)].astype(F32)
    lane = lax.broadcasted_iota(jnp.int32, (8, LANES), 1)
    diagonal = lax.broadcasted_iota(jnp.int32, (8, 8), 0) == lax.broadcasted_iota(jnp.int32, (8, 8), 1)

    def column(row):
        full = jnp.broadcast_to(row[...].astype(F32), (8, 8))
        return jnp.sum(jnp.where(diagonal, full, 0.0), 1, keepdims=True)

    lines[96:104, :CM] = wct[...].astype(F32)
    biases = jnp.where(lane == CM, column(gb), jnp.where(lane == CM + 1, column(ob), 0.0))
    lines[96:104, :] += biases
    lines[104:124, :CM] = u1t[...].astype(F32)
    lines[124:144, :CM] = u2t[...].astype(F32)
    block = lines[...].astype(BF16)
    for k in range(out.shape[0]):
        out[k] = block


def spread(wd, wot, wct, u1t, u2t, gb, ob):
    return pl.pallas_call(
        spread_kernel,
        out_shape=jax.ShapeDtypeStruct((64, LINES, LANES), BF16),
        scratch_shapes=[pltpu.VMEM((LINES, LANES), F32)],
    )(wd, wot, wct, u1t, u2t, gb, ob)


def turn_kernel(starts, seq_at, resets, tail, audio_before, audio, g_res, g_skip, past, mask, xt, gt, g_sum):
    step = pl.program_id(0)
    tile, half = audio.shape
    base = step * tile
    position = (seq_at[0] * pl.num_programs(0) + step) * tile + lax.broadcasted_iota(jnp.int32, (1, tile), 1)
    blocked = position < STEP
    for k in range(starts.shape[1]):
        first = starts[0, k]
        blocked = blocked | ((first > position - STEP) & (first <= position))
    keep = jnp.where(blocked, 0, resets[...]).astype(F32)
    column = jnp.broadcast_to(keep, (LANES, tile)).T
    mask[...] = column.astype(BF16)
    before = jnp.where(step == 0, tail[...], audio_before[...])
    moved = jnp.concatenate([before, audio[: tile - STEP, :]], 0).astype(F32)
    kept = (moved * jnp.concatenate([column] * (half // LANES), 1)).astype(BF16)
    past[...] = kept
    xt[:half, :] = kept.T
    xt[half:, :] = audio[...].T
    gt[:half, :] = g_res[...].T
    gt[half:, :] = g_skip[...].T

    @pl.when(step == 0)
    def _():
        g_sum[...] = jnp.zeros_like(g_sum)

    g_sum[:, :half] += jnp.sum(g_res[...].astype(F32), 0, keepdims=True)
    g_sum[:, half:] += jnp.sum(g_skip[...].astype(F32), 0, keepdims=True)


def turn(starts, seq_at, resets, tail, audio, g_res, g_skip, tile):
    samples, width = audio.shape
    steps = tile // STEP
    rows = pl.BlockSpec((tile, width), lambda i: (i, 0))
    cols = pl.BlockSpec((2 * width, tile), lambda i: (0, i))
    scalars = pl.BlockSpec(memory_space=pltpu.SMEM)
    shape = jax.ShapeDtypeStruct((2 * width, samples), BF16)
    return pl.pallas_call(
        turn_kernel,
        grid=(samples // tile,),
        in_specs=[
            scalars,
            scalars,
            pl.BlockSpec((1, tile), lambda i: (0, i)),
            pl.BlockSpec((STEP, width), lambda i: (0, 0)),
            pl.BlockSpec((STEP, width), lambda i: (jnp.maximum(i * steps - 1, 0), 0)),
            rows,
            rows,
            rows,
        ],
        out_specs=[
            rows,
            pl.BlockSpec((tile, LANES), lambda i: (i, 0)),
            cols,
            cols,
            pl.BlockSpec((1, 2 * width), lambda i: (0, 0)),
        ],
        out_shape=[
            jax.ShapeDtypeStruct((samples, width), BF16),
            jax.ShapeDtypeStruct((samples, LANES), BF16),
            shape,
            shape,
            jax.ShapeDtypeStruct((1, 2 * width), F32),
        ],
        compiler_params=pltpu.CompilerParams(vmem_limit_bytes=SIDE_VMEM_BYTES),
        cost_estimate=pl.CostEstimate(flops=0, bytes_accessed=18 * samples * width, transcendentals=0),
    )(starts, seq_at, resets, tail, audio, audio, g_res, g_skip)


def main_kernel(
    core, mel_a, mel_b, past, audio, g_res, g_skip, xt, gt, head_mask, g_sum, own, other,
    dp_out, gated_out, stay, send, wd_out, wot_out, halo, mel_here, ob,
    wd, wot, wct, u1t, u2t, wc, inter, cond_all, dcond_all, dinter, xg, owg, du, mine, theirs, in_sems, out_sems, weight_sems,
):
    step = pl.program_id(0)
    tile = audio.shape[0]
    half = audio.shape[1]
    frames = cond_all.shape[0] // HALF_TAPS
    first_rows = mel_a.shape[0]
    keep_weights = [
        pltpu.make_async_copy(a, b, weight_sems.at[k]) for k, (a, b) in enumerate(((wd, wd_out), (wot, wot_out)))
    ]

    @pl.when(step == 0)
    def _():
        fetch = [pltpu.make_async_copy(a, b, in_sems.at[k]) for k, (a, b) in enumerate(((own, mine), (other, theirs)))]
        for copy in fetch:
            copy.start()
        xg[...] = jnp.zeros_like(xg)
        owg[...] = jnp.zeros_like(owg)
        xg[2 * half + CM + 1 : 2 * half + CM + 2, :] = g_sum[...]
        u1t[TAPS * CM :, :] = jnp.zeros_like(u1t[TAPS * CM :, :])
        u2t[TAPS * CM :, :] = jnp.zeros_like(u2t[TAPS * CM :, :])
        for copy in fetch:
            copy.wait()

        def unpack(a, _):
            for ref, side in ((mine, core[0]), (theirs, 1 - core[0])):
                for b in range(0, 8, 2):
                    at_row = pl.multiple_of(a * 128 + side * 64 + b * 8, 16)
                    pair = [a * 8 + b, a * 8 + b + 1]
                    rows = pl.ds(at_row, 16)
                    for m in range(4):
                        two = [ref[k, pl.ds(16 * m, 16), :].astype(F32) for k in pair]
                        wd[rows, pl.ds(256 * m, 128)] = jnp.concatenate([t[:8] for t in two], 0).astype(BF16)
                        wd[rows, pl.ds(256 * m + 128, 128)] = jnp.concatenate([t[8:] for t in two], 0).astype(BF16)
                    for m in range(2):
                        two = [ref[k, pl.ds(64 + 16 * m, 16), :].astype(F32) for k in pair]
                        wot[rows, pl.ds(256 * m, 128)] = jnp.concatenate([t[:8] for t in two], 0).astype(BF16)
                        wot[rows, pl.ds(256 * m + 128, 128)] = jnp.concatenate([t[8:] for t in two], 0).astype(BF16)
                    two = [ref[k, pl.ds(96, 16), :].astype(F32) for k in pair]
                    wct[rows, :] = jnp.concatenate([t[:8] for t in two], 0).astype(BF16)
                for b in range(0, 8, 4):
                    tap_row = pl.multiple_of((a * 16 + side * 8 + b) * SHARE, 16)
                    four = [ref[a * 8 + b + k, pl.ds(96, 48), :].astype(F32) for k in range(4)]
                    for k, out in ((8, u1t), (8 + SHARE, u2t)):
                        out[pl.ds(tap_row, CM), :] = jnp.concatenate([t[k : k + SHARE] for t in four], 0).astype(BF16)
            return _

        lax.fori_loop(0, 8, unpack, 0)
        for copy in keep_weights:
            copy.start()
        wc[...] = wct[...].T
        ob[...] = wc[CM : CM + 2, :].astype(F32)
        keep = lane_mask(first_rows)
        for r in range(HALF_TAPS):
            here = dot_nt(mel_a[...], u1t[pl.ds(CM * r, LANES), :])
            before = dot_nt(mel_b[...], u1t[pl.ds(CM * (r + HALF_TAPS), LANES), :])
            rounded = jnp.where(keep, here + before, 0.0).astype(BF16).astype(F32)
            inter[pl.ds(r, first_rows, stride=HALF_TAPS), :] = rounded
        rows_a = inter[pl.ds(HALF_TAPS, frames), :].astype(BF16)
        rows_b = inter[pl.ds(HALF_TAPS - 1, frames), :].astype(BF16)
        lane = lax.broadcasted_iota(jnp.int32, (frames, LANES), 1)
        one = jnp.where(lane == CM, 1.0, 0.0)
        for r in range(HALF_TAPS):
            here = dot_nt(rows_a, u2t[pl.ds(CM * r, LANES), :])
            before = dot_nt(rows_b, u2t[pl.ds(CM * (r + HALF_TAPS), LANES), :])
            cond_all[pl.ds(r, frames, stride=HALF_TAPS), :] = jnp.where(lane < CM, here + before, one)

    at = pl.multiple_of(step * tile, tile)
    cond = cond_all[pl.ds(at, tile), :].astype(BF16)
    pre = dot(past[...], wd[:half, :]) + dot(audio[...], wd[half:, :]) + dot(cond, wc[...])
    th = jnp.tanh(pre[:, :half])
    sg = 0.5 * jnp.tanh(0.5 * pre[:, half:]) + 0.5
    gated = (th * sg).astype(BF16)
    gated_out[...] = gated
    dg = dot(g_res[...], wot[:half, :]) + dot(g_skip[...], wot[half:, :])
    dgs = dg * sg
    dp = jnp.concatenate([dgs * (1.0 - th * th), dgs * th * (1.0 - sg)], 1).astype(BF16)
    dp_out[...] = dp
    dcond_all[pl.ds(at, tile), :] = dot(dp, wct[...])
    owg[...] += dot(gt[...], gated)
    xg[...] += dot(jnp.concatenate([xt[...], cond.T], 0), dp)

    @pl.when(step == 0)
    def _():
        kept = jnp.concatenate([head_mask[...].astype(F32)] * (2 * half // LANES), 1)
        halo[:STEP, :] = (dp[:STEP, :].astype(F32) * kept).astype(BF16)

    @pl.when(step == pl.num_programs(0) - 1)
    def _():
        rows_a = inter[pl.ds(HALF_TAPS, frames), :].astype(BF16)
        rows_b = inter[pl.ds(HALF_TAPS - 1, frames), :].astype(BF16)
        both = jnp.concatenate([rows_a, rows_b], 1)
        keep = lane_mask(frames)
        sum_a = jnp.zeros((frames, LANES), F32)
        sum_b = jnp.zeros((frames, LANES), F32)

        def put(grads, tap, first):
            for q in range(CM // SHARE):
                du[pl.ds((CM // SHARE * tap + q) * 2 * SHARE + first, SHARE), :] = grads[SHARE * q : SHARE * (q + 1)]

        for r in range(HALF_TAPS):
            e = jnp.where(keep, dcond_all[pl.ds(r, frames, stride=HALF_TAPS), :], 0.0).astype(BF16)
            grads = dot_tn(e, both)
            put(grads[:, :LANES], r, SHARE)
            put(grads[:, LANES:], r + HALF_TAPS, SHARE)
            sum_a += dot(e, u2t[pl.ds(CM * r, LANES), :])
            sum_b += dot(e, u2t[pl.ds(CM * (r + HALF_TAPS), LANES), :])
        dinter[...] = jnp.zeros_like(dinter)
        dinter[pl.ds(HALF_TAPS, frames), :] = sum_a
        dinter[pl.ds(HALF_TAPS - 1, frames), :] += sum_b
        mels = jnp.concatenate([mel_a[...], mel_b[...]], 1)
        keep = lane_mask(first_rows)
        mel_sum_a = jnp.zeros((first_rows, LANES), F32)
        mel_sum_b = jnp.zeros((first_rows, LANES), F32)
        for r in range(HALF_TAPS):
            f = jnp.where(keep, dinter[pl.ds(r, first_rows, stride=HALF_TAPS), :], 0.0).astype(BF16)
            grads = dot_tn(f, mels)
            put(grads[:, :LANES], r, 0)
            put(grads[:, LANES:], r + HALF_TAPS, 0)
            mel_sum_a += dot(f, u1t[pl.ds(CM * r, LANES), :])
            mel_sum_b += dot(f, u1t[pl.ds(CM * (r + HALF_TAPS), LANES), :])
        zero = jnp.zeros((1, LANES), F32)
        mel_sum = jnp.concatenate([zero, mel_sum_a], 0) + jnp.concatenate([mel_sum_b, zero], 0)
        real = mel_here.shape[0]
        mel_here[...] = mel_sum[2 : 2 + real]
        halo[STEP:, :] = jnp.zeros_like(halo[STEP:, :])
        halo[STEP:, :LANES] = jnp.concatenate([mel_sum[:2], jnp.zeros((14, LANES), F32)], 0).astype(BF16)
        cwgt = xg[2 * half :, :].T
        dcond_all[: cwgt.shape[0], :] = cwgt

        def give(a, k):
            part = pl.ds(pl.multiple_of(a * 8, 8), 8)
            src, dst = ((mine, stay), (theirs, send))[k]
            return pltpu.make_async_copy(src.at[part], dst.at[part], out_sems.at[k, a])

        def pack(a, _):
            for k, (out, side) in enumerate(((mine, core[0]), (theirs, 1 - core[0]))):
                for b in range(8):
                    at_row = pl.multiple_of(a * 128 + side * 64 + b * 8, 8)
                    rows = pl.ds(at_row, 8)
                    place = a * 8 + b
                    for m in range(4):
                        two = [xg[rows, pl.ds(256 * m, 128)], xg[rows, pl.ds(256 * m + 128, 128)]]
                        out[place, pl.ds(16 * m, 16), :] = jnp.concatenate(two, 0).astype(BF16)
                    for m in range(2):
                        two = [owg[rows, pl.ds(256 * m, 128)], owg[rows, pl.ds(256 * m + 128, 128)]]
                        out[place, pl.ds(64 + 16 * m, 16), :] = jnp.concatenate(two, 0).astype(BF16)
                    du_row = pl.multiple_of(at_row * 5, 8)
                    rest = [dcond_all[rows, :], du[pl.ds(du_row, 2 * SHARE), :]]
                    out[place, pl.ds(96, 48), :] = jnp.concatenate(rest, 0).astype(BF16)
                give(a, k).start()
            return _

        lax.fori_loop(0, 8, pack, 0)

        def finish(a, _):
            give(a, 0).wait()
            give(a, 1).wait()
            return _

        lax.fori_loop(0, 8, finish, 0)
        for copy in keep_weights:
            copy.wait()


def main_pass(core, mel_a, mel_b, past, audio, g_res, g_skip, xt, gt, mask, g_sum, own, other, tile):
    samples, width = audio.shape
    first_rows = mel_a.shape[0]
    rows = pl.BlockSpec((tile, width), lambda i: (i, 0))
    cols = pl.BlockSpec((2 * width, tile), lambda i: (0, i))

    def whole(shape):
        return pl.BlockSpec(shape, lambda i: (0,) * len(shape))

    anywhere = pl.BlockSpec(memory_space=pl.ANY)
    packed = (64, LINES, LANES)
    outs = [
        ((samples, 2 * width), BF16),
        ((samples, width), BF16),
        (packed, BF16),
        (packed, BF16),
        ((2 * width, 2 * width), BF16),
        ((2 * width, width), BF16),
        ((STEP + 16, 2 * width), BF16),
        ((samples // (HALF_TAPS * HALF_TAPS), LANES), F32),
        ((2, 2 * width), F32),
    ]
    return pl.pallas_call(
        main_kernel,
        grid=(samples // tile,),
        in_specs=[pl.BlockSpec(memory_space=pltpu.SMEM)]
        + [whole(mel_a.shape), whole(mel_b.shape), rows, rows, rows, rows, cols, cols]
        + [whole((STEP, LANES)), whole(g_sum.shape), anywhere, anywhere],
        out_specs=[
            pl.BlockSpec((tile, 2 * width), lambda i: (i, 0)),
            pl.BlockSpec((tile, width), lambda i: (i, 0)),
            anywhere,
            anywhere,
            anywhere,
            anywhere,
        ]
        + [whole(s) for s, _ in outs[6:]],
        out_shape=[jax.ShapeDtypeStruct(s, d) for s, d in outs],
        scratch_shapes=[
            pltpu.VMEM((2 * width, 2 * width), BF16),
            pltpu.VMEM((2 * width, width), BF16),
            pltpu.VMEM((2 * width, LANES), BF16),
            pltpu.VMEM((TAPS * CM + 48, LANES), BF16),
            pltpu.VMEM((TAPS * CM + 48, LANES), BF16),
            pltpu.VMEM((LANES, 2 * width), BF16),
            pltpu.VMEM((first_rows * HALF_TAPS, LANES), F32),
            pltpu.VMEM((samples, LANES), F32),
            pltpu.VMEM((samples, LANES), F32),
            pltpu.VMEM((first_rows * HALF_TAPS, LANES), F32),
            pltpu.VMEM((2 * width + LANES, 2 * width), F32),
            pltpu.VMEM((2 * width, width), F32),
            pltpu.VMEM((2 * TAPS * CM, LANES), F32),
            pltpu.VMEM(packed, BF16),
            pltpu.VMEM(packed, BF16),
            pltpu.SemaphoreType.DMA((2,)),
            pltpu.SemaphoreType.DMA((2, 8)),
            pltpu.SemaphoreType.DMA((2,)),
        ],
        compiler_params=pltpu.CompilerParams(vmem_limit_bytes=VMEM_BYTES),
        cost_estimate=pl.CostEstimate(
            flops=28_000_000_000, bytes_accessed=48 * samples * width, transcendentals=0
        ),
    )(core, mel_a, mel_b, past, audio, g_res, g_skip, xt, gt, mask, g_sum, own, other)


def tail_kernel(
    dp, dp_next, dp_halo, gated, audio, g_res, mask, mask_next, wd, wot, ob, res_out, skip_out, res_grad, wdt, wo
):
    step = pl.program_id(0)
    tile, half = audio.shape

    @pl.when(step == 0)
    def _():
        wdt[...] = wd[...].T
        wo[...] = wot[...].T

    out = dot(gated[...], wo[...]) + ob[1:2, :]
    res_out[...] = (audio[...].astype(F32) + out[:, :half]).astype(BF16)
    skip_out[...] = out[:, half:].astype(BF16)
    last = step == pl.num_programs(0) - 1
    after = jnp.where(last, dp_halo[...], dp_next[...])
    mask_after = jnp.where(last, jnp.ones_like(mask_next[...]), mask_next[...])
    ahead = jnp.concatenate([dp[STEP:, :], after], 0)
    d_past = dot(ahead, wdt[:, :half])
    kept = jnp.concatenate([mask[STEP:, :], mask_after], 0).astype(F32)
    kept = jnp.concatenate([kept] * (half // LANES), 1)
    d_now = dot(dp[...], wdt[:, half:])
    res_grad[...] = (g_res[...].astype(F32) + d_now + d_past * kept).astype(BF16)


def tail_pass(dp, dp_halo, gated, audio, g_res, mask, wd, wot, ob, tile):
    samples, width = audio.shape
    rows = pl.BlockSpec((tile, width), lambda i: (i, 0))
    step_blocks = tile // STEP
    final = samples // STEP - 1

    def whole(shape):
        return pl.BlockSpec(shape, lambda i: (0,) * len(shape))

    shape = jax.ShapeDtypeStruct((samples, width), BF16)
    return pl.pallas_call(
        tail_kernel,
        grid=(samples // tile,),
        in_specs=[
            pl.BlockSpec((tile, 2 * width), lambda i: (i, 0)),
            pl.BlockSpec((STEP, 2 * width), lambda i: (jnp.minimum((i + 1) * step_blocks, final), 0)),
            whole((STEP, 2 * width)),
            rows,
            rows,
            rows,
            pl.BlockSpec((tile, LANES), lambda i: (i, 0)),
            pl.BlockSpec((STEP, LANES), lambda i: (jnp.minimum((i + 1) * step_blocks, final), 0)),
            whole(wd.shape),
            whole(wot.shape),
            whole((2, 2 * width)),
        ],
        out_specs=[rows] * 3,
        out_shape=[shape] * 3,
        scratch_shapes=[
            pltpu.VMEM((2 * width, 2 * width), BF16),
            pltpu.VMEM((width, 2 * width), BF16),
        ],
        compiler_params=pltpu.CompilerParams(vmem_limit_bytes=VMEM_BYTES),
        cost_estimate=pl.CostEstimate(
            flops=13_000_000_000, bytes_accessed=20 * samples * width, transcendentals=0
        ),
    )(dp, dp, dp_halo, gated, audio, g_res, mask, mask, wd, wot, ob)


def shifted(value, steps, count=8):
    first, last = max(0, -steps), min(count, count - steps)
    return lax.ppermute(value, SEQ, [(s, s + steps) for s in range(first, last)])


def swap(value):
    return lax.ppermute(value, "c", [(0, 1), (1, 0)])


def on_device(
    residual_input, mel_input_frames, starts, resets, residual_gradient, skip_gradient,
    first_upsample_weight, second_upsample_weight, conditioning_weight, dilated_weight,
    gate_bias_vector, output_weight, output_bias_vector,
):
    core = lax.axis_index("c")
    audio, mel = residual_input[0], mel_input_frames[0]
    g_res, g_skip = residual_gradient[0], skip_gradient[0]
    samples, width = audio.shape
    frames = mel.shape[0]

    tails = jnp.concatenate([audio[-STEP:], jnp.pad(mel[-2:], ((0, 14), (0, width - CM)))], 0)
    tails = shifted(tails, 1)

    shares = spread(
        dilated_weight,
        output_weight.T,
        conditioning_weight.T,
        first_upsample_weight.T,
        second_upsample_weight.T,
        gate_bias_vector[None],
        output_bias_vector[None],
    )
    own = lax.all_to_all(shares, CHIPS, 0, 0)

    mel_tail = tails[STEP : STEP + 2, :CM]
    mel_ext = jnp.concatenate([mel_tail, mel, jnp.zeros((14, CM), BF16)], 0)
    mel_ext = jnp.pad(mel_ext, ((0, 0), (0, LANES - CM)))
    mel_b, mel_a = mel_ext[: 2 * frames - 8], mel_ext[1 : 2 * frames - 7]
    seq_at = lax.axis_index(SEQ).astype(jnp.int32)[None]
    past, mask, xt, gt, g_sum = turn(starts, seq_at, resets, tails, audio, g_res, g_skip, 512)

    own = own + jnp.minimum(jnp.abs(g_sum[0, 0]) + jnp.abs(mel_a[8, 0]).astype(F32), 0.0).astype(BF16)
    other = swap(own)

    dp, gated, stay, send, wd, wot, halo, mel_here, biases = main_pass(
        core.astype(jnp.int32)[None], mel_a, mel_b, past, audio, g_res, g_skip, xt, gt, mask, g_sum, own, other, 512
    )

    halo_next = shifted(halo, -1)
    came = swap(send)
    pair = (stay.astype(F32) + came.astype(F32) + halo_next[-1, -1].astype(F32)).astype(BF16)
    all_parts = lax.all_to_all(pair, CHIPS, 0, 0)

    mel_back = halo_next[STEP : STEP + 2, :CM].astype(F32)
    mel_grad = mel_here[:, :CM] + jnp.pad(mel_back, ((frames - 2, 0), (0, 0)))
    res_out, skip_out, res_grad = tail_pass(dp, halo_next, gated, audio, g_res, mask, wd, wot, biases, 512)

    total = jnp.sum(all_parts.astype(F32), 0)
    return (
        res_out[None],
        skip_out[None],
        res_grad[None],
        mel_grad.astype(BF16)[None],
        total[104:124, :CM].T,
        total[124:144, :CM].T,
        total[96:104, :CM].T,
        total[:64].reshape(8, 8, LANES).transpose(1, 0, 2).reshape(8, 1024),
        total[96:104, CM],
        total[64:96].reshape(4, 8, LANES).transpose(1, 0, 2).reshape(8, 512).T,
        total[96:104, CM + 1],
    )


def solution(mesh):
    fine = Mesh(mesh.devices.reshape(4, 2, 2, 2, 4), ("y", "xh", "c", "xl", "z"))
    dp, seq = ("y", "xh", "c"), ("xl", "z")
    every = dp + seq
    return jax.shard_map(
        on_device,
        mesh=fine,
        in_specs=(
            P(dp, seq, None),
            P(dp, seq, None),
            P(dp, None),
            P(dp, seq),
            P(dp, seq, None),
            P(dp, seq, None),
            P(None, every),
            P(None, every),
            P(None, every),
            P(every, None),
            P(every),
            P(None, every),
            P(every),
        ),
        out_specs=(
            P(dp, seq, None),
            P(dp, seq, None),
            P(dp, seq, None),
            P(dp, seq, None),
            P(None, every),
            P(None, every),
            P(None, every),
            P(every, None),
            P(every),
            P(None, every),
            P(every),
        ),
        check_vma=False,
    )
```

```python
import jax
import jax.numpy as jnp
from jax import lax
from jax.experimental import pallas as pl
from jax.experimental.pallas import tpu as pltpu
from jax.sharding import Mesh, PartitionSpec as P

STEP = 64
SEQ = ("xl", "z")
CHIPS = ("y", "xh", "xl", "z")
BF16 = jnp.bfloat16
F32 = jnp.float32
LANES = 128
TAPS = 32
HALF_TAPS = 16
CM = 80
SHARE = 20
LINES = 144
VMEM_BYTES = 50 * 1024 * 1024
SIDE_VMEM_BYTES = 60 * 1024 * 1024


def dot(a, b):
    return jnp.dot(a, b, preferred_element_type=F32)


def dot_nt(a, b):
    return lax.dot_general(a, b, (((1,), (1,)), ((), ())), preferred_element_type=F32)


def dot_tn(a, b):
    return lax.dot_general(a, b, (((0,), (0,)), ((), ())), preferred_element_type=F32)


def lane_mask(rows):
    return lax.broadcasted_iota(jnp.int32, (rows, LANES), 1) < CM


def spread_kernel(wd, wot, wct, u1t, u2t, gb, ob, out, lines):
    lines[...] = jnp.zeros_like(lines)
    for j in range(8):
        lines[8 * j : 8 * j + 8, :] = wd[:, LANES * j : LANES * (j + 1)].astype(F32)
    for j in range(4):
        lines[64 + 8 * j : 72 + 8 * j, :] = wot[:, LANES * j : LANES * (j + 1)].astype(F32)
    lane = lax.broadcasted_iota(jnp.int32, (8, LANES), 1)
    diagonal = lax.broadcasted_iota(jnp.int32, (8, 8), 0) == lax.broadcasted_iota(jnp.int32, (8, 8), 1)

    def column(row):
        full = jnp.broadcast_to(row[...].astype(F32), (8, 8))
        return jnp.sum(jnp.where(diagonal, full, 0.0), 1, keepdims=True)

    lines[96:104, :CM] = wct[...].astype(F32)
    biases = jnp.where(lane == CM, column(gb), jnp.where(lane == CM + 1, column(ob), 0.0))
    lines[96:104, :] += biases
    lines[104:124, :CM] = u1t[...].astype(F32)
    lines[124:144, :CM] = u2t[...].astype(F32)
    block = lines[...].astype(BF16)
    for k in range(out.shape[0]):
        out[k] = block


def spread(wd, wot, wct, u1t, u2t, gb, ob):
    return pl.pallas_call(
        spread_kernel,
        out_shape=jax.ShapeDtypeStruct((64, LINES, LANES), BF16),
        scratch_shapes=[pltpu.VMEM((LINES, LANES), F32)],
    )(wd, wot, wct, u1t, u2t, gb, ob)


def masked_past(before, audio, column):
    tile, half = audio.shape
    moved = jnp.concatenate([before, audio[: tile - STEP, :]], 0)
    return moved * jnp.concatenate([column] * (half // LANES), 1)


def turn_kernel(starts, seq_at, resets, audio_before, audio, g_res, g_skip, mask, xt, gt, g_sum):
    step = pl.program_id(0)
    tile, half = audio.shape
    position = (seq_at[0] * pl.num_programs(0) + step) * tile + lax.broadcasted_iota(jnp.int32, (1, tile), 1)
    blocked = position < STEP
    for k in range(starts.shape[1]):
        first = starts[0, k]
        blocked = blocked | ((first > position - STEP) & (first <= position))
    keep = jnp.where(blocked, 0, resets[...]).astype(F32)
    column = jnp.broadcast_to(keep, (LANES, tile)).T.astype(BF16)
    mask[...] = column
    before = jnp.where(step == 0, jnp.zeros_like(audio_before[...]), audio_before[...])
    xt[:half, :] = masked_past(before, audio[...], column).T
    xt[half:, :] = audio[...].T
    gt[:half, :] = g_res[...].T
    gt[half:, :] = g_skip[...].T

    @pl.when(step == 0)
    def _():
        g_sum[...] = jnp.zeros_like(g_sum)

    g_sum[:, :half] += jnp.sum(g_res[...].astype(F32), 0, keepdims=True)
    g_sum[:, half:] += jnp.sum(g_skip[...].astype(F32), 0, keepdims=True)


def turn(starts, seq_at, resets, audio, g_res, g_skip, tile):
    samples, width = audio.shape
    steps = tile // STEP
    rows = pl.BlockSpec((tile, width), lambda i: (i, 0))
    cols = pl.BlockSpec((2 * width, tile), lambda i: (0, i))
    scalars = pl.BlockSpec(memory_space=pltpu.SMEM)
    shape = jax.ShapeDtypeStruct((2 * width, samples), BF16)
    return pl.pallas_call(
        turn_kernel,
        grid=(samples // tile,),
        in_specs=[
            scalars,
            scalars,
            pl.BlockSpec((1, tile), lambda i: (0, i)),
            pl.BlockSpec((STEP, width), lambda i: (jnp.maximum(i * steps - 1, 0), 0)),
            rows,
            rows,
            rows,
        ],
        out_specs=[
            pl.BlockSpec((tile, LANES), lambda i: (i, 0)),
            cols,
            cols,
            pl.BlockSpec((1, 2 * width), lambda i: (0, 0)),
        ],
        out_shape=[
            jax.ShapeDtypeStruct((samples, LANES), BF16),
            shape,
            shape,
            jax.ShapeDtypeStruct((1, 2 * width), F32),
        ],
        compiler_params=pltpu.CompilerParams(vmem_limit_bytes=SIDE_VMEM_BYTES),
        cost_estimate=pl.CostEstimate(flops=0, bytes_accessed=18 * samples * width, transcendentals=0),
    )(starts, seq_at, resets, audio, audio, g_res, g_skip)


def main_kernel(
    core, mel_a, mel_b, tails, audio_before, audio, g_res, g_skip, mask, xt, gt, g_sum, own, other,
    dp_out, gated_out, stay, send, wd_out, wot_out, halo, mel_here, ob,
    wd, wot, wct, u1t, u2t, wc, inter, cond_all, dcond_all, dinter, xg, owg, du, mine, theirs, in_sems, out_sems, weight_sems,
):
    step = pl.program_id(0)
    tile = audio.shape[0]
    half = audio.shape[1]
    frames = cond_all.shape[0] // HALF_TAPS
    first_rows = mel_a.shape[0]
    keep_weights = [
        pltpu.make_async_copy(a, b, weight_sems.at[k]) for k, (a, b) in enumerate(((wd, wd_out), (wot, wot_out)))
    ]

    @pl.when(step == 0)
    def _():
        fetch = [pltpu.make_async_copy(a, b, in_sems.at[k]) for k, (a, b) in enumerate(((own, mine), (other, theirs)))]
        for copy in fetch:
            copy.start()
        xg[...] = jnp.zeros_like(xg)
        owg[...] = jnp.zeros_like(owg)
        xg[2 * half + CM + 1 : 2 * half + CM + 2, :] = g_sum[...]
        u1t[TAPS * CM :, :] = jnp.zeros_like(u1t[TAPS * CM :, :])
        u2t[TAPS * CM :, :] = jnp.zeros_like(u2t[TAPS * CM :, :])
        for copy in fetch:
            copy.wait()

        def unpack(a, _):
            for ref, side in ((mine, core[0]), (theirs, 1 - core[0])):
                for b in range(0, 8, 2):
                    at_row = pl.multiple_of(a * 128 + side * 64 + b * 8, 16)
                    pair = [a * 8 + b, a * 8 + b + 1]
                    rows = pl.ds(at_row, 16)
                    for m in range(4):
                        two = [ref[k, pl.ds(16 * m, 16), :].astype(F32) for k in pair]
                        wd[rows, pl.ds(256 * m, 128)] = jnp.concatenate([t[:8] for t in two], 0).astype(BF16)
                        wd[rows, pl.ds(256 * m + 128, 128)] = jnp.concatenate([t[8:] for t in two], 0).astype(BF16)
                    for m in range(2):
                        two = [ref[k, pl.ds(64 + 16 * m, 16), :].astype(F32) for k in pair]
                        wot[rows, pl.ds(256 * m, 128)] = jnp.concatenate([t[:8] for t in two], 0).astype(BF16)
                        wot[rows, pl.ds(256 * m + 128, 128)] = jnp.concatenate([t[8:] for t in two], 0).astype(BF16)
                    two = [ref[k, pl.ds(96, 16), :].astype(F32) for k in pair]
                    wct[rows, :] = jnp.concatenate([t[:8] for t in two], 0).astype(BF16)
                for b in range(0, 8, 4):
                    tap_row = pl.multiple_of((a * 16 + side * 8 + b) * SHARE, 16)
                    four = [ref[a * 8 + b + k, pl.ds(96, 48), :].astype(F32) for k in range(4)]
                    for k, out in ((8, u1t), (8 + SHARE, u2t)):
                        out[pl.ds(tap_row, CM), :] = jnp.concatenate([t[k : k + SHARE] for t in four], 0).astype(BF16)
            return _

        lax.fori_loop(0, 8, unpack, 0)
        for copy in keep_weights:
            copy.start()
        wc[...] = wct[...].T
        ob[...] = wc[CM : CM + 2, :].astype(F32)
        keep = lane_mask(first_rows)
        for r in range(HALF_TAPS):
            here = dot_nt(mel_a[...], u1t[pl.ds(CM * r, LANES), :])
            before = dot_nt(mel_b[...], u1t[pl.ds(CM * (r + HALF_TAPS), LANES), :])
            rounded = jnp.where(keep, here + before, 0.0).astype(BF16).astype(F32)
            inter[pl.ds(r, first_rows, stride=HALF_TAPS), :] = rounded
        rows_a = inter[pl.ds(HALF_TAPS, frames), :].astype(BF16)
        rows_b = inter[pl.ds(HALF_TAPS - 1, frames), :].astype(BF16)
        lane = lax.broadcasted_iota(jnp.int32, (frames, LANES), 1)
        one = jnp.where(lane == CM, 1.0, 0.0)
        for r in range(HALF_TAPS):
            here = dot_nt(rows_a, u2t[pl.ds(CM * r, LANES), :])
            before = dot_nt(rows_b, u2t[pl.ds(CM * (r + HALF_TAPS), LANES), :])
            cond_all[pl.ds(r, frames, stride=HALF_TAPS), :] = jnp.where(lane < CM, here + before, one)

    at = pl.multiple_of(step * tile, tile)
    cond = cond_all[pl.ds(at, tile), :].astype(BF16)
    past = masked_past(jnp.where(step == 0, tails[...], audio_before[...]), audio[...], mask[...])
    pre = dot(past, wd[:half, :]) + dot(audio[...], wd[half:, :]) + dot(cond, wc[...])
    th = jnp.tanh(pre[:, :half])
    sg = 0.5 * jnp.tanh(0.5 * pre[:, half:]) + 0.5
    gated = (th * sg).astype(BF16)
    gated_out[...] = gated
    dg = dot(g_res[...], wot[:half, :]) + dot(g_skip[...], wot[half:, :])
    dgs = dg * sg
    dp = jnp.concatenate([dgs * (1.0 - th * th), dgs * th * (1.0 - sg)], 1).astype(BF16)
    dp_out[...] = dp
    dcond_all[pl.ds(at, tile), :] = dot(dp, wct[...])
    owg[...] += dot(gt[...], gated)
    xg[...] += dot(jnp.concatenate([xt[...], cond.T], 0), dp)

    @pl.when(step == 0)
    def _():
        xg[:half, :] += dot_tn(past[:STEP, :], dp[:STEP, :])
        halo[:STEP, :] = dp[:STEP, :] * jnp.concatenate([mask[:STEP, :]] * (2 * half // LANES), 1)

    @pl.when(step == pl.num_programs(0) - 1)
    def _():
        rows_a = inter[pl.ds(HALF_TAPS, frames), :].astype(BF16)
        rows_b = inter[pl.ds(HALF_TAPS - 1, frames), :].astype(BF16)
        both = jnp.concatenate([rows_a, rows_b], 1)
        keep = lane_mask(frames)
        sum_a = jnp.zeros((frames, LANES), F32)
        sum_b = jnp.zeros((frames, LANES), F32)

        def put(grads, tap, first):
            for q in range(CM // SHARE):
                du[pl.ds((CM // SHARE * tap + q) * 2 * SHARE + first, SHARE), :] = grads[SHARE * q : SHARE * (q + 1)]

        for r in range(HALF_TAPS):
            e = jnp.where(keep, dcond_all[pl.ds(r, frames, stride=HALF_TAPS), :], 0.0).astype(BF16)
            grads = dot_tn(e, both)
            put(grads[:, :LANES], r, SHARE)
            put(grads[:, LANES:], r + HALF_TAPS, SHARE)
            sum_a += dot(e, u2t[pl.ds(CM * r, LANES), :])
            sum_b += dot(e, u2t[pl.ds(CM * (r + HALF_TAPS), LANES), :])
        dinter[...] = jnp.zeros_like(dinter)
        dinter[pl.ds(HALF_TAPS, frames), :] = sum_a
        dinter[pl.ds(HALF_TAPS - 1, frames), :] += sum_b
        mels = jnp.concatenate([mel_a[...], mel_b[...]], 1)
        keep = lane_mask(first_rows)
        mel_sum_a = jnp.zeros((first_rows, LANES), F32)
        mel_sum_b = jnp.zeros((first_rows, LANES), F32)
        for r in range(HALF_TAPS):
            f = jnp.where(keep, dinter[pl.ds(r, first_rows, stride=HALF_TAPS), :], 0.0).astype(BF16)
            grads = dot_tn(f, mels)
            put(grads[:, :LANES], r, 0)
            put(grads[:, LANES:], r + HALF_TAPS, 0)
            mel_sum_a += dot(f, u1t[pl.ds(CM * r, LANES), :])
            mel_sum_b += dot(f, u1t[pl.ds(CM * (r + HALF_TAPS), LANES), :])
        zero = jnp.zeros((1, LANES), F32)
        mel_sum = jnp.concatenate([zero, mel_sum_a], 0) + jnp.concatenate([mel_sum_b, zero], 0)
        real = mel_here.shape[0]
        mel_here[...] = mel_sum[2 : 2 + real]
        halo[STEP:, :] = jnp.zeros_like(halo[STEP:, :])
        halo[STEP:, :LANES] = jnp.concatenate([mel_sum[:2], jnp.zeros((14, LANES), F32)], 0).astype(BF16)
        cwgt = xg[2 * half :, :].T
        dcond_all[: cwgt.shape[0], :] = cwgt

        def give(a, k):
            part = pl.ds(pl.multiple_of(a * 8, 8), 8)
            src, dst = ((mine, stay), (theirs, send))[k]
            return pltpu.make_async_copy(src.at[part], dst.at[part], out_sems.at[k, a])

        def pack(a, _):
            for k, (out, side) in enumerate(((mine, core[0]), (theirs, 1 - core[0]))):
                for b in range(8):
                    at_row = pl.multiple_of(a * 128 + side * 64 + b * 8, 8)
                    rows = pl.ds(at_row, 8)
                    place = a * 8 + b
                    for m in range(4):
                        two = [xg[rows, pl.ds(256 * m, 128)], xg[rows, pl.ds(256 * m + 128, 128)]]
                        out[place, pl.ds(16 * m, 16), :] = jnp.concatenate(two, 0).astype(BF16)
                    for m in range(2):
                        two = [owg[rows, pl.ds(256 * m, 128)], owg[rows, pl.ds(256 * m + 128, 128)]]
                        out[place, pl.ds(64 + 16 * m, 16), :] = jnp.concatenate(two, 0).astype(BF16)
                    du_row = pl.multiple_of(at_row * 5, 8)
                    rest = [dcond_all[rows, :], du[pl.ds(du_row, 2 * SHARE), :]]
                    out[place, pl.ds(96, 48), :] = jnp.concatenate(rest, 0).astype(BF16)
                give(a, k).start()
            return _

        lax.fori_loop(0, 8, pack, 0)

        def finish(a, _):
            give(a, 0).wait()
            give(a, 1).wait()
            return _

        lax.fori_loop(0, 8, finish, 0)
        for copy in keep_weights:
            copy.wait()


def main_pass(core, mel_a, mel_b, tails, audio, g_res, g_skip, mask, xt, gt, g_sum, own, other, tile):
    samples, width = audio.shape
    first_rows = mel_a.shape[0]
    rows = pl.BlockSpec((tile, width), lambda i: (i, 0))
    cols = pl.BlockSpec((2 * width, tile), lambda i: (0, i))

    def whole(shape):
        return pl.BlockSpec(shape, lambda i: (0,) * len(shape))

    anywhere = pl.BlockSpec(memory_space=pl.ANY)
    packed = (64, LINES, LANES)
    outs = [
        ((samples, 2 * width), BF16),
        ((samples, width), BF16),
        (packed, BF16),
        (packed, BF16),
        ((2 * width, 2 * width), BF16),
        ((2 * width, width), BF16),
        ((STEP + 16, 2 * width), BF16),
        ((samples // (HALF_TAPS * HALF_TAPS), LANES), F32),
        ((2, 2 * width), F32),
    ]
    return pl.pallas_call(
        main_kernel,
        grid=(samples // tile,),
        in_specs=[pl.BlockSpec(memory_space=pltpu.SMEM)]
        + [whole(mel_a.shape), whole(mel_b.shape), whole((STEP, width))]
        + [pl.BlockSpec((STEP, width), lambda i: (jnp.maximum(i * (tile // STEP) - 1, 0), 0))]
        + [rows, rows, rows, pl.BlockSpec((tile, LANES), lambda i: (i, 0)), cols, cols]
        + [whole(g_sum.shape), anywhere, anywhere],
        out_specs=[
            pl.BlockSpec((tile, 2 * width), lambda i: (i, 0)),
            pl.BlockSpec((tile, width), lambda i: (i, 0)),
            anywhere,
            anywhere,
            anywhere,
            anywhere,
        ]
        + [whole(s) for s, _ in outs[6:]],
        out_shape=[jax.ShapeDtypeStruct(s, d) for s, d in outs],
        scratch_shapes=[
            pltpu.VMEM((2 * width, 2 * width), BF16),
            pltpu.VMEM((2 * width, width), BF16),
            pltpu.VMEM((2 * width, LANES), BF16),
            pltpu.VMEM((TAPS * CM + 48, LANES), BF16),
            pltpu.VMEM((TAPS * CM + 48, LANES), BF16),
            pltpu.VMEM((LANES, 2 * width), BF16),
            pltpu.VMEM((first_rows * HALF_TAPS, LANES), F32),
            pltpu.VMEM((samples, LANES), F32),
            pltpu.VMEM((samples, LANES), F32),
            pltpu.VMEM((first_rows * HALF_TAPS, LANES), F32),
            pltpu.VMEM((2 * width + LANES, 2 * width), F32),
            pltpu.VMEM((2 * width, width), F32),
            pltpu.VMEM((2 * TAPS * CM, LANES), F32),
            pltpu.VMEM(packed, BF16),
            pltpu.VMEM(packed, BF16),
            pltpu.SemaphoreType.DMA((2,)),
            pltpu.SemaphoreType.DMA((2, 8)),
            pltpu.SemaphoreType.DMA((2,)),
        ],
        compiler_params=pltpu.CompilerParams(vmem_limit_bytes=VMEM_BYTES),
        cost_estimate=pl.CostEstimate(
            flops=28_000_000_000, bytes_accessed=48 * samples * width, transcendentals=0
        ),
    )(core, mel_a, mel_b, tails, audio, audio, g_res, g_skip, mask, xt, gt, g_sum, own, other)


def tail_kernel(
    dp, dp_next, gated, audio, g_res, mask, mask_next, wd, wot, ob, res_out, skip_out, res_grad, rest, wdt, wo
):
    step = pl.program_id(0)
    tile, half = audio.shape

    @pl.when(step == 0)
    def _():
        wdt[...] = wd[...].T
        wo[...] = wot[...].T

    out = dot(gated[...], wo[...]) + ob[1:2, :]
    res_out[...] = (audio[...].astype(F32) + out[:, :half]).astype(BF16)
    skip_out[...] = out[:, half:].astype(BF16)
    last = step == pl.num_programs(0) - 1
    after = jnp.where(last, jnp.zeros_like(dp_next[...]), dp_next[...])
    ahead = jnp.concatenate([dp[STEP:, :], after], 0)
    d_past = dot(ahead, wdt[:, :half]).astype(BF16)
    kept = jnp.concatenate([mask[STEP:, :], mask_next[...]], 0)
    d_past = (d_past * jnp.concatenate([kept] * (half // LANES), 1)).astype(F32)
    here = g_res[...].astype(F32) + dot(dp[...], wdt[:, half:])
    rest[...] = here[tile - STEP :, :]
    res_grad[...] = (here + d_past).astype(BF16)


def fix_kernel(grad, rest, halo, wd, out):
    out[...] = (rest[...] + dot_nt(halo[...], wd[...]).astype(BF16).astype(F32)).astype(BF16)


def fix_pass(grad, rest, halo, wd):
    samples, width = grad.shape
    return pl.pallas_call(
        fix_kernel,
        grid=(1,),
        in_specs=[
            pl.BlockSpec(memory_space=pl.ANY),
            pl.BlockSpec((STEP, width), lambda i: (0, 0)),
            pl.BlockSpec((STEP, 2 * width), lambda i: (0, 0)),
            pl.BlockSpec((width, 2 * width), lambda i: (0, 0)),
        ],
        out_specs=pl.BlockSpec((STEP, width), lambda i: (samples // STEP - 1, 0)),
        out_shape=jax.ShapeDtypeStruct(grad.shape, BF16),
        input_output_aliases={0: 0},
        compiler_params=pltpu.CompilerParams(vmem_limit_bytes=SIDE_VMEM_BYTES),
    )(grad, rest, halo, wd)


def total_kernel(parts, wd, wot, wct, u1t, u2t, gb, ob, total):
    step = pl.program_id(0)

    @pl.when(step == 0)
    def _():
        total[...] = jnp.zeros_like(total)

    total[...] += jnp.sum(parts[...].astype(F32), 0)

    @pl.when(step == pl.num_programs(0) - 1)
    def _():
        for j in range(8):
            wd[:, LANES * j : LANES * (j + 1)] = total[8 * j : 8 * j + 8, :]
        for j in range(4):
            wot[:, LANES * j : LANES * (j + 1)] = total[64 + 8 * j : 72 + 8 * j, :]
        wct[...] = total[96:104, :CM]
        u1t[...] = total[104:124, :CM]
        u2t[...] = total[124:144, :CM]
        diagonal = lax.broadcasted_iota(jnp.int32, (8, 8), 0) == lax.broadcasted_iota(jnp.int32, (8, 8), 1)
        for lane, out in ((CM, gb), (CM + 1, ob)):
            column = jnp.broadcast_to(total[96:104, lane : lane + 1], (8, 8))
            out[...] = jnp.sum(jnp.where(diagonal, column, 0.0), 0, keepdims=True)


def total_pass(parts):
    shapes = [(8, 1024), (8, 512), (8, CM), (SHARE, CM), (SHARE, CM), (1, 8), (1, 8)]
    return pl.pallas_call(
        total_kernel,
        grid=(4,),
        in_specs=[pl.BlockSpec((16, LINES, LANES), lambda i: (i, 0, 0))],
        out_specs=[pl.BlockSpec(s, lambda i: (0, 0)) for s in shapes],
        out_shape=[jax.ShapeDtypeStruct(s, F32) for s in shapes],
        scratch_shapes=[pltpu.VMEM((LINES, LANES), F32)],
    )(parts)


def tail_pass(dp, gated, audio, g_res, mask, wd, wot, ob, tile):
    samples, width = audio.shape
    rows = pl.BlockSpec((tile, width), lambda i: (i, 0))
    step_blocks = tile // STEP
    final = samples // STEP - 1

    def whole(shape):
        return pl.BlockSpec(shape, lambda i: (0,) * len(shape))

    shape = jax.ShapeDtypeStruct((samples, width), BF16)
    return pl.pallas_call(
        tail_kernel,
        grid=(samples // tile,),
        in_specs=[
            pl.BlockSpec((tile, 2 * width), lambda i: (i, 0)),
            pl.BlockSpec((STEP, 2 * width), lambda i: (jnp.minimum((i + 1) * step_blocks, final), 0)),
            rows,
            rows,
            rows,
            pl.BlockSpec((tile, LANES), lambda i: (i, 0)),
            pl.BlockSpec((STEP, LANES), lambda i: (jnp.minimum((i + 1) * step_blocks, final), 0)),
            whole(wd.shape),
            whole(wot.shape),
            whole((2, 2 * width)),
        ],
        out_specs=[rows] * 3 + [whole((STEP, width))],
        out_shape=[shape] * 3 + [jax.ShapeDtypeStruct((STEP, width), F32)],
        scratch_shapes=[
            pltpu.VMEM((2 * width, 2 * width), BF16),
            pltpu.VMEM((width, 2 * width), BF16),
        ],
        compiler_params=pltpu.CompilerParams(vmem_limit_bytes=SIDE_VMEM_BYTES),
        cost_estimate=pl.CostEstimate(
            flops=13_000_000_000, bytes_accessed=20 * samples * width, transcendentals=0
        ),
    )(dp, dp, gated, audio, g_res, mask, mask, wd, wot, ob)


def shifted(value, steps, count=8):
    first, last = max(0, -steps), min(count, count - steps)
    return lax.ppermute(value, SEQ, [(s, s + steps) for s in range(first, last)])


def no_change(value):
    return jnp.minimum(jnp.abs(value), 0)


def swap(value):
    return lax.ppermute(value, "c", [(0, 1), (1, 0)])


def on_device(
    residual_input, mel_input_frames, starts, resets, residual_gradient, skip_gradient,
    first_upsample_weight, second_upsample_weight, conditioning_weight, dilated_weight,
    gate_bias_vector, output_weight, output_bias_vector,
):
    core = lax.axis_index("c")
    audio, mel = residual_input[0], mel_input_frames[0]
    g_res, g_skip = residual_gradient[0], skip_gradient[0]
    samples, width = audio.shape
    frames = mel.shape[0]

    tails = jnp.concatenate([audio[-STEP:], jnp.pad(mel[-2:], ((0, 14), (0, width - CM)))], 0)
    tails = shifted(tails, 1)

    shares = spread(
        dilated_weight,
        output_weight.T,
        conditioning_weight.T,
        first_upsample_weight.T,
        second_upsample_weight.T,
        gate_bias_vector[None],
        output_bias_vector[None],
    )
    own = lax.all_to_all(shares, CHIPS, 0, 0)

    mel_tail = tails[STEP : STEP + 2, :CM]
    mel_ext = jnp.concatenate([mel_tail, mel, jnp.zeros((14, CM), BF16)], 0)
    mel_ext = jnp.pad(mel_ext, ((0, 0), (0, LANES - CM)))
    mel_b, mel_a = mel_ext[: 2 * frames - 8], mel_ext[1 : 2 * frames - 7]
    seq_at = lax.axis_index(SEQ).astype(jnp.int32)[None]
    mask, xt, gt, g_sum = turn(starts, seq_at, resets, audio, g_res, g_skip, 512)

    own = own + no_change(jnp.abs(g_sum[0, 0]) + jnp.abs(mel_a[0, 0]).astype(F32)).astype(BF16)
    other = swap(own)

    dp, gated, stay, send, wd, wot, halo, mel_here, biases = main_pass(
        core.astype(jnp.int32)[None], mel_a, mel_b, tails, audio, g_res, g_skip, mask, xt, gt, g_sum, own, other, 512
    )

    came = swap(send)
    pair = stay + came
    all_parts = lax.all_to_all(pair, CHIPS, 0, 0)

    late = no_change(pair[0, 0, 0])
    halo_next = shifted(halo + late, -1)
    res_out, skip_out, res_grad, rest = tail_pass(
        dp, gated, audio, g_res, mask, wd, wot, biases + late.astype(F32), 512
    )
    res_grad = fix_pass(res_grad, rest, halo_next, wd)
    mel_back = halo_next[STEP : STEP + 2, :CM].astype(F32)
    mel_grad = mel_here[:, :CM] + jnp.pad(mel_back, ((frames - 2, 0), (0, 0)))

    d_wd, d_wot, d_wct, d_u1t, d_u2t, d_gb, d_ob = total_pass(all_parts)
    return (
        res_out[None],
        skip_out[None],
        res_grad[None],
        mel_grad.astype(BF16)[None],
        d_u1t.T,
        d_u2t.T,
        d_wct.T,
        d_wd,
        d_gb[0],
        d_wot.T,
        d_ob[0],
    )


def solution(mesh):
    fine = Mesh(mesh.devices.reshape(4, 2, 2, 2, 4), ("y", "xh", "c", "xl", "z"))
    dp, seq = ("y", "xh", "c"), ("xl", "z")
    every = dp + seq
    return jax.shard_map(
        on_device,
        mesh=fine,
        in_specs=(
            P(dp, seq, None),
            P(dp, seq, None),
            P(dp, None),
            P(dp, seq),
            P(dp, seq, None),
            P(dp, seq, None),
            P(None, every),
            P(None, every),
            P(None, every),
            P(every, None),
            P(every),
            P(None, every),
            P(every),
        ),
        out_specs=(
            P(dp, seq, None),
            P(dp, seq, None),
            P(dp, seq, None),
            P(dp, seq, None),
            P(None, every),
            P(None, every),
            P(None, every),
            P(every, None),
            P(every),
            P(None, every),
            P(every),
        ),
        check_vma=False,
    )
```

```python
import jax
import jax.numpy as jnp
from jax import lax
from jax.experimental import pallas as pl
from jax.experimental.pallas import tpu as pltpu
from jax.sharding import Mesh, PartitionSpec as P

STEP = 64
SEQ = ("xl", "z")
CHIPS = ("y", "xh", "xl", "z")
BF16 = jnp.bfloat16
F32 = jnp.float32
LANES = 128
TAPS = 32
HALF_TAPS = 16
CM = 80
SHARE = 20
LINES = 128
BIG = 96
VMEM_BYTES = 50 * 1024 * 1024
SIDE_VMEM_BYTES = 60 * 1024 * 1024
TAIL_VMEM_BYTES = 40 * 1024 * 1024


def dot(a, b):
    return jnp.dot(a, b, preferred_element_type=F32)


def dot_nt(a, b):
    return lax.dot_general(a, b, (((1,), (1,)), ((), ())), preferred_element_type=F32)


def dot_tn(a, b):
    return lax.dot_general(a, b, (((0,), (0,)), ((), ())), preferred_element_type=F32)


def lane_mask(rows):
    return lax.broadcasted_iota(jnp.int32, (rows, LANES), 1) < CM


SPLIT = LANES - CM
PIECE = CM - SPLIT


def fold(head, u1, u2):
    u2 = jnp.concatenate([u2, jnp.zeros((4, LANES), F32)], 0)
    lane = lax.broadcasted_iota(jnp.int32, (24, LANES), 1)
    top = jnp.where(lane[:8] < LANES - PIECE, head, pltpu.roll(u2[:8], LANES - PIECE - SPLIT, 1))
    middle = jnp.where(lane[:SHARE] < CM, u1, pltpu.roll(u2, CM, 1)[:SHARE])
    last = jnp.zeros((3, LANES), F32)
    for g in range(4):
        moved = pltpu.roll(u2, (PIECE * g - SPLIT) % LANES, 1)[8 + 3 * g : 11 + 3 * g]
        last = jnp.where(lane[:3] // PIECE == g, moved, last)
    return jnp.concatenate([top, middle, last, jnp.zeros((1, LANES), F32)], 0)


def unfold(rows):
    lane = lax.broadcasted_iota(jnp.int32, (SHARE, LANES), 1)
    low = pltpu.roll(rows[8:], LANES - CM, 1)[:SHARE]
    high = [pltpu.roll(rows[:8], (SPLIT - LANES + PIECE) % LANES, 1)]
    for g in range(4):
        high.append(pltpu.roll(rows[24:], (SPLIT - PIECE * g) % LANES, 1)[4:7])
    u2 = jnp.where(lane < SPLIT, low, jnp.concatenate(high, 0))
    return rows[:8], rows[8 : 8 + SHARE], u2


def spread_kernel(wd, wot, wct, u1t, u2t, gb, ob, out, lines, narrow):
    for j in range(8):
        lines[8 * j : 8 * j + 8, :] = wd[:, LANES * j : LANES * (j + 1)].astype(F32)
    for j in range(4):
        lines[64 + 8 * j : 72 + 8 * j, :] = wot[:, LANES * j : LANES * (j + 1)].astype(F32)
    lane = lax.broadcasted_iota(jnp.int32, (8, LANES), 1)
    diagonal = lax.broadcasted_iota(jnp.int32, (8, 8), 0) == lax.broadcasted_iota(jnp.int32, (8, 8), 1)

    def column(row):
        full = jnp.broadcast_to(row[...].astype(F32), (8, 8))
        return jnp.sum(jnp.where(diagonal, full, 0.0), 1, keepdims=True)

    narrow[...] = jnp.zeros_like(narrow)
    narrow[:8, :CM] = wct[...].astype(F32)
    narrow[8 : 8 + SHARE, :CM] = u1t[...].astype(F32)
    narrow[32 : 32 + SHARE, :CM] = u2t[...].astype(F32)
    biases = jnp.where(lane == CM, column(gb), jnp.where(lane == CM + 1, column(ob), 0.0))
    lines[BIG:, :] = fold(narrow[:8, :] + biases, narrow[8 : 8 + SHARE, :], narrow[32 : 32 + SHARE, :])
    block = lines[...].astype(BF16)
    for k in range(out.shape[0]):
        out[k] = block


def spread(wd, wot, wct, u1t, u2t, gb, ob):
    return pl.pallas_call(
        spread_kernel,
        out_shape=jax.ShapeDtypeStruct((64, LINES, LANES), BF16),
        scratch_shapes=[pltpu.VMEM((LINES, LANES), F32), pltpu.VMEM((56, LANES), F32)],
    )(wd, wot, wct, u1t, u2t, gb, ob)


def masked_past(before, audio, column):
    tile, half = audio.shape
    moved = jnp.concatenate([before, audio[: tile - STEP, :]], 0)
    return moved * jnp.concatenate([column] * (half // LANES), 1)


def turn_kernel(starts, seq_at, resets, audio_before, audio, g_res, g_skip, mask, xt, gt, g_sum):
    step = pl.program_id(0)
    tile, half = audio.shape
    position = (seq_at[0] * pl.num_programs(0) + step) * tile + lax.broadcasted_iota(jnp.int32, (1, tile), 1)
    blocked = position < STEP
    for k in range(starts.shape[1]):
        first = starts[0, k]
        blocked = blocked | ((first > position - STEP) & (first <= position))
    keep = jnp.where(blocked, 0, resets[...]).astype(F32)
    column = jnp.broadcast_to(keep, (LANES, tile)).T.astype(BF16)
    mask[...] = column
    before = jnp.where(step == 0, jnp.zeros_like(audio_before[...]), audio_before[...])
    xt[:half, :] = masked_past(before, audio[...], column).T
    xt[half:, :] = audio[...].T
    gt[:half, :] = g_res[...].T
    gt[half:, :] = g_skip[...].T

    @pl.when(step == 0)
    def _():
        g_sum[...] = jnp.zeros_like(g_sum)

    g_sum[:, :half] += jnp.sum(g_res[...].astype(F32), 0, keepdims=True)
    g_sum[:, half:] += jnp.sum(g_skip[...].astype(F32), 0, keepdims=True)


def turn(starts, seq_at, resets, audio, g_res, g_skip, tile):
    samples, width = audio.shape
    steps = tile // STEP
    rows = pl.BlockSpec((tile, width), lambda i: (i, 0))
    cols = pl.BlockSpec((2 * width, tile), lambda i: (0, i))
    scalars = pl.BlockSpec(memory_space=pltpu.SMEM)
    shape = jax.ShapeDtypeStruct((2 * width, samples), BF16)
    return pl.pallas_call(
        turn_kernel,
        grid=(samples // tile,),
        in_specs=[
            scalars,
            scalars,
            pl.BlockSpec((1, tile), lambda i: (0, i)),
            pl.BlockSpec((STEP, width), lambda i: (jnp.maximum(i * steps - 1, 0), 0)),
            rows,
            rows,
            rows,
        ],
        out_specs=[
            pl.BlockSpec((tile, LANES), lambda i: (i, 0)),
            cols,
            cols,
            pl.BlockSpec((1, 2 * width), lambda i: (0, 0)),
        ],
        out_shape=[
            jax.ShapeDtypeStruct((samples, LANES), BF16),
            shape,
            shape,
            jax.ShapeDtypeStruct((1, 2 * width), F32),
        ],
        compiler_params=pltpu.CompilerParams(vmem_limit_bytes=SIDE_VMEM_BYTES),
        cost_estimate=pl.CostEstimate(flops=0, bytes_accessed=18 * samples * width, transcendentals=0),
    )(starts, seq_at, resets, audio, audio, g_res, g_skip)


def unpack_wide(ref, a, side, wd, wot):
    for b in range(0, 8, 2):
        rows = pl.ds(pl.multiple_of(a * 128 + side * 64 + b * 8, 16), 16)
        pair = [a * 8 + b, a * 8 + b + 1]
        for out, first, count in ((wd, 0, 4), (wot, 64, 2)):
            for m in range(count):
                two = [ref[k, pl.ds(first + 16 * m, 16), :].astype(F32) for k in pair]
                out[rows, pl.ds(256 * m, 128)] = jnp.concatenate([t[:8] for t in two], 0).astype(BF16)
                out[rows, pl.ds(256 * m + 128, 128)] = jnp.concatenate([t[8:] for t in two], 0).astype(BF16)


def main_kernel(
    core, mel_a, mel_b, tails, audio_before, audio, g_res, g_skip, mask, xt, gt, g_sum, own, other,
    dp_out, gated_out, stay, send, halo, mel_here, ob,
    wd, wot, wct, u1t, u2t, wc, inter, cond_all, dcond_all, dinter, xg, owg, du, mine, theirs, in_sems, out_sems,
):
    step = pl.program_id(0)
    tile = audio.shape[0]
    half = audio.shape[1]
    frames = cond_all.shape[0] // HALF_TAPS
    first_rows = mel_a.shape[0]
    @pl.when(step == 0)
    def _():
        fetch = [pltpu.make_async_copy(a, b, in_sems.at[k]) for k, (a, b) in enumerate(((own, mine), (other, theirs)))]
        for copy in fetch:
            copy.start()
        xg[...] = jnp.zeros_like(xg)
        owg[...] = jnp.zeros_like(owg)
        xg[2 * half + CM + 1 : 2 * half + CM + 2, :] = g_sum[...]
        u1t[HALF_TAPS * CM :, :] = jnp.zeros_like(u1t[HALF_TAPS * CM :, :])
        u2t[HALF_TAPS * CM :, :] = jnp.zeros_like(u2t[HALF_TAPS * CM :, :])
        for copy in fetch:
            copy.wait()

        def unpack(a, _):
            for ref, side in ((mine, core[0]), (theirs, 1 - core[0])):
                unpack_wide(ref, a, side, wd, wot)
                for b in range(0, 8, 2):
                    rows = pl.ds(pl.multiple_of(a * 128 + side * 64 + b * 8, 16), 16)
                    two = [ref[a * 8 + b + k, pl.ds(BIG, 16), :].astype(F32) for k in range(2)]
                    wct[rows, :] = jnp.concatenate([t[:8] for t in two], 0).astype(BF16)
                for b in range(0, 8, 4):
                    tap_row = pl.multiple_of((a % 4 * 16 + side * 8 + b) * SHARE, 16)
                    lanes = pl.ds(pl.multiple_of(a // 4 * LANES, LANES), LANES)
                    four = [unfold(ref[a * 8 + b + k, pl.ds(BIG, 32), :].astype(F32)) for k in range(4)]
                    for k, out in ((1, u1t), (2, u2t)):
                        out[pl.ds(tap_row, CM), lanes] = jnp.concatenate([t[k] for t in four], 0).astype(BF16)
            return _

        lax.fori_loop(0, 8, unpack, 0)
        wc[...] = wct[...].T
        ob[...] = wc[CM : CM + 2, :].astype(F32)
        keep = lane_mask(first_rows)
        mels = jnp.concatenate([mel_a[...], mel_b[...]], 1)
        for r in range(HALF_TAPS):
            both = dot_nt(mels, u1t[pl.ds(CM * r, LANES), :])
            rounded = jnp.where(keep, both, 0.0).astype(BF16).astype(F32)
            inter[pl.ds(r, first_rows, stride=HALF_TAPS), :] = rounded
        rows_a = inter[pl.ds(HALF_TAPS, frames), :].astype(BF16)
        rows_b = inter[pl.ds(HALF_TAPS - 1, frames), :].astype(BF16)
        lane = lax.broadcasted_iota(jnp.int32, (frames, LANES), 1)
        one = jnp.where(lane == CM, 1.0, 0.0)
        rows_ab = jnp.concatenate([rows_a, rows_b], 1)
        for r in range(HALF_TAPS):
            both = dot_nt(rows_ab, u2t[pl.ds(CM * r, LANES), :])
            cond_all[pl.ds(r, frames, stride=HALF_TAPS), :] = jnp.where(lane < CM, both, one)

    at = pl.multiple_of(step * tile, tile)
    cond = cond_all[pl.ds(at, tile), :].astype(BF16)
    past = masked_past(jnp.where(step == 0, tails[...], audio_before[...]), audio[...], mask[...])
    pre = dot(past, wd[:half, :]) + dot(audio[...], wd[half:, :]) + dot(cond, wc[...])
    th = jnp.tanh(pre[:, :half])
    sg = 0.5 * jnp.tanh(0.5 * pre[:, half:]) + 0.5
    gated = (th * sg).astype(BF16)
    gated_out[...] = gated
    dg = dot(g_res[...], wot[:half, :]) + dot(g_skip[...], wot[half:, :])
    dgs = dg * sg
    dp = jnp.concatenate([dgs * (1.0 - th * th), dgs * th * (1.0 - sg)], 1).astype(BF16)
    dp_out[...] = dp
    dcond_all[pl.ds(at, tile), :] = dot(dp, wct[...])
    owg[...] += dot(gt[...], gated)
    xg[...] += dot(jnp.concatenate([xt[...], cond.T], 0), dp)

    @pl.when(step == 0)
    def _():
        xg[:half, :] += dot_tn(past[:STEP, :], dp[:STEP, :])
        halo[:STEP, :] = dp[:STEP, :] * jnp.concatenate([mask[:STEP, :]] * (2 * half // LANES), 1)

    @pl.when(step == pl.num_programs(0) - 1)
    def _():
        def give(a, k, first, count):
            part, lines = pl.ds(pl.multiple_of(a * 8, 8), 8), pl.ds(first, count)
            src, dst = ((mine, stay), (theirs, send))[k]
            return pltpu.make_async_copy(src.at[part, lines], dst.at[part, lines], out_sems.at[first // BIG, k, a])

        def pack_big(a, _):
            for k, (out, side) in enumerate(((mine, core[0]), (theirs, 1 - core[0]))):
                for b in range(8):
                    rows = pl.ds(pl.multiple_of(a * 128 + side * 64 + b * 8, 8), 8)
                    place = a * 8 + b
                    for m in range(4):
                        two = [xg[rows, pl.ds(256 * m, 128)], xg[rows, pl.ds(256 * m + 128, 128)]]
                        out[place, pl.ds(16 * m, 16), :] = jnp.concatenate(two, 0).astype(BF16)
                    for m in range(2):
                        two = [owg[rows, pl.ds(256 * m, 128)], owg[rows, pl.ds(256 * m + 128, 128)]]
                        out[place, pl.ds(64 + 16 * m, 16), :] = jnp.concatenate(two, 0).astype(BF16)
                give(a, k, 0, BIG).start()
            return _

        lax.fori_loop(0, 8, pack_big, 0)
        rows_a = inter[pl.ds(HALF_TAPS, frames), :].astype(BF16)
        rows_b = inter[pl.ds(HALF_TAPS - 1, frames), :].astype(BF16)
        both = jnp.concatenate([rows_a, rows_b], 1)
        keep = lane_mask(frames)
        sums = jnp.zeros((frames, 2 * LANES), F32)

        def put(grads, tap, first):
            for q in range(CM // SHARE):
                du[pl.ds((CM // SHARE * tap + q) * 2 * SHARE + first, SHARE), :] = grads[SHARE * q : SHARE * (q + 1)]

        for r in range(HALF_TAPS):
            e = jnp.where(keep, dcond_all[pl.ds(r, frames, stride=HALF_TAPS), :], 0.0).astype(BF16)
            grads = dot_tn(e, both)
            put(grads[:, :LANES], r, SHARE)
            put(grads[:, LANES:], r + HALF_TAPS, SHARE)
            sums += dot(e, u2t[pl.ds(CM * r, LANES), :])
        dinter[...] = jnp.zeros_like(dinter)
        dinter[pl.ds(HALF_TAPS, frames), :] = sums[:, :LANES]
        dinter[pl.ds(HALF_TAPS - 1, frames), :] += sums[:, LANES:]
        mels = jnp.concatenate([mel_a[...], mel_b[...]], 1)
        keep = lane_mask(first_rows)
        mel_sums = jnp.zeros((first_rows, 2 * LANES), F32)
        for r in range(HALF_TAPS):
            f = jnp.where(keep, dinter[pl.ds(r, first_rows, stride=HALF_TAPS), :], 0.0).astype(BF16)
            grads = dot_tn(f, mels)
            put(grads[:, :LANES], r, 0)
            put(grads[:, LANES:], r + HALF_TAPS, 0)
            mel_sums += dot(f, u1t[pl.ds(CM * r, LANES), :])
        zero = jnp.zeros((1, LANES), F32)
        mel_sum = jnp.concatenate([zero, mel_sums[:, :LANES]], 0) + jnp.concatenate([mel_sums[:, LANES:], zero], 0)
        real = mel_here.shape[0]
        mel_here[...] = mel_sum[2 : 2 + real]
        halo[STEP:, :] = jnp.zeros_like(halo[STEP:, :])
        halo[STEP:, :LANES] = jnp.concatenate([mel_sum[:2], jnp.zeros((14, LANES), F32)], 0).astype(BF16)
        cwgt = xg[2 * half :, :].T
        dcond_all[: cwgt.shape[0], :] = cwgt

        def pack_small(a, _):
            for k, (out, side) in enumerate(((mine, core[0]), (theirs, 1 - core[0]))):
                for b in range(8):
                    at_row = pl.multiple_of(a * 128 + side * 64 + b * 8, 8)
                    narrow = du[pl.ds(pl.multiple_of(at_row * 5, 8), 2 * SHARE), :]
                    folded = fold(dcond_all[pl.ds(at_row, 8), :], narrow[:SHARE], narrow[SHARE:])
                    out[a * 8 + b, pl.ds(BIG, LINES - BIG), :] = folded.astype(BF16)
                give(a, k, BIG, LINES - BIG).start()
            return _

        lax.fori_loop(0, 8, pack_small, 0)

        def finish(a, _):
            for k in range(2):
                give(a, k, 0, BIG).wait()
                give(a, k, BIG, LINES - BIG).wait()
            return _

        lax.fori_loop(0, 8, finish, 0)


def main_pass(core, mel_a, mel_b, tails, audio, g_res, g_skip, mask, xt, gt, g_sum, own, other, tile):
    samples, width = audio.shape
    first_rows = mel_a.shape[0]
    rows = pl.BlockSpec((tile, width), lambda i: (i, 0))
    cols = pl.BlockSpec((2 * width, tile), lambda i: (0, i))

    def whole(shape):
        return pl.BlockSpec(shape, lambda i: (0,) * len(shape))

    anywhere = pl.BlockSpec(memory_space=pl.ANY)
    hbm = pl.BlockSpec(memory_space=pltpu.HBM)
    packed = (64, LINES, LANES)
    outs = [
        ((samples, 2 * width), BF16),
        ((samples, width), BF16),
        (packed, BF16),
        (packed, BF16),
        ((STEP + 16, 2 * width), BF16),
        ((samples // (HALF_TAPS * HALF_TAPS), LANES), F32),
        ((2, 2 * width), F32),
    ]
    return pl.pallas_call(
        main_kernel,
        grid=(samples // tile,),
        in_specs=[pl.BlockSpec(memory_space=pltpu.SMEM)]
        + [whole(mel_a.shape), whole(mel_b.shape), whole((STEP, width))]
        + [pl.BlockSpec((STEP, width), lambda i: (jnp.maximum(i * (tile // STEP) - 1, 0), 0))]
        + [rows, rows, rows, pl.BlockSpec((tile, LANES), lambda i: (i, 0)), cols, cols]
        + [whole(g_sum.shape), anywhere, anywhere],
        out_specs=[
            pl.BlockSpec((tile, 2 * width), lambda i: (i, 0)),
            pl.BlockSpec((tile, width), lambda i: (i, 0)),
        ]
        + [hbm] * 2
        + [whole(s) for s, _ in outs[4:]],
        out_shape=[jax.ShapeDtypeStruct(s, d) for s, d in outs],
        scratch_shapes=[
            pltpu.VMEM((2 * width, 2 * width), BF16),
            pltpu.VMEM((2 * width, width), BF16),
            pltpu.VMEM((2 * width, LANES), BF16),
            pltpu.VMEM((HALF_TAPS * CM + 48, 2 * LANES), BF16),
            pltpu.VMEM((HALF_TAPS * CM + 48, 2 * LANES), BF16),
            pltpu.VMEM((LANES, 2 * width), BF16),
            pltpu.VMEM((first_rows * HALF_TAPS, LANES), F32),
            pltpu.VMEM((samples, LANES), F32),
            pltpu.VMEM((samples, LANES), F32),
            pltpu.VMEM((first_rows * HALF_TAPS, LANES), F32),
            pltpu.VMEM((2 * width + LANES, 2 * width), F32),
            pltpu.VMEM((2 * width, width), F32),
            pltpu.VMEM((2 * TAPS * CM, LANES), F32),
            pltpu.VMEM(packed, BF16),
            pltpu.VMEM(packed, BF16),
            pltpu.SemaphoreType.DMA((2,)),
            pltpu.SemaphoreType.DMA((2, 2, 8)),
        ],
        compiler_params=pltpu.CompilerParams(vmem_limit_bytes=VMEM_BYTES),
        cost_estimate=pl.CostEstimate(
            flops=28_000_000_000, bytes_accessed=48 * samples * width, transcendentals=0
        ),
    )(core, mel_a, mel_b, tails, audio, audio, g_res, g_skip, mask, xt, gt, g_sum, own, other)


def tail_kernel(
    core, dp, dp_next, gated, audio, g_res, mask, mask_next, own, other, ob,
    res_out, skip_out, res_grad, rest, wd_past,
    wd, wot, wdt, wo, mine, theirs, in_sems,
):
    step = pl.program_id(0)
    tile, half = audio.shape

    @pl.when(step == 0)
    def _():
        fetch = [pltpu.make_async_copy(a, b, in_sems.at[k]) for k, (a, b) in enumerate(((own, mine), (other, theirs)))]
        for copy in fetch:
            copy.start()
        for copy in fetch:
            copy.wait()

        def unpack(a, _):
            for ref, side in ((mine, core[0]), (theirs, 1 - core[0])):
                unpack_wide(ref, a, side, wd, wot)
            return _

        lax.fori_loop(0, 8, unpack, 0)
        wdt[...] = wd[...].T
        wo[...] = wot[...].T
        wd_past[...] = wdt[:, :half]

    out = dot(gated[...], wo[...]) + ob[1:2, :]
    res_out[...] = (audio[...].astype(F32) + out[:, :half]).astype(BF16)
    skip_out[...] = out[:, half:].astype(BF16)
    last = step == pl.num_programs(0) - 1
    after = jnp.where(last, jnp.zeros_like(dp_next[...]), dp_next[...])
    ahead = jnp.concatenate([dp[STEP:, :], after], 0)
    d_past = dot(ahead, wdt[:, :half]).astype(BF16)
    kept = jnp.concatenate([mask[STEP:, :], mask_next[...]], 0)
    d_past = (d_past * jnp.concatenate([kept] * (half // LANES), 1)).astype(F32)
    here = g_res[...].astype(F32) + dot(dp[...], wdt[:, half:])
    rest[...] = here[tile - STEP :, :]
    res_grad[...] = (here + d_past).astype(BF16)


def tail_pass(core, dp, gated, audio, g_res, mask, own, other, ob, tile):
    samples, width = audio.shape
    rows = pl.BlockSpec((tile, width), lambda i: (i, 0))
    anywhere = pl.BlockSpec(memory_space=pl.ANY)
    step_blocks = tile // STEP
    final = samples // STEP - 1

    def whole(shape):
        return pl.BlockSpec(shape, lambda i: (0,) * len(shape))

    shape = jax.ShapeDtypeStruct((samples, width), BF16)
    return pl.pallas_call(
        tail_kernel,
        grid=(samples // tile,),
        in_specs=[
            pl.BlockSpec(memory_space=pltpu.SMEM),
            pl.BlockSpec((tile, 2 * width), lambda i: (i, 0)),
            pl.BlockSpec((STEP, 2 * width), lambda i: (jnp.minimum((i + 1) * step_blocks, final), 0)),
            rows,
            rows,
            rows,
            pl.BlockSpec((tile, LANES), lambda i: (i, 0)),
            pl.BlockSpec((STEP, LANES), lambda i: (jnp.minimum((i + 1) * step_blocks, final), 0)),
            anywhere,
            anywhere,
            whole((2, 2 * width)),
        ],
        out_specs=[rows] * 3 + [whole((STEP, width)), whole((2 * width, width))],
        out_shape=[shape] * 3
        + [jax.ShapeDtypeStruct((STEP, width), F32), jax.ShapeDtypeStruct((2 * width, width), BF16)],
        scratch_shapes=[
            pltpu.VMEM((2 * width, 2 * width), BF16),
            pltpu.VMEM((2 * width, width), BF16),
            pltpu.VMEM((2 * width, 2 * width), BF16),
            pltpu.VMEM((width, 2 * width), BF16),
            pltpu.VMEM(own.shape, BF16),
            pltpu.VMEM(own.shape, BF16),
            pltpu.SemaphoreType.DMA((2,)),
        ],
        compiler_params=pltpu.CompilerParams(vmem_limit_bytes=TAIL_VMEM_BYTES),
        cost_estimate=pl.CostEstimate(
            flops=13_000_000_000, bytes_accessed=20 * samples * width, transcendentals=0
        ),
    )(core, dp, dp, gated, audio, g_res, mask, mask, own, other, ob)


def end_kernel(
    grad, rest, halo, wd_past, mel_here, parts,
    out, mel_out, wd, wot, wct, u1t, u2t, gb, ob,
    total,
):
    step = pl.program_id(0)

    @pl.when(step == 0)
    def _():
        total[...] = jnp.zeros_like(total)
        out[...] = (rest[...] + dot(halo[:STEP, :], wd_past[...]).astype(BF16).astype(F32)).astype(BF16)
        frames = mel_here.shape[0]
        back = halo[STEP:, :LANES].astype(F32)[:2]
        mel = mel_here[...] + jnp.concatenate([jnp.zeros((frames - 2, LANES), F32), back], 0)
        mel_out[...] = mel[:, :CM].astype(BF16)

    total[...] += jnp.sum(parts[...].astype(F32), 0)

    @pl.when(step == pl.num_programs(0) - 1)
    def _():
        for j in range(8):
            wd[:, LANES * j : LANES * (j + 1)] = total[8 * j : 8 * j + 8, :]
        for j in range(4):
            wot[:, LANES * j : LANES * (j + 1)] = total[64 + 8 * j : 72 + 8 * j, :]
        head, u1, u2 = unfold(total[BIG:, :])
        wct[...] = head[:, :CM]
        u1t[...] = u1[:, :CM]
        u2t[...] = u2[:, :CM]
        diagonal = lax.broadcasted_iota(jnp.int32, (8, 8), 0) == lax.broadcasted_iota(jnp.int32, (8, 8), 1)
        for lane, row in ((CM, gb), (CM + 1, ob)):
            column = jnp.broadcast_to(head[:, lane : lane + 1], (8, 8))
            row[...] = jnp.sum(jnp.where(diagonal, column, 0.0), 0, keepdims=True)


def end_pass(grad, rest, halo, wd_past, mel_here, parts):
    samples, width = grad.shape
    frames = mel_here.shape[0]
    steps = 4
    shapes = [(8, 1024), (8, 512), (8, CM), (SHARE, CM), (SHARE, CM), (1, 8), (1, 8)]

    def whole(shape):
        return pl.BlockSpec(shape, lambda i: (0,) * len(shape))

    return pl.pallas_call(
        end_kernel,
        grid=(steps,),
        in_specs=[pl.BlockSpec(memory_space=pl.ANY)]
        + [whole(s) for s in ((STEP, width), halo.shape, wd_past.shape, mel_here.shape)]
        + [pl.BlockSpec((64 // steps, LINES, LANES), lambda i: (i, 0, 0))],
        out_specs=[pl.BlockSpec((STEP, width), lambda i: (samples // STEP - 1, 0))]
        + [whole(s) for s in [(frames, CM)] + shapes],
        out_shape=[jax.ShapeDtypeStruct(grad.shape, BF16), jax.ShapeDtypeStruct((frames, CM), BF16)]
        + [jax.ShapeDtypeStruct(s, F32) for s in shapes],
        scratch_shapes=[pltpu.VMEM((LINES, LANES), F32)],
        input_output_aliases={0: 0},
        compiler_params=pltpu.CompilerParams(vmem_limit_bytes=SIDE_VMEM_BYTES),
    )(grad, rest, halo, wd_past, mel_here, parts)


def shifted(value, steps, count=8):
    first, last = max(0, -steps), min(count, count - steps)
    return lax.ppermute(value, SEQ, [(s, s + steps) for s in range(first, last)])


def no_change(value):
    return jnp.minimum(jnp.abs(value), 0)


def swap(value):
    return lax.ppermute(value, "c", [(0, 1), (1, 0)])


def on_device(
    residual_input, mel_input_frames, starts, resets, residual_gradient, skip_gradient,
    first_upsample_weight, second_upsample_weight, conditioning_weight, dilated_weight,
    gate_bias_vector, output_weight, output_bias_vector,
):
    core = lax.axis_index("c")
    audio, mel = residual_input[0], mel_input_frames[0]
    g_res, g_skip = residual_gradient[0], skip_gradient[0]
    samples, width = audio.shape
    frames = mel.shape[0]

    tails = jnp.concatenate([audio[-STEP:], jnp.pad(mel[-2:], ((0, 14), (0, width - CM)))], 0)
    tails = shifted(tails, 1)

    shares = spread(
        dilated_weight,
        output_weight.T,
        conditioning_weight.T,
        first_upsample_weight.T,
        second_upsample_weight.T,
        gate_bias_vector[None],
        output_bias_vector[None],
    )
    own = lax.all_to_all(shares, CHIPS, 0, 0)

    mel_tail = tails[STEP : STEP + 2, :CM]
    mel_ext = jnp.concatenate([mel_tail, mel, jnp.zeros((14, CM), BF16)], 0)
    mel_ext = jnp.pad(mel_ext, ((0, 0), (0, LANES - CM)))
    mel_b, mel_a = mel_ext[: 2 * frames - 8], mel_ext[1 : 2 * frames - 7]
    seq_at = lax.axis_index(SEQ).astype(jnp.int32)[None]
    mask, xt, gt, g_sum = turn(starts, seq_at, resets, audio, g_res, g_skip, 512)

    zero = no_change(jnp.abs(g_sum[0, 0]) + jnp.abs(mel_a[0, 0]).astype(F32)).astype(BF16)
    own = lax.dynamic_update_slice(own, own[:1, :16] + zero, (0, 0, 0))
    other = swap(own)

    core = core.astype(jnp.int32)[None]
    dp, gated, stay, send, halo, mel_here, biases = main_pass(
        core, mel_a, mel_b, tails, audio, g_res, g_skip, mask, xt, gt, g_sum, own, other, 512
    )

    came = swap(send)
    pair = stay + came
    all_parts = lax.all_to_all(pair, CHIPS, 0, 0)

    late = no_change(pair[0, 0, 0])
    halo_next = shifted(halo + late, -1)
    res_out, skip_out, res_grad, rest, wd_past = tail_pass(
        core, dp, gated, audio, g_res, mask, own, other, biases + late.astype(F32), 512
    )
    res_grad, mel_grad, d_wd, d_wot, d_wct, d_u1t, d_u2t, d_gb, d_ob = end_pass(
        res_grad, rest, halo_next, wd_past, mel_here, all_parts
    )
    return (
        res_out[None],
        skip_out[None],
        res_grad[None],
        mel_grad[None],
        d_u1t.T,
        d_u2t.T,
        d_wct.T,
        d_wd,
        d_gb[0],
        d_wot.T,
        d_ob[0],
    )


def solution(mesh):
    fine = Mesh(mesh.devices.reshape(4, 2, 2, 2, 4), ("y", "xh", "c", "xl", "z"))
    dp, seq = ("y", "xh", "c"), ("xl", "z")
    every = dp + seq
    return jax.shard_map(
        on_device,
        mesh=fine,
        in_specs=(
            P(dp, seq, None),
            P(dp, seq, None),
            P(dp, None),
            P(dp, seq),
            P(dp, seq, None),
            P(dp, seq, None),
            P(None, every),
            P(None, every),
            P(None, every),
            P(every, None),
            P(every),
            P(None, every),
            P(every),
        ),
        out_specs=(
            P(dp, seq, None),
            P(dp, seq, None),
            P(dp, seq, None),
            P(dp, seq, None),
            P(None, every),
            P(None, every),
            P(None, every),
            P(every, None),
            P(every),
            P(None, every),
            P(every),
        ),
        check_vma=False,
    )
```

```python
import jax
import jax.numpy as jnp
from jax import lax
from jax.experimental import pallas as pl
from jax.experimental.pallas import tpu as pltpu
from jax.sharding import Mesh, PartitionSpec as P

STEP = 64
SEQ = ("xl", "z")
CHIPS = ("y", "xh", "xl", "z")
BF16 = jnp.bfloat16
F32 = jnp.float32
LANES = 128
TAPS = 32
HALF_TAPS = 16
CM = 80
SHARE = 20
LINES = 128
BIG = 96
VMEM_BYTES = 50 * 1024 * 1024
SIDE_VMEM_BYTES = 60 * 1024 * 1024
END_VMEM_BYTES = 50 * 1024 * 1024
TAIL_VMEM_BYTES = 58 * 1024 * 1024


def dot(a, b):
    return jnp.dot(a, b, preferred_element_type=F32)


def dot_nt(a, b):
    return lax.dot_general(a, b, (((1,), (1,)), ((), ())), preferred_element_type=F32)


def dot_tn(a, b):
    return lax.dot_general(a, b, (((0,), (0,)), ((), ())), preferred_element_type=F32)


def lane_mask(rows):
    return lax.broadcasted_iota(jnp.int32, (rows, LANES), 1) < CM


SPLIT = LANES - CM
PIECE = CM - SPLIT


def fold(head, u1, u2):
    u2 = jnp.concatenate([u2, jnp.zeros((4, LANES), F32)], 0)
    lane = lax.broadcasted_iota(jnp.int32, (24, LANES), 1)
    top = jnp.where(lane[:8] < LANES - PIECE, head, pltpu.roll(u2[:8], LANES - PIECE - SPLIT, 1))
    middle = jnp.where(lane[:SHARE] < CM, u1, pltpu.roll(u2, CM, 1)[:SHARE])
    last = jnp.zeros((3, LANES), F32)
    for g in range(4):
        moved = pltpu.roll(u2, (PIECE * g - SPLIT) % LANES, 1)[8 + 3 * g : 11 + 3 * g]
        last = jnp.where(lane[:3] // PIECE == g, moved, last)
    return jnp.concatenate([top, middle, last, jnp.zeros((1, LANES), F32)], 0)


def unfold(rows):
    lane = lax.broadcasted_iota(jnp.int32, (SHARE, LANES), 1)
    low = pltpu.roll(rows[8:], LANES - CM, 1)[:SHARE]
    high = [pltpu.roll(rows[:8], (SPLIT - LANES + PIECE) % LANES, 1)]
    for g in range(4):
        high.append(pltpu.roll(rows[24:], (SPLIT - PIECE * g) % LANES, 1)[4:7])
    u2 = jnp.where(lane < SPLIT, low, jnp.concatenate(high, 0))
    return rows[:8], rows[8 : 8 + SHARE], u2


def spread_kernel(wd, wot, wct, u1t, u2t, gb, ob, out, lines, narrow):
    for j in range(8):
        lines[8 * j : 8 * j + 8, :] = wd[:, LANES * j : LANES * (j + 1)].astype(F32)
    for j in range(4):
        lines[64 + 8 * j : 72 + 8 * j, :] = wot[:, LANES * j : LANES * (j + 1)].astype(F32)
    lane = lax.broadcasted_iota(jnp.int32, (8, LANES), 1)
    diagonal = lax.broadcasted_iota(jnp.int32, (8, 8), 0) == lax.broadcasted_iota(jnp.int32, (8, 8), 1)

    def column(row):
        full = jnp.broadcast_to(row[...].astype(F32), (8, 8))
        return jnp.sum(jnp.where(diagonal, full, 0.0), 1, keepdims=True)

    narrow[...] = jnp.zeros_like(narrow)
    narrow[:8, :CM] = wct[...].astype(F32)
    narrow[8 : 8 + SHARE, :CM] = u1t[...].astype(F32)
    narrow[32 : 32 + SHARE, :CM] = u2t[...].astype(F32)
    biases = jnp.where(lane == CM, column(gb), jnp.where(lane == CM + 1, column(ob), 0.0))
    lines[BIG:, :] = fold(narrow[:8, :] + biases, narrow[8 : 8 + SHARE, :], narrow[32 : 32 + SHARE, :])
    block = lines[...].astype(BF16)
    for k in range(out.shape[0]):
        out[k] = block


def spread(wd, wot, wct, u1t, u2t, gb, ob):
    return pl.pallas_call(
        spread_kernel,
        out_shape=jax.ShapeDtypeStruct((64, LINES, LANES), BF16),
        scratch_shapes=[pltpu.VMEM((LINES, LANES), F32), pltpu.VMEM((56, LANES), F32)],
    )(wd, wot, wct, u1t, u2t, gb, ob)


def masked_past(before, audio, column):
    tile, half = audio.shape
    moved = jnp.concatenate([before, audio[: tile - STEP, :]], 0)
    return moved * jnp.concatenate([column] * (half // LANES), 1)


def roomy(shape, dtype):
    rows = 16 * 1024 * 1024 // (shape[1] * jnp.dtype(dtype).itemsize)
    return jax.ShapeDtypeStruct((rows, shape[1]), dtype)


def keep_columns(starts, seq_at, resets):
    tile = resets.shape[1]
    span = seq_at[0] * pl.num_programs(0) + pl.program_id(0)
    position = span * tile + lax.broadcasted_iota(jnp.int32, (1, tile), 1)
    blocked = position < STEP
    for k in range(starts.shape[1]):
        first = starts[0, k]
        blocked = blocked | ((first > position - STEP) & (first <= position))
    keep = jnp.where(blocked, 0, resets[...]).astype(F32)
    return jnp.broadcast_to(keep, (LANES, tile)).T.astype(BF16)


def turn_kernel(starts, seq_at, resets, audio_before, audio, g_res, g_skip, mask, xt, gt, g_sum):
    step = pl.program_id(0)
    tile, half = audio.shape
    column = keep_columns(starts, seq_at, resets)
    mask[...] = column
    before = jnp.where(step == 0, jnp.zeros_like(audio_before[...]), audio_before[...])
    xt[:half, :] = masked_past(before, audio[...], column).T
    xt[half:, :] = audio[...].T
    gt[:half, :] = g_res[...].T
    gt[half:, :] = g_skip[...].T

    @pl.when(step == 0)
    def _():
        g_sum[...] = jnp.zeros_like(g_sum)

    g_sum[:, :half] += jnp.sum(g_res[...].astype(F32).reshape(tile // 8, 8, half), 0)
    g_sum[:, half:] += jnp.sum(g_skip[...].astype(F32).reshape(tile // 8, 8, half), 0)


def turn(starts, seq_at, resets, audio, g_res, g_skip, tile):
    samples, width = audio.shape
    steps = tile // STEP
    rows = pl.BlockSpec((tile, width), lambda i: (i, 0))
    cols = pl.BlockSpec((2 * width, tile), lambda i: (0, i))
    scalars = pl.BlockSpec(memory_space=pltpu.SMEM)
    shape = jax.ShapeDtypeStruct((2 * width, samples), BF16)
    return pl.pallas_call(
        turn_kernel,
        grid=(samples // tile,),
        in_specs=[
            scalars,
            scalars,
            pl.BlockSpec((1, tile), lambda i: (0, i)),
            pl.BlockSpec((STEP, width), lambda i: (jnp.maximum(i * steps - 1, 0), 0)),
            rows,
            rows,
            rows,
        ],
        out_specs=[
            pl.BlockSpec((tile, LANES), lambda i: (i, 0)),
            cols,
            cols,
            pl.BlockSpec((8, 2 * width), lambda i: (0, 0)),
        ],
        out_shape=[
            jax.ShapeDtypeStruct((samples, LANES), BF16),
            shape,
            shape,
            roomy((8, 2 * width), F32),
        ],
        compiler_params=pltpu.CompilerParams(vmem_limit_bytes=SIDE_VMEM_BYTES),
        cost_estimate=pl.CostEstimate(flops=0, bytes_accessed=18 * samples * width, transcendentals=0),
    )(starts, seq_at, resets, audio, audio, g_res, g_skip)


def unpack_wide(ref, a, side, wd, wot):
    for b in range(0, 8, 2):
        rows = pl.ds(pl.multiple_of(a * 128 + side * 64 + b * 8, 16), 16)
        pair = [a * 8 + b, a * 8 + b + 1]
        for out, first, count in ((wd, 0, 4), (wot, 64, 2)):
            for m in range(count):
                two = [ref[k, pl.ds(first + 16 * m, 16), :].astype(F32) for k in pair]
                out[rows, pl.ds(256 * m, 128)] = jnp.concatenate([t[:8] for t in two], 0).astype(BF16)
                out[rows, pl.ds(256 * m + 128, 128)] = jnp.concatenate([t[8:] for t in two], 0).astype(BF16)


def unpack_head(ref, a, side, wct):
    for b in range(0, 8, 2):
        rows = pl.ds(pl.multiple_of(a * 128 + side * 64 + b * 8, 16), 16)
        two = [ref[a * 8 + b + k, pl.ds(BIG, 16), :].astype(F32) for k in range(2)]
        wct[rows, :] = jnp.concatenate([t[:8] for t in two], 0).astype(BF16)


def main_kernel(
    core, starts, seq_at, resets, mel_a, mel_b, tails, audio_before, audio, g_res, g_skip, xt, gt, g_sum, own, other,
    dp_out, gated_out, stay, send, mel_here, halo,
    wd, wot, wct, u1t, u2t, wc, inter, cond_all, dcond_all, dinter, xg, owg, du, mine, theirs, mel_rows, in_sems, out_sems, mel_sem,
):
    step = pl.program_id(0)
    tile = audio.shape[0]
    half = audio.shape[1]
    frames = cond_all.shape[0] // HALF_TAPS
    first_rows = mel_a.shape[0]
    give_mel = pltpu.make_async_copy(mel_rows, mel_here.at[pl.ds(0, mel_rows.shape[0])], mel_sem)

    @pl.when(step == 0)
    def _():
        fetched = ((own, mine), (other, theirs))
        fetch = [pltpu.make_async_copy(a, b, in_sems.at[k]) for k, (a, b) in enumerate(fetched)]
        for copy in fetch:
            copy.start()
        xg[...] = jnp.zeros_like(xg)
        owg[...] = jnp.zeros_like(owg)
        u1t[HALF_TAPS * CM :, :] = jnp.zeros_like(u1t[HALF_TAPS * CM :, :])
        u2t[HALF_TAPS * CM :, :] = jnp.zeros_like(u2t[HALF_TAPS * CM :, :])
        for copy in fetch:
            copy.wait()

        def unpack(a, _):
            for ref, side in ((mine, core[0]), (theirs, 1 - core[0])):
                unpack_wide(ref, a, side, wd, wot)
                unpack_head(ref, a, side, wct)
                for b in range(0, 8, 4):
                    tap_row = pl.multiple_of((a % 4 * 16 + side * 8 + b) * SHARE, 16)
                    lanes = pl.ds(pl.multiple_of(a // 4 * LANES, LANES), LANES)
                    four = [unfold(ref[a * 8 + b + k, pl.ds(BIG, 32), :].astype(F32)) for k in range(4)]
                    for k, out in ((1, u1t), (2, u2t)):
                        out[pl.ds(tap_row, CM), lanes] = jnp.concatenate([t[k] for t in four], 0).astype(BF16)
            return _

        lax.fori_loop(0, 8, unpack, 0)
        wc[...] = wct[...].T
        keep = lane_mask(first_rows)
        mels = jnp.concatenate([mel_a[...], mel_b[...]], 1)
        for r in range(HALF_TAPS):
            both = dot_nt(mels, u1t[pl.ds(CM * r, LANES), :])
            rounded = jnp.where(keep, both, 0.0).astype(BF16).astype(F32)
            inter[pl.ds(r, first_rows, stride=HALF_TAPS), :] = rounded
        rows_a = inter[pl.ds(HALF_TAPS, frames), :].astype(BF16)
        rows_b = inter[pl.ds(HALF_TAPS - 1, frames), :].astype(BF16)
        lane = lax.broadcasted_iota(jnp.int32, (frames, LANES), 1)
        one = jnp.where(lane == CM, 1.0, 0.0)
        rows_ab = jnp.concatenate([rows_a, rows_b], 1)
        for r in range(HALF_TAPS):
            both = dot_nt(rows_ab, u2t[pl.ds(CM * r, LANES), :])
            cond_all[pl.ds(r, frames, stride=HALF_TAPS), :] = jnp.where(lane < CM, both, one)

    at = pl.multiple_of(step * tile, tile)
    cond = cond_all[pl.ds(at, tile), :].astype(BF16)
    before = jnp.where(step == 0, tails[...], audio_before[...])
    column = keep_columns(starts, seq_at, resets)
    past = masked_past(before, audio[...], column)
    pre = dot(past, wd[:half, :]) + dot(audio[...], wd[half:, :]) + dot(cond, wc[...])
    th = jnp.tanh(pre[:, :half])
    sg = 0.5 * jnp.tanh(0.5 * pre[:, half:]) + 0.5
    gated = (th * sg).astype(BF16)
    gated_out[...] = gated
    dg = dot(g_res[...], wot[:half, :]) + dot(g_skip[...], wot[half:, :])
    dgs = dg * sg
    dp = jnp.concatenate([dgs * (1.0 - th * th), dgs * th * (1.0 - sg)], 1).astype(BF16)
    dp_out[...] = dp
    dcond_all[pl.ds(at, tile), :] = dot(dp, wct[...])
    owg[...] += dot(gt[...], gated)
    xg[...] += dot(jnp.concatenate([xt[...], cond.T], 0), dp)

    @pl.when(step == 0)
    def _():
        xg[:half, :] += dot_tn(past[:STEP, :], dp[:STEP, :])
        halo[:STEP, :] = dp[:STEP, :] * jnp.concatenate([column[:STEP, :]] * (2 * half // LANES), 1)

    @pl.when(step == pl.num_programs(0) - 1)
    def _():
        def give(a, k, first, count):
            part, lines = pl.ds(pl.multiple_of(a * 8, 8), 8), pl.ds(first, count)
            src, dst = ((mine, stay), (theirs, send))[k]
            return pltpu.make_async_copy(src.at[part, lines], dst.at[part, lines], out_sems.at[first // BIG, k, a])

        def pack_big(a, _):
            for k, (out, side) in enumerate(((mine, core[0]), (theirs, 1 - core[0]))):
                for b in range(8):
                    rows = pl.ds(pl.multiple_of(a * 128 + side * 64 + b * 8, 8), 8)
                    place = a * 8 + b
                    for m in range(4):
                        two = [xg[rows, pl.ds(256 * m, 128)], xg[rows, pl.ds(256 * m + 128, 128)]]
                        out[place, pl.ds(16 * m, 16), :] = jnp.concatenate(two, 0).astype(BF16)
                    for m in range(2):
                        two = [owg[rows, pl.ds(256 * m, 128)], owg[rows, pl.ds(256 * m + 128, 128)]]
                        out[place, pl.ds(64 + 16 * m, 16), :] = jnp.concatenate(two, 0).astype(BF16)
                give(a, k, 0, BIG).start()
            return _

        lax.fori_loop(0, 8, pack_big, 0)
        rows_a = inter[pl.ds(HALF_TAPS, frames), :].astype(BF16)
        rows_b = inter[pl.ds(HALF_TAPS - 1, frames), :].astype(BF16)
        both = jnp.concatenate([rows_a, rows_b], 1)
        keep = lane_mask(frames)
        sums = jnp.zeros((frames, 2 * LANES), F32)

        def put(grads, tap, first):
            for q in range(CM // SHARE):
                du[pl.ds((CM // SHARE * tap + q) * 2 * SHARE + first, SHARE), :] = grads[SHARE * q : SHARE * (q + 1)]

        for r in range(HALF_TAPS):
            e = jnp.where(keep, dcond_all[pl.ds(r, frames, stride=HALF_TAPS), :], 0.0).astype(BF16)
            grads = dot_tn(e, both)
            put(grads[:, :LANES], r, SHARE)
            put(grads[:, LANES:], r + HALF_TAPS, SHARE)
            sums += dot(e, u2t[pl.ds(CM * r, LANES), :])
        dinter[...] = jnp.zeros_like(dinter)
        dinter[pl.ds(HALF_TAPS, frames), :] = sums[:, :LANES]
        dinter[pl.ds(HALF_TAPS - 1, frames), :] += sums[:, LANES:]
        mels = jnp.concatenate([mel_a[...], mel_b[...]], 1)
        keep = lane_mask(first_rows)
        mel_sums = jnp.zeros((first_rows, 2 * LANES), F32)
        for r in range(HALF_TAPS):
            f = jnp.where(keep, dinter[pl.ds(r, first_rows, stride=HALF_TAPS), :], 0.0).astype(BF16)
            grads = dot_tn(f, mels)
            put(grads[:, :LANES], r, 0)
            put(grads[:, LANES:], r + HALF_TAPS, 0)
            mel_sums += dot(f, u1t[pl.ds(CM * r, LANES), :])
        zero = jnp.zeros((1, LANES), F32)
        mel_sum = jnp.concatenate([zero, mel_sums[:, :LANES]], 0) + jnp.concatenate([mel_sums[:, LANES:], zero], 0)
        real = mel_rows.shape[0]
        mel_rows[...] = mel_sum[2 : 2 + real]
        give_mel.start()
        halo[STEP:, :] = jnp.zeros_like(halo[STEP:, :])
        halo[STEP:, :LANES] = jnp.concatenate([mel_sum[:2], jnp.zeros((14, LANES), F32)], 0).astype(BF16)
        xg[2 * half + CM + 1 : 2 * half + CM + 2, :] = jnp.sum(g_sum[...], 0, keepdims=True)
        cwgt = xg[2 * half :, :].T
        dcond_all[: cwgt.shape[0], :] = cwgt

        def pack_small(a, _):
            for k, (out, side) in enumerate(((mine, core[0]), (theirs, 1 - core[0]))):
                for b in range(8):
                    at_row = pl.multiple_of(a * 128 + side * 64 + b * 8, 8)
                    narrow = du[pl.ds(pl.multiple_of(at_row * 5, 8), 2 * SHARE), :]
                    folded = fold(dcond_all[pl.ds(at_row, 8), :], narrow[:SHARE], narrow[SHARE:])
                    out[a * 8 + b, pl.ds(BIG, LINES - BIG), :] = folded.astype(BF16)
                give(a, k, BIG, LINES - BIG).start()
            return _

        lax.fori_loop(0, 8, pack_small, 0)

        def finish(a, _):
            for k in range(2):
                give(a, k, 0, BIG).wait()
                give(a, k, BIG, LINES - BIG).wait()
            return _

        lax.fori_loop(0, 8, finish, 0)
        give_mel.wait()


def main_pass(core, starts, seq_at, resets, mel_a, mel_b, tails, audio, g_res, g_skip, xt, gt, g_sum, own, other, tile):
    samples, width = audio.shape
    first_rows = mel_a.shape[0]
    rows = pl.BlockSpec((tile, width), lambda i: (i, 0))
    cols = pl.BlockSpec((2 * width, tile), lambda i: (0, i))

    def whole(shape):
        return pl.BlockSpec(shape, lambda i: (0,) * len(shape))

    anywhere = pl.BlockSpec(memory_space=pl.ANY)
    hbm = pl.BlockSpec(memory_space=pltpu.HBM)
    packed = (64, LINES, LANES)
    outs = [
        ((samples, 2 * width), BF16),
        ((samples, width), BF16),
        (packed, BF16),
        (packed, BF16),
        ((samples // (HALF_TAPS * HALF_TAPS), LANES), F32),
        ((STEP + 16, 2 * width), BF16),
    ]
    return pl.pallas_call(
        main_kernel,
        grid=(samples // tile,),
        in_specs=[pl.BlockSpec(memory_space=pltpu.SMEM)] * 3
        + [pl.BlockSpec((1, tile), lambda i: (0, i))]
        + [whole(mel_a.shape), whole(mel_b.shape), whole((STEP, width))]
        + [pl.BlockSpec((STEP, width), lambda i: (jnp.maximum(i * (tile // STEP) - 1, 0), 0))]
        + [rows, rows, rows, cols, cols, whole((8, 2 * width)), anywhere, anywhere],
        out_specs=[
            pl.BlockSpec((tile, 2 * width), lambda i: (i, 0)),
            pl.BlockSpec((tile, width), lambda i: (i, 0)),
        ]
        + [hbm] * 3
        + [whole(s) for s, _ in outs[5:]],
        out_shape=[roomy(s, d) if s == outs[4][0] else jax.ShapeDtypeStruct(s, d) for s, d in outs],
        scratch_shapes=[
            pltpu.VMEM((2 * width, 2 * width), BF16),
            pltpu.VMEM((2 * width, width), BF16),
            pltpu.VMEM((2 * width, LANES), BF16),
            pltpu.VMEM((HALF_TAPS * CM + 48, 2 * LANES), BF16),
            pltpu.VMEM((HALF_TAPS * CM + 48, 2 * LANES), BF16),
            pltpu.VMEM((LANES, 2 * width), BF16),
            pltpu.VMEM((first_rows * HALF_TAPS, LANES), F32),
            pltpu.VMEM((samples, LANES), F32),
            pltpu.VMEM((samples, LANES), F32),
            pltpu.VMEM((first_rows * HALF_TAPS, LANES), F32),
            pltpu.VMEM((2 * width + LANES, 2 * width), F32),
            pltpu.VMEM((2 * width, width), F32),
            pltpu.VMEM((2 * TAPS * CM, LANES), F32),
            pltpu.VMEM(packed, BF16),
            pltpu.VMEM(packed, BF16),
            pltpu.VMEM(outs[4][0], F32),
            pltpu.SemaphoreType.DMA((2,)),
            pltpu.SemaphoreType.DMA((2, 2, 8)),
            pltpu.SemaphoreType.DMA,
        ],
        compiler_params=pltpu.CompilerParams(vmem_limit_bytes=VMEM_BYTES),
        cost_estimate=pl.CostEstimate(
            flops=28_000_000_000, bytes_accessed=48 * samples * width, transcendentals=0
        ),
    )(core, starts, seq_at, resets, mel_a, mel_b, tails, audio, audio, g_res, g_skip, xt, gt, g_sum, own, other)


def tail_kernel(
    core, dp, dp_next, gated, audio, g_res, mask, mask_next, own, other, pair,
    res_out, skip_out, res_grad, rest, wd_past,
    wd, wot, wct, ob, wdt, wo, mine, theirs, in_sems,
):
    step = pl.program_id(0)
    tile, half = audio.shape

    @pl.when(step == 0)
    def _():
        fetch = [pltpu.make_async_copy(a, b, in_sems.at[k]) for k, (a, b) in enumerate(((own, mine), (other, theirs)))]
        for copy in fetch:
            copy.start()
        for copy in fetch:
            copy.wait()

        def unpack(a, _):
            for ref, side in ((mine, core[0]), (theirs, 1 - core[0])):
                unpack_wide(ref, a, side, wd, wot)
                unpack_head(ref, a, side, wct)
            return _

        lax.fori_loop(0, 8, unpack, 0)
        ob[...] = wct[...].T[CM + 1 : CM + 2, :].astype(F32)
        wdt[...] = wd[...].T
        wo[...] = wot[...].T
        wd_past[...] = wdt[:, :half]

    out = dot(gated[...], wo[...]) + ob[...]
    res_out[...] = (audio[...].astype(F32) + out[:, :half]).astype(BF16)
    skip_out[...] = out[:, half:].astype(BF16)
    last = step == pl.num_programs(0) - 1
    after = jnp.where(last, jnp.zeros_like(dp_next[...]), dp_next[...])
    ahead = jnp.concatenate([dp[STEP:, :], after], 0)
    d_past = dot(ahead, wdt[:, :half]).astype(BF16)
    kept = jnp.concatenate([mask[STEP:, :], mask_next[...]], 0)
    d_past = (d_past * jnp.concatenate([kept] * (half // LANES), 1)).astype(F32)
    here = g_res[...].astype(F32) + dot(dp[...], wdt[:, half:])
    rest[...] = here[tile - STEP :, :]
    res_grad[...] = (here + d_past).astype(BF16)


def tail_pass(core, dp, gated, audio, g_res, mask, own, other, pair, tile):
    samples, width = audio.shape
    rows = pl.BlockSpec((tile, width), lambda i: (i, 0))
    anywhere = pl.BlockSpec(memory_space=pl.ANY)
    step_blocks = tile // STEP
    final = samples // STEP - 1

    def whole(shape):
        return pl.BlockSpec(shape, lambda i: (0,) * len(shape))

    shape = jax.ShapeDtypeStruct((samples, width), BF16)
    return pl.pallas_call(
        tail_kernel,
        grid=(samples // tile,),
        in_specs=[
            pl.BlockSpec(memory_space=pltpu.SMEM),
            pl.BlockSpec((tile, 2 * width), lambda i: (i, 0)),
            pl.BlockSpec((STEP, 2 * width), lambda i: (jnp.minimum((i + 1) * step_blocks, final), 0)),
            rows,
            rows,
            rows,
            pl.BlockSpec((tile, LANES), lambda i: (i, 0)),
            pl.BlockSpec((STEP, LANES), lambda i: (jnp.minimum((i + 1) * step_blocks, final), 0)),
            anywhere,
            anywhere,
            anywhere,
        ],
        out_specs=[rows] * 3 + [whole((STEP, width)), whole((2 * width, width))],
        out_shape=[shape] * 3
        + [roomy((STEP, width), F32), roomy((2 * width, width), BF16)],
        scratch_shapes=[
            pltpu.VMEM((2 * width, 2 * width), BF16),
            pltpu.VMEM((2 * width, width), BF16),
            pltpu.VMEM((2 * width, LANES), BF16),
            pltpu.VMEM((1, 2 * width), F32),
            pltpu.VMEM((2 * width, 2 * width), BF16),
            pltpu.VMEM((width, 2 * width), BF16),
            pltpu.VMEM(own.shape, BF16),
            pltpu.VMEM(own.shape, BF16),
            pltpu.SemaphoreType.DMA((2,)),
        ],
        compiler_params=pltpu.CompilerParams(vmem_limit_bytes=TAIL_VMEM_BYTES),
        cost_estimate=pl.CostEstimate(
            flops=13_000_000_000, bytes_accessed=20 * samples * width, transcendentals=0
        ),
    )(core, dp, dp, gated, audio, g_res, mask, mask, own, other, pair)


def end_kernel(
    grad, rest, halo, wd_past, mel_here, parts,
    out, mel_out, wd, wot, wct, u1t, u2t, gb, ob,
    total,
):
    step = pl.program_id(0)

    @pl.when(step == 0)
    def _():
        total[...] = jnp.zeros_like(total)
        out[...] = (rest[...] + dot(halo[:STEP, :], wd_past[...]).astype(BF16).astype(F32)).astype(BF16)
        frames = mel_here.shape[0]
        back = halo[STEP:, :LANES].astype(F32)[:2]
        mel = mel_here[...] + jnp.concatenate([jnp.zeros((frames - 2, LANES), F32), back], 0)
        mel_out[...] = mel[:, :CM].astype(BF16)

    total[...] += jnp.sum(parts[...].astype(F32), 0)

    @pl.when(step == pl.num_programs(0) - 1)
    def _():
        for j in range(8):
            wd[:, LANES * j : LANES * (j + 1)] = total[8 * j : 8 * j + 8, :]
        for j in range(4):
            wot[:, LANES * j : LANES * (j + 1)] = total[64 + 8 * j : 72 + 8 * j, :]
        head, u1, u2 = unfold(total[BIG:, :])
        wct[...] = head[:, :CM]
        u1t[...] = u1[:, :CM]
        u2t[...] = u2[:, :CM]
        diagonal = lax.broadcasted_iota(jnp.int32, (8, 8), 0) == lax.broadcasted_iota(jnp.int32, (8, 8), 1)
        for lane, row in ((CM, gb), (CM + 1, ob)):
            column = jnp.broadcast_to(head[:, lane : lane + 1], (8, 8))
            row[...] = jnp.sum(jnp.where(diagonal, column, 0.0), 0, keepdims=True)


def end_pass(grad, rest, halo, wd_past, mel_here, parts, frames):
    samples, width = grad.shape
    steps = 4
    shapes = [(8, 1024), (8, 512), (8, CM), (SHARE, CM), (SHARE, CM), (1, 8), (1, 8)]

    def whole(shape):
        return pl.BlockSpec(shape, lambda i: (0,) * len(shape))

    return pl.pallas_call(
        end_kernel,
        grid=(steps,),
        in_specs=[pl.BlockSpec(memory_space=pl.ANY)]
        + [whole(s) for s in ((STEP, width), halo.shape, (2 * width, width), (frames, LANES))]
        + [pl.BlockSpec((64 // steps, LINES, LANES), lambda i: (i, 0, 0))],
        out_specs=[pl.BlockSpec((STEP, width), lambda i: (samples // STEP - 1, 0))]
        + [whole(s) for s in [(frames, CM)] + shapes],
        out_shape=[jax.ShapeDtypeStruct(grad.shape, BF16), jax.ShapeDtypeStruct((frames, CM), BF16)]
        + [jax.ShapeDtypeStruct(s, F32) for s in shapes],
        scratch_shapes=[pltpu.VMEM((LINES, LANES), F32)],
        input_output_aliases={0: 0},
        compiler_params=pltpu.CompilerParams(vmem_limit_bytes=END_VMEM_BYTES),
    )(grad, rest, halo, wd_past, mel_here, parts)


def shifted(value, steps, count=8):
    first, last = max(0, -steps), min(count, count - steps)
    return lax.ppermute(value, SEQ, [(s, s + steps) for s in range(first, last)])


def no_change(value):
    return jnp.minimum(jnp.abs(value), 0)


def swap(value):
    return lax.ppermute(value, "c", [(0, 1), (1, 0)])


def on_device(
    residual_input, mel_input_frames, starts, resets, residual_gradient, skip_gradient,
    first_upsample_weight, second_upsample_weight, conditioning_weight, dilated_weight,
    gate_bias_vector, output_weight, output_bias_vector,
):
    core = lax.axis_index("c")
    audio, mel = residual_input[0], mel_input_frames[0]
    g_res, g_skip = residual_gradient[0], skip_gradient[0]
    samples, width = audio.shape
    frames = mel.shape[0]

    tails = jnp.concatenate([audio[-STEP:], jnp.pad(mel[-2:], ((0, 14), (0, width - CM)))], 0)
    tails = shifted(tails, 1)

    shares = spread(
        dilated_weight,
        output_weight.T,
        conditioning_weight.T,
        first_upsample_weight.T,
        second_upsample_weight.T,
        gate_bias_vector[None],
        output_bias_vector[None],
    )
    own = lax.all_to_all(shares, CHIPS, 0, 0)

    mel_tail = tails[STEP : STEP + 2, :CM]
    mel_ext = jnp.concatenate([mel_tail, mel, jnp.zeros((14, CM), BF16)], 0)
    mel_ext = jnp.pad(mel_ext, ((0, 0), (0, LANES - CM)))
    mel_b, mel_a = mel_ext[: 2 * frames - 8], mel_ext[1 : 2 * frames - 7]
    seq_at = lax.axis_index(SEQ).astype(jnp.int32)[None]
    mask, xt, gt, g_sum = turn(starts, seq_at, resets, audio, g_res, g_skip, 512)

    zero = no_change(jnp.abs(gt[0, 0]) + jnp.abs(mel_a[0, 0]))
    own = lax.dynamic_update_slice(own, own[:1, :16] + zero, (0, 0, 0))
    other = swap(own)

    core = core.astype(jnp.int32)[None]
    dp, gated, stay, send, mel_here, halo = main_pass(
        core, starts, seq_at, resets, mel_a, mel_b, tails, audio, g_res, g_skip, xt, gt, g_sum, own, other, 512
    )

    came = swap(send)
    pair = stay + came
    all_parts = lax.all_to_all(pair, CHIPS, 0, 0)

    halo_next = shifted(halo, -1)
    res_out, skip_out, res_grad, rest, wd_past = tail_pass(
        core, dp, gated, audio, g_res, mask, own, other, pair, 512
    )
    res_grad, mel_grad, d_wd, d_wot, d_wct, d_u1t, d_u2t, d_gb, d_ob = end_pass(
        res_grad, rest, halo_next, wd_past, mel_here, all_parts, frames
    )
    return (
        res_out[None],
        skip_out[None],
        res_grad[None],
        mel_grad[None],
        d_u1t.T,
        d_u2t.T,
        d_wct.T,
        d_wd,
        d_gb[0],
        d_wot.T,
        d_ob[0],
    )


def solution(mesh):
    fine = Mesh(mesh.devices.reshape(4, 2, 2, 2, 4), ("y", "xh", "c", "xl", "z"))
    dp, seq = ("y", "xh", "c"), ("xl", "z")
    every = dp + seq
    return jax.shard_map(
        on_device,
        mesh=fine,
        in_specs=(
            P(dp, seq, None),
            P(dp, seq, None),
            P(dp, None),
            P(dp, seq),
            P(dp, seq, None),
            P(dp, seq, None),
            P(None, every),
            P(None, every),
            P(None, every),
            P(every, None),
            P(every),
            P(None, every),
            P(every),
        ),
        out_specs=(
            P(dp, seq, None),
            P(dp, seq, None),
            P(dp, seq, None),
            P(dp, seq, None),
            P(None, every),
            P(None, every),
            P(None, every),
            P(every, None),
            P(every),
            P(None, every),
            P(every),
        ),
        check_vma=False,
    )
```

```python
import jax
import jax.numpy as jnp
from jax import lax
from jax.experimental import pallas as pl
from jax.experimental.pallas import tpu as pltpu
from jax.sharding import Mesh, PartitionSpec as P

STEP = 64
SEQ = ("xl", "z")
CHIPS = ("y", "xh", "xl", "z")
BF16 = jnp.bfloat16
F32 = jnp.float32
LANES = 128
TAPS = 32
HALF_TAPS = 16
CM = 80
SHARE = 20
LINES = 128
BIG = 96
VMEM_BYTES = 46 * 1024 * 1024
SIDE_VMEM_BYTES = 60 * 1024 * 1024
END_VMEM_BYTES = 50 * 1024 * 1024
TAIL_VMEM_BYTES = 58 * 1024 * 1024


def dot(a, b):
    return jnp.dot(a, b, preferred_element_type=F32)


def dot_nt(a, b):
    return lax.dot_general(a, b, (((1,), (1,)), ((), ())), preferred_element_type=F32)


def dot_tn(a, b):
    return lax.dot_general(a, b, (((0,), (0,)), ((), ())), preferred_element_type=F32)


def lane_mask(rows):
    return lax.broadcasted_iota(jnp.int32, (rows, LANES), 1) < CM


SPLIT = LANES - CM
PIECE = CM - SPLIT


def fold(head, u1, u2):
    u2 = jnp.concatenate([u2, jnp.zeros((4, LANES), F32)], 0)
    lane = lax.broadcasted_iota(jnp.int32, (24, LANES), 1)
    top = jnp.where(lane[:8] < LANES - PIECE, head, pltpu.roll(u2[:8], LANES - PIECE - SPLIT, 1))
    middle = jnp.where(lane[:SHARE] < CM, u1, pltpu.roll(u2, CM, 1)[:SHARE])
    last = jnp.zeros((3, LANES), F32)
    for g in range(4):
        moved = pltpu.roll(u2, (PIECE * g - SPLIT) % LANES, 1)[8 + 3 * g : 11 + 3 * g]
        last = jnp.where(lane[:3] // PIECE == g, moved, last)
    return jnp.concatenate([top, middle, last, jnp.zeros((1, LANES), F32)], 0)


def unfold(rows):
    lane = lax.broadcasted_iota(jnp.int32, (SHARE, LANES), 1)
    low = pltpu.roll(rows[8:], LANES - CM, 1)[:SHARE]
    high = [pltpu.roll(rows[:8], (SPLIT - LANES + PIECE) % LANES, 1)]
    for g in range(4):
        high.append(pltpu.roll(rows[24:], (SPLIT - PIECE * g) % LANES, 1)[4:7])
    u2 = jnp.where(lane < SPLIT, low, jnp.concatenate(high, 0))
    return rows[:8], rows[8 : 8 + SHARE], u2


def spread_kernel(wd, wot, wct, u1t, u2t, gb, ob, out, lines, narrow):
    for j in range(8):
        lines[8 * j : 8 * j + 8, :] = wd[:, LANES * j : LANES * (j + 1)].astype(F32)
    for j in range(4):
        lines[64 + 8 * j : 72 + 8 * j, :] = wot[:, LANES * j : LANES * (j + 1)].astype(F32)
    lane = lax.broadcasted_iota(jnp.int32, (8, LANES), 1)
    diagonal = lax.broadcasted_iota(jnp.int32, (8, 8), 0) == lax.broadcasted_iota(jnp.int32, (8, 8), 1)

    def column(row):
        full = jnp.broadcast_to(row[...].astype(F32), (8, 8))
        return jnp.sum(jnp.where(diagonal, full, 0.0), 1, keepdims=True)

    narrow[...] = jnp.zeros_like(narrow)
    narrow[:8, :CM] = wct[...].astype(F32)
    narrow[8 : 8 + SHARE, :CM] = u1t[...].astype(F32)
    narrow[32 : 32 + SHARE, :CM] = u2t[...].astype(F32)
    biases = jnp.where(lane == CM, column(gb), jnp.where(lane == CM + 1, column(ob), 0.0))
    lines[BIG:, :] = fold(narrow[:8, :] + biases, narrow[8 : 8 + SHARE, :], narrow[32 : 32 + SHARE, :])
    block = lines[...].astype(BF16)
    for k in range(out.shape[0]):
        out[k] = block


def spread(wd, wot, wct, u1t, u2t, gb, ob):
    return pl.pallas_call(
        spread_kernel,
        out_shape=jax.ShapeDtypeStruct((64, LINES, LANES), BF16),
        scratch_shapes=[pltpu.VMEM((LINES, LANES), F32), pltpu.VMEM((56, LANES), F32)],
    )(wd, wot, wct, u1t, u2t, gb, ob)


def masked_past(before, audio, column):
    tile, half = audio.shape
    moved = jnp.concatenate([before, audio[: tile - STEP, :]], 0)
    return moved * jnp.concatenate([column] * (half // LANES), 1)


def roomy(shape, dtype):
    rows = 16 * 1024 * 1024 // (shape[1] * jnp.dtype(dtype).itemsize)
    return jax.ShapeDtypeStruct((rows, shape[1]), dtype)


def keep_columns(starts, seq_at, resets):
    tile = resets.shape[1]
    span = seq_at[0] * pl.num_programs(0) + pl.program_id(0)
    position = span * tile + lax.broadcasted_iota(jnp.int32, (1, tile), 1)
    blocked = position < STEP
    for k in range(starts.shape[1]):
        first = starts[0, k]
        blocked = blocked | ((first > position - STEP) & (first <= position))
    keep = jnp.where(blocked, 0, resets[...]).astype(F32)
    return jnp.broadcast_to(keep, (LANES, tile)).T.astype(BF16)


def turn_kernel(starts, seq_at, resets, audio_before, audio, g_res, g_skip, mask, xt, gt, g_sum):
    step = pl.program_id(0)
    tile, half = audio.shape
    column = keep_columns(starts, seq_at, resets)
    mask[...] = column
    before = jnp.where(step == 0, jnp.zeros_like(audio_before[...]), audio_before[...])
    xt[:half, :] = masked_past(before, audio[...], column).T
    xt[half:, :] = audio[...].T
    gt[:half, :] = g_res[...].T
    gt[half:, :] = g_skip[...].T

    @pl.when(step == 0)
    def _():
        g_sum[...] = jnp.zeros_like(g_sum)

    g_sum[:, :half] += jnp.sum(g_res[...].astype(F32).reshape(tile // 8, 8, half), 0)
    g_sum[:, half:] += jnp.sum(g_skip[...].astype(F32).reshape(tile // 8, 8, half), 0)


def turn(starts, seq_at, resets, audio, g_res, g_skip, tile):
    samples, width = audio.shape
    steps = tile // STEP
    rows = pl.BlockSpec((tile, width), lambda i: (i, 0))
    cols = pl.BlockSpec((2 * width, tile), lambda i: (0, i))
    scalars = pl.BlockSpec(memory_space=pltpu.SMEM)
    shape = jax.ShapeDtypeStruct((2 * width, samples), BF16)
    return pl.pallas_call(
        turn_kernel,
        grid=(samples // tile,),
        in_specs=[
            scalars,
            scalars,
            pl.BlockSpec((1, tile), lambda i: (0, i)),
            pl.BlockSpec((STEP, width), lambda i: (jnp.maximum(i * steps - 1, 0), 0)),
            rows,
            rows,
            rows,
        ],
        out_specs=[
            pl.BlockSpec((tile, LANES), lambda i: (i, 0)),
            cols,
            cols,
            pl.BlockSpec((8, 2 * width), lambda i: (0, 0)),
        ],
        out_shape=[
            jax.ShapeDtypeStruct((samples, LANES), BF16),
            shape,
            shape,
            roomy((8, 2 * width), F32),
        ],
        compiler_params=pltpu.CompilerParams(vmem_limit_bytes=SIDE_VMEM_BYTES),
        cost_estimate=pl.CostEstimate(flops=0, bytes_accessed=18 * samples * width, transcendentals=0),
    )(starts, seq_at, resets, audio, audio, g_res, g_skip)


def unpack_wide(ref, a, side, wd, wot):
    for b in range(0, 8, 2):
        rows = pl.ds(pl.multiple_of(a * 128 + side * 64 + b * 8, 16), 16)
        pair = [a * 8 + b, a * 8 + b + 1]
        for out, first, count in ((wd, 0, 4), (wot, 64, 2)):
            for m in range(count):
                two = [ref[k, pl.ds(first + 16 * m, 16), :].astype(F32) for k in pair]
                out[rows, pl.ds(256 * m, 128)] = jnp.concatenate([t[:8] for t in two], 0).astype(BF16)
                out[rows, pl.ds(256 * m + 128, 128)] = jnp.concatenate([t[8:] for t in two], 0).astype(BF16)


def unpack_head(ref, a, side, wct):
    for b in range(0, 8, 2):
        rows = pl.ds(pl.multiple_of(a * 128 + side * 64 + b * 8, 16), 16)
        two = [ref[a * 8 + b + k, pl.ds(BIG, 16), :].astype(F32) for k in range(2)]
        wct[rows, :] = jnp.concatenate([t[:8] for t in two], 0).astype(BF16)


def main_kernel(
    core, starts, seq_at, resets, mel_a, mel_b, tails, audio_all, g_res_all, g_skip_all, xt_all, gt_all, g_sum, own, other,
    dp_out, gated_out, stay, send, mel_here, halo,
    wd, wot, wct, u1t, u2t, wc, inter, cond_all, dcond_all, dinter, xg, owg, du, mine, theirs, mel_rows,
    audio, g_res, g_skip, xt, gt, in_sems, out_sems, mel_sem, tile_sems,
):
    step = pl.program_id(0)
    steps = pl.num_programs(0)
    tile, half = g_res.shape[1:]
    frames = cond_all.shape[0] // HALF_TAPS
    first_rows = mel_a.shape[0]
    slot = lax.rem(step, 2)

    def tile_copies(i, to, lead):
        at = pl.multiple_of(i * tile, tile)
        rows, cols = pl.ds(at, tile), pl.ds(at, tile)
        audio_from = pl.ds(pl.multiple_of(i * tile - lead, STEP), tile + lead)
        pairs = (
            (audio_all.at[audio_from], audio.at[to, pl.ds(STEP - lead, tile + lead)]),
            (g_res_all.at[rows], g_res.at[to]),
            (g_skip_all.at[rows], g_skip.at[to]),
            (xt_all.at[:, cols], xt.at[to]),
            (gt_all.at[:, cols], gt.at[to]),
        )
        return [pltpu.make_async_copy(a, b, tile_sems.at[to, k]) for k, (a, b) in enumerate(pairs)]

    give_mel = pltpu.make_async_copy(mel_rows, mel_here.at[pl.ds(0, mel_rows.shape[0])], mel_sem)

    @pl.when(step == 0)
    def _():
        fetched = ((own, mine), (other, theirs))
        fetch = [pltpu.make_async_copy(a, b, in_sems.at[k]) for k, (a, b) in enumerate(fetched)]
        for copy in fetch + tile_copies(0, 0, 0):
            copy.start()
        audio[0, :STEP, :] = tails[...]
        xg[...] = jnp.zeros_like(xg)
        owg[...] = jnp.zeros_like(owg)
        u1t[HALF_TAPS * CM :, :] = jnp.zeros_like(u1t[HALF_TAPS * CM :, :])
        u2t[HALF_TAPS * CM :, :] = jnp.zeros_like(u2t[HALF_TAPS * CM :, :])
        for copy in fetch:
            copy.wait()

        def unpack(a, _):
            for ref, side in ((mine, core[0]), (theirs, 1 - core[0])):
                unpack_wide(ref, a, side, wd, wot)
                unpack_head(ref, a, side, wct)
                for b in range(0, 8, 4):
                    tap_row = pl.multiple_of((a % 4 * 16 + side * 8 + b) * SHARE, 16)
                    lanes = pl.ds(pl.multiple_of(a // 4 * LANES, LANES), LANES)
                    four = [unfold(ref[a * 8 + b + k, pl.ds(BIG, 32), :].astype(F32)) for k in range(4)]
                    for k, out in ((1, u1t), (2, u2t)):
                        out[pl.ds(tap_row, CM), lanes] = jnp.concatenate([t[k] for t in four], 0).astype(BF16)
            return _

        lax.fori_loop(0, 8, unpack, 0)
        wc[...] = wct[...].T
        keep = lane_mask(first_rows)
        mels = jnp.concatenate([mel_a[...], mel_b[...]], 1)
        for r in range(HALF_TAPS):
            both = dot_nt(mels, u1t[pl.ds(CM * r, LANES), :])
            rounded = jnp.where(keep, both, 0.0).astype(BF16).astype(F32)
            inter[pl.ds(r, first_rows, stride=HALF_TAPS), :] = rounded
        rows_a = inter[pl.ds(HALF_TAPS, frames), :].astype(BF16)
        rows_b = inter[pl.ds(HALF_TAPS - 1, frames), :].astype(BF16)
        lane = lax.broadcasted_iota(jnp.int32, (frames, LANES), 1)
        one = jnp.where(lane == CM, 1.0, 0.0)
        rows_ab = jnp.concatenate([rows_a, rows_b], 1)
        for r in range(HALF_TAPS):
            both = dot_nt(rows_ab, u2t[pl.ds(CM * r, LANES), :])
            cond_all[pl.ds(r, frames, stride=HALF_TAPS), :] = jnp.where(lane < CM, both, one)

        for copy in tile_copies(0, 0, 0):
            copy.wait()

    @pl.when(step + 1 < steps)
    def _():
        for copy in tile_copies(step + 1, 1 - slot, STEP):
            copy.start()

    @pl.when(step > 0)
    def _():
        for copy in tile_copies(step, slot, STEP):
            copy.wait()

    at = pl.multiple_of(step * tile, tile)
    cond = cond_all[pl.ds(at, tile), :].astype(BF16)
    column = keep_columns(starts, seq_at, resets)
    past = audio[slot, :tile, :] * jnp.concatenate([column] * (half // LANES), 1)
    pre = dot(past, wd[:half, :]) + dot(audio[slot, STEP:, :], wd[half:, :]) + dot(cond, wc[...])
    th = jnp.tanh(pre[:, :half])
    sg = 0.5 * jnp.tanh(0.5 * pre[:, half:]) + 0.5
    gated = (th * sg).astype(BF16)
    gated_out[...] = gated
    dg = dot(g_res[slot], wot[:half, :]) + dot(g_skip[slot], wot[half:, :])
    dgs = dg * sg
    dp = jnp.concatenate([dgs * (1.0 - th * th), dgs * th * (1.0 - sg)], 1).astype(BF16)
    dp_out[...] = dp
    dcond_all[pl.ds(at, tile), :] = dot(dp, wct[...])
    owg[...] += dot(gt[slot], gated)
    xg[...] += dot(jnp.concatenate([xt[slot], cond.T], 0), dp)

    @pl.when(step == 0)
    def _():
        xg[:half, :] += dot_tn(past[:STEP, :], dp[:STEP, :])
        halo[:STEP, :] = dp[:STEP, :] * jnp.concatenate([column[:STEP, :]] * (2 * half // LANES), 1)

    @pl.when(step == pl.num_programs(0) - 1)
    def _():
        def give(a, k, first, count):
            part, lines = pl.ds(pl.multiple_of(a * 8, 8), 8), pl.ds(first, count)
            src, dst = ((mine, stay), (theirs, send))[k]
            return pltpu.make_async_copy(src.at[part, lines], dst.at[part, lines], out_sems.at[first // BIG, k, a])

        def pack_big(a, _):
            for k, (out, side) in enumerate(((mine, core[0]), (theirs, 1 - core[0]))):
                for b in range(8):
                    rows = pl.ds(pl.multiple_of(a * 128 + side * 64 + b * 8, 8), 8)
                    place = a * 8 + b
                    for m in range(4):
                        two = [xg[rows, pl.ds(256 * m, 128)], xg[rows, pl.ds(256 * m + 128, 128)]]
                        out[place, pl.ds(16 * m, 16), :] = jnp.concatenate(two, 0).astype(BF16)
                    for m in range(2):
                        two = [owg[rows, pl.ds(256 * m, 128)], owg[rows, pl.ds(256 * m + 128, 128)]]
                        out[place, pl.ds(64 + 16 * m, 16), :] = jnp.concatenate(two, 0).astype(BF16)
                give(a, k, 0, BIG).start()
            return _

        lax.fori_loop(0, 8, pack_big, 0)
        rows_a = inter[pl.ds(HALF_TAPS, frames), :].astype(BF16)
        rows_b = inter[pl.ds(HALF_TAPS - 1, frames), :].astype(BF16)
        both = jnp.concatenate([rows_a, rows_b], 1)
        keep = lane_mask(frames)
        sums = jnp.zeros((frames, 2 * LANES), F32)

        def put(grads, tap, first):
            for q in range(CM // SHARE):
                du[pl.ds((CM // SHARE * tap + q) * 2 * SHARE + first, SHARE), :] = grads[SHARE * q : SHARE * (q + 1)]

        for r in range(HALF_TAPS):
            e = jnp.where(keep, dcond_all[pl.ds(r, frames, stride=HALF_TAPS), :], 0.0).astype(BF16)
            grads = dot_tn(e, both)
            put(grads[:, :LANES], r, SHARE)
            put(grads[:, LANES:], r + HALF_TAPS, SHARE)
            sums += dot(e, u2t[pl.ds(CM * r, LANES), :])
        dinter[...] = jnp.zeros_like(dinter)
        dinter[pl.ds(HALF_TAPS, frames), :] = sums[:, :LANES]
        dinter[pl.ds(HALF_TAPS - 1, frames), :] += sums[:, LANES:]
        mels = jnp.concatenate([mel_a[...], mel_b[...]], 1)
        keep = lane_mask(first_rows)
        mel_sums = jnp.zeros((first_rows, 2 * LANES), F32)
        for r in range(HALF_TAPS):
            f = jnp.where(keep, dinter[pl.ds(r, first_rows, stride=HALF_TAPS), :], 0.0).astype(BF16)
            grads = dot_tn(f, mels)
            put(grads[:, :LANES], r, 0)
            put(grads[:, LANES:], r + HALF_TAPS, 0)
            mel_sums += dot(f, u1t[pl.ds(CM * r, LANES), :])
        zero = jnp.zeros((1, LANES), F32)
        mel_sum = jnp.concatenate([zero, mel_sums[:, :LANES]], 0) + jnp.concatenate([mel_sums[:, LANES:], zero], 0)
        real = mel_rows.shape[0]
        mel_rows[...] = mel_sum[2 : 2 + real]
        give_mel.start()
        halo[STEP:, :] = jnp.zeros_like(halo[STEP:, :])
        halo[STEP:, :LANES] = jnp.concatenate([mel_sum[:2], jnp.zeros((14, LANES), F32)], 0).astype(BF16)
        xg[2 * half + CM + 1 : 2 * half + CM + 2, :] = jnp.sum(g_sum[...], 0, keepdims=True)
        cwgt = xg[2 * half :, :].T
        dcond_all[: cwgt.shape[0], :] = cwgt

        def pack_small(a, _):
            for k, (out, side) in enumerate(((mine, core[0]), (theirs, 1 - core[0]))):
                for b in range(8):
                    at_row = pl.multiple_of(a * 128 + side * 64 + b * 8, 8)
                    narrow = du[pl.ds(pl.multiple_of(at_row * 5, 8), 2 * SHARE), :]
                    folded = fold(dcond_all[pl.ds(at_row, 8), :], narrow[:SHARE], narrow[SHARE:])
                    out[a * 8 + b, pl.ds(BIG, LINES - BIG), :] = folded.astype(BF16)
                give(a, k, BIG, LINES - BIG).start()
            return _

        lax.fori_loop(0, 8, pack_small, 0)

        def finish(a, _):
            for k in range(2):
                give(a, k, 0, BIG).wait()
                give(a, k, BIG, LINES - BIG).wait()
            return _

        lax.fori_loop(0, 8, finish, 0)
        give_mel.wait()


def main_pass(core, starts, seq_at, resets, mel_a, mel_b, tails, audio, g_res, g_skip, xt, gt, g_sum, own, other, tile):
    samples, width = audio.shape
    first_rows = mel_a.shape[0]

    def whole(shape):
        return pl.BlockSpec(shape, lambda i: (0,) * len(shape))

    anywhere = pl.BlockSpec(memory_space=pl.ANY)
    hbm = pl.BlockSpec(memory_space=pltpu.HBM)
    packed = (64, LINES, LANES)
    outs = [
        ((samples, 2 * width), BF16),
        ((samples, width), BF16),
        (packed, BF16),
        (packed, BF16),
        ((samples // (HALF_TAPS * HALF_TAPS), LANES), F32),
        ((STEP + 16, 2 * width), BF16),
    ]
    return pl.pallas_call(
        main_kernel,
        grid=(samples // tile,),
        in_specs=[pl.BlockSpec(memory_space=pltpu.SMEM)] * 3
        + [pl.BlockSpec((1, tile), lambda i: (0, i))]
        + [whole(mel_a.shape), whole(mel_b.shape), whole((STEP, width))]
        + [anywhere] * 5
        + [whole((8, 2 * width)), anywhere, anywhere],
        out_specs=[
            pl.BlockSpec((tile, 2 * width), lambda i: (i, 0)),
            pl.BlockSpec((tile, width), lambda i: (i, 0)),
        ]
        + [hbm] * 3
        + [whole(s) for s, _ in outs[5:]],
        out_shape=[roomy(s, d) if s == outs[4][0] else jax.ShapeDtypeStruct(s, d) for s, d in outs],
        scratch_shapes=[
            pltpu.VMEM((2 * width, 2 * width), BF16),
            pltpu.VMEM((2 * width, width), BF16),
            pltpu.VMEM((2 * width, LANES), BF16),
            pltpu.VMEM((HALF_TAPS * CM + 48, 2 * LANES), BF16),
            pltpu.VMEM((HALF_TAPS * CM + 48, 2 * LANES), BF16),
            pltpu.VMEM((LANES, 2 * width), BF16),
            pltpu.VMEM((first_rows * HALF_TAPS, LANES), F32),
            pltpu.VMEM((samples, LANES), F32),
            pltpu.VMEM((samples, LANES), F32),
            pltpu.VMEM((first_rows * HALF_TAPS, LANES), F32),
            pltpu.VMEM((2 * width + LANES, 2 * width), F32),
            pltpu.VMEM((2 * width, width), F32),
            pltpu.VMEM((2 * TAPS * CM, LANES), F32),
            pltpu.VMEM(packed, BF16),
            pltpu.VMEM(packed, BF16),
            pltpu.VMEM(outs[4][0], F32),
            pltpu.VMEM((2, tile + STEP, width), BF16),
            pltpu.VMEM((2, tile, width), BF16),
            pltpu.VMEM((2, tile, width), BF16),
            pltpu.VMEM((2, 2 * width, tile), BF16),
            pltpu.VMEM((2, 2 * width, tile), BF16),
            pltpu.SemaphoreType.DMA((2,)),
            pltpu.SemaphoreType.DMA((2, 2, 8)),
            pltpu.SemaphoreType.DMA,
            pltpu.SemaphoreType.DMA((2, 5)),
        ],
        compiler_params=pltpu.CompilerParams(vmem_limit_bytes=VMEM_BYTES),
        cost_estimate=pl.CostEstimate(
            flops=28_000_000_000, bytes_accessed=48 * samples * width, transcendentals=0
        ),
    )(core, starts, seq_at, resets, mel_a, mel_b, tails, audio, g_res, g_skip, xt, gt, g_sum, own, other)


def tail_kernel(
    core, dp, dp_next, gated, audio, g_res, mask, mask_next, own, other, pair,
    res_out, skip_out, res_grad, rest, wd_past,
    wd, wot, wct, ob, wdt, wo, mine, theirs, in_sems,
):
    step = pl.program_id(0)
    tile, half = audio.shape

    @pl.when(step == 0)
    def _():
        fetch = [pltpu.make_async_copy(a, b, in_sems.at[k]) for k, (a, b) in enumerate(((own, mine), (other, theirs)))]
        for copy in fetch:
            copy.start()
        for copy in fetch:
            copy.wait()

        def unpack(a, _):
            for ref, side in ((mine, core[0]), (theirs, 1 - core[0])):
                unpack_wide(ref, a, side, wd, wot)
                unpack_head(ref, a, side, wct)
            return _

        lax.fori_loop(0, 8, unpack, 0)
        ob[...] = wct[...].T[CM + 1 : CM + 2, :].astype(F32)
        wdt[...] = wd[...].T
        wo[...] = wot[...].T
        wd_past[...] = wdt[:, :half]

    out = dot(gated[...], wo[...]) + ob[...]
    res_out[...] = (audio[...].astype(F32) + out[:, :half]).astype(BF16)
    skip_out[...] = out[:, half:].astype(BF16)
    last = step == pl.num_programs(0) - 1
    after = jnp.where(last, jnp.zeros_like(dp_next[...]), dp_next[...])
    ahead = jnp.concatenate([dp[STEP:, :], after], 0)
    d_past = dot(ahead, wdt[:, :half]).astype(BF16)
    kept = jnp.concatenate([mask[STEP:, :], mask_next[...]], 0)
    d_past = (d_past * jnp.concatenate([kept] * (half // LANES), 1)).astype(F32)
    here = g_res[...].astype(F32) + dot(dp[...], wdt[:, half:])
    rest[...] = here[tile - STEP :, :]
    res_grad[...] = (here + d_past).astype(BF16)


def tail_pass(core, dp, gated, audio, g_res, mask, own, other, pair, tile):
    samples, width = audio.shape
    rows = pl.BlockSpec((tile, width), lambda i: (i, 0))
    anywhere = pl.BlockSpec(memory_space=pl.ANY)
    step_blocks = tile // STEP
    final = samples // STEP - 1

    def whole(shape):
        return pl.BlockSpec(shape, lambda i: (0,) * len(shape))

    shape = jax.ShapeDtypeStruct((samples, width), BF16)
    return pl.pallas_call(
        tail_kernel,
        grid=(samples // tile,),
        in_specs=[
            pl.BlockSpec(memory_space=pltpu.SMEM),
            pl.BlockSpec((tile, 2 * width), lambda i: (i, 0)),
            pl.BlockSpec((STEP, 2 * width), lambda i: (jnp.minimum((i + 1) * step_blocks, final), 0)),
            rows,
            rows,
            rows,
            pl.BlockSpec((tile, LANES), lambda i: (i, 0)),
            pl.BlockSpec((STEP, LANES), lambda i: (jnp.minimum((i + 1) * step_blocks, final), 0)),
            anywhere,
            anywhere,
            anywhere,
        ],
        out_specs=[rows] * 3 + [whole((STEP, width)), whole((2 * width, width))],
        out_shape=[shape] * 3
        + [roomy((STEP, width), F32), roomy((2 * width, width), BF16)],
        scratch_shapes=[
            pltpu.VMEM((2 * width, 2 * width), BF16),
            pltpu.VMEM((2 * width, width), BF16),
            pltpu.VMEM((2 * width, LANES), BF16),
            pltpu.VMEM((1, 2 * width), F32),
            pltpu.VMEM((2 * width, 2 * width), BF16),
            pltpu.VMEM((width, 2 * width), BF16),
            pltpu.VMEM(own.shape, BF16),
            pltpu.VMEM(own.shape, BF16),
            pltpu.SemaphoreType.DMA((2,)),
        ],
        compiler_params=pltpu.CompilerParams(vmem_limit_bytes=TAIL_VMEM_BYTES),
        cost_estimate=pl.CostEstimate(
            flops=13_000_000_000, bytes_accessed=20 * samples * width, transcendentals=0
        ),
    )(core, dp, dp, gated, audio, g_res, mask, mask, own, other, pair)


def end_kernel(
    grad, rest, halo, wd_past, mel_here, parts,
    out, mel_out, wd, wot, wct, u1t, u2t, gb, ob,
    total,
):
    step = pl.program_id(0)

    @pl.when(step == 0)
    def _():
        total[...] = jnp.zeros_like(total)
        out[...] = (rest[...] + dot(halo[:STEP, :], wd_past[...]).astype(BF16).astype(F32)).astype(BF16)
        frames = mel_here.shape[0]
        back = halo[STEP:, :LANES].astype(F32)[:2]
        mel = mel_here[...] + jnp.concatenate([jnp.zeros((frames - 2, LANES), F32), back], 0)
        mel_out[...] = mel[:, :CM].astype(BF16)

    total[...] += jnp.sum(parts[...].astype(F32), 0)

    @pl.when(step == pl.num_programs(0) - 1)
    def _():
        for j in range(8):
            wd[:, LANES * j : LANES * (j + 1)] = total[8 * j : 8 * j + 8, :]
        for j in range(4):
            wot[:, LANES * j : LANES * (j + 1)] = total[64 + 8 * j : 72 + 8 * j, :]
        head, u1, u2 = unfold(total[BIG:, :])
        wct[...] = head[:, :CM]
        u1t[...] = u1[:, :CM]
        u2t[...] = u2[:, :CM]
        diagonal = lax.broadcasted_iota(jnp.int32, (8, 8), 0) == lax.broadcasted_iota(jnp.int32, (8, 8), 1)
        for lane, row in ((CM, gb), (CM + 1, ob)):
            column = jnp.broadcast_to(head[:, lane : lane + 1], (8, 8))
            row[...] = jnp.sum(jnp.where(diagonal, column, 0.0), 0, keepdims=True)


def end_pass(grad, rest, halo, wd_past, mel_here, parts, frames):
    samples, width = grad.shape
    steps = 4
    shapes = [(8, 1024), (8, 512), (8, CM), (SHARE, CM), (SHARE, CM), (1, 8), (1, 8)]

    def whole(shape):
        return pl.BlockSpec(shape, lambda i: (0,) * len(shape))

    return pl.pallas_call(
        end_kernel,
        grid=(steps,),
        in_specs=[pl.BlockSpec(memory_space=pl.ANY)]
        + [whole(s) for s in ((STEP, width), halo.shape, (2 * width, width), (frames, LANES))]
        + [pl.BlockSpec((64 // steps, LINES, LANES), lambda i: (i, 0, 0))],
        out_specs=[pl.BlockSpec((STEP, width), lambda i: (samples // STEP - 1, 0))]
        + [whole(s) for s in [(frames, CM)] + shapes],
        out_shape=[jax.ShapeDtypeStruct(grad.shape, BF16), jax.ShapeDtypeStruct((frames, CM), BF16)]
        + [jax.ShapeDtypeStruct(s, F32) for s in shapes],
        scratch_shapes=[pltpu.VMEM((LINES, LANES), F32)],
        input_output_aliases={0: 0},
        compiler_params=pltpu.CompilerParams(vmem_limit_bytes=END_VMEM_BYTES),
    )(grad, rest, halo, wd_past, mel_here, parts)


def shifted(value, steps, count=8):
    first, last = max(0, -steps), min(count, count - steps)
    return lax.ppermute(value, SEQ, [(s, s + steps) for s in range(first, last)])


def no_change(value):
    return jnp.minimum(jnp.abs(value), 0)


def swap(value):
    return lax.ppermute(value, "c", [(0, 1), (1, 0)])


def on_device(
    residual_input, mel_input_frames, starts, resets, residual_gradient, skip_gradient,
    first_upsample_weight, second_upsample_weight, conditioning_weight, dilated_weight,
    gate_bias_vector, output_weight, output_bias_vector,
):
    core = lax.axis_index("c")
    audio, mel = residual_input[0], mel_input_frames[0]
    g_res, g_skip = residual_gradient[0], skip_gradient[0]
    samples, width = audio.shape
    frames = mel.shape[0]

    tails = jnp.concatenate([audio[-STEP:], jnp.pad(mel[-2:], ((0, 14), (0, width - CM)))], 0)
    tails = shifted(tails, 1)

    shares = spread(
        dilated_weight,
        output_weight.T,
        conditioning_weight.T,
        first_upsample_weight.T,
        second_upsample_weight.T,
        gate_bias_vector[None],
        output_bias_vector[None],
    )
    own = lax.all_to_all(shares, CHIPS, 0, 0)

    mel_tail = tails[STEP : STEP + 2, :CM]
    mel_ext = jnp.concatenate([mel_tail, mel, jnp.zeros((14, CM), BF16)], 0)
    mel_ext = jnp.pad(mel_ext, ((0, 0), (0, LANES - CM)))
    mel_b, mel_a = mel_ext[: 2 * frames - 8], mel_ext[1 : 2 * frames - 7]
    seq_at = lax.axis_index(SEQ).astype(jnp.int32)[None]
    mask, xt, gt, g_sum = turn(starts, seq_at, resets, audio, g_res, g_skip, 512)

    zero = no_change(jnp.abs(gt[0, 0]) + jnp.abs(mel_a[0, 0]))
    own = lax.dynamic_update_slice(own, own[:1, :16] + zero, (0, 0, 0))
    other = swap(own)

    core = core.astype(jnp.int32)[None]
    dp, gated, stay, send, mel_here, halo = main_pass(
        core, starts, seq_at, resets, mel_a, mel_b, tails, audio, g_res, g_skip, xt, gt, g_sum, own, other, 512
    )

    came = swap(send)
    pair = stay + came
    all_parts = lax.all_to_all(pair, CHIPS, 0, 0)

    halo_next = shifted(halo, -1)
    res_out, skip_out, res_grad, rest, wd_past = tail_pass(
        core, dp, gated, audio, g_res, mask, own, other, pair, 512
    )
    res_grad, mel_grad, d_wd, d_wot, d_wct, d_u1t, d_u2t, d_gb, d_ob = end_pass(
        res_grad, rest, halo_next, wd_past, mel_here, all_parts, frames
    )
    return (
        res_out[None],
        skip_out[None],
        res_grad[None],
        mel_grad[None],
        d_u1t.T,
        d_u2t.T,
        d_wct.T,
        d_wd,
        d_gb[0],
        d_wot.T,
        d_ob[0],
    )


def solution(mesh):
    fine = Mesh(mesh.devices.reshape(4, 2, 2, 2, 4), ("y", "xh", "c", "xl", "z"))
    dp, seq = ("y", "xh", "c"), ("xl", "z")
    every = dp + seq
    return jax.shard_map(
        on_device,
        mesh=fine,
        in_specs=(
            P(dp, seq, None),
            P(dp, seq, None),
            P(dp, None),
            P(dp, seq),
            P(dp, seq, None),
            P(dp, seq, None),
            P(None, every),
            P(None, every),
            P(None, every),
            P(every, None),
            P(every),
            P(None, every),
            P(every),
        ),
        out_specs=(
            P(dp, seq, None),
            P(dp, seq, None),
            P(dp, seq, None),
            P(dp, seq, None),
            P(None, every),
            P(None, every),
            P(None, every),
            P(every, None),
            P(every),
            P(None, every),
            P(every),
        ),
        check_vma=False,
    )
```

```python
import jax
import jax.numpy as jnp
from jax import lax
from jax.experimental import pallas as pl
from jax.experimental.pallas import tpu as pltpu
from jax.sharding import Mesh, PartitionSpec as P

STEP = 64
SEQ = ("xl", "z")
CHIPS = ("y", "xh", "xl", "z")
BF16 = jnp.bfloat16
F32 = jnp.float32
LANES = 128
TAPS = 32
HALF_TAPS = 16
CM = 80
SHARE = 20
LINES = 128
BIG = 96
VMEM_BYTES = 46 * 1024 * 1024
SIDE_VMEM_BYTES = 60 * 1024 * 1024
END_VMEM_BYTES = 50 * 1024 * 1024
TAIL_VMEM_BYTES = 58 * 1024 * 1024


def dot(a, b):
    return jnp.dot(a, b, preferred_element_type=F32)


def dot_nt(a, b):
    return lax.dot_general(a, b, (((1,), (1,)), ((), ())), preferred_element_type=F32)


def dot_tn(a, b):
    return lax.dot_general(a, b, (((0,), (0,)), ((), ())), preferred_element_type=F32)


def lane_mask(rows):
    return lax.broadcasted_iota(jnp.int32, (rows, LANES), 1) < CM


SPLIT = LANES - CM
PIECE = CM - SPLIT


def fold(head, u1, u2):
    u2 = jnp.concatenate([u2, jnp.zeros((4, LANES), F32)], 0)
    lane = lax.broadcasted_iota(jnp.int32, (24, LANES), 1)
    top = jnp.where(lane[:8] < LANES - PIECE, head, pltpu.roll(u2[:8], LANES - PIECE - SPLIT, 1))
    middle = jnp.where(lane[:SHARE] < CM, u1, pltpu.roll(u2, CM, 1)[:SHARE])
    last = jnp.zeros((3, LANES), F32)
    for g in range(4):
        moved = pltpu.roll(u2, (PIECE * g - SPLIT) % LANES, 1)[8 + 3 * g : 11 + 3 * g]
        last = jnp.where(lane[:3] // PIECE == g, moved, last)
    return jnp.concatenate([top, middle, last, jnp.zeros((1, LANES), F32)], 0)


def unfold(rows):
    lane = lax.broadcasted_iota(jnp.int32, (SHARE, LANES), 1)
    low = pltpu.roll(rows[8:], LANES - CM, 1)[:SHARE]
    high = [pltpu.roll(rows[:8], (SPLIT - LANES + PIECE) % LANES, 1)]
    for g in range(4):
        high.append(pltpu.roll(rows[24:], (SPLIT - PIECE * g) % LANES, 1)[4:7])
    u2 = jnp.where(lane < SPLIT, low, jnp.concatenate(high, 0))
    return rows[:8], rows[8 : 8 + SHARE], u2


def spread_kernel(wd, wot, wct, u1t, u2t, gb, ob, out, lines, narrow):
    for j in range(8):
        lines[8 * j : 8 * j + 8, :] = wd[:, LANES * j : LANES * (j + 1)].astype(F32)
    for j in range(4):
        lines[64 + 8 * j : 72 + 8 * j, :] = wot[:, LANES * j : LANES * (j + 1)].astype(F32)
    lane = lax.broadcasted_iota(jnp.int32, (8, LANES), 1)
    diagonal = lax.broadcasted_iota(jnp.int32, (8, 8), 0) == lax.broadcasted_iota(jnp.int32, (8, 8), 1)

    def column(row):
        full = jnp.broadcast_to(row[...].astype(F32), (8, 8))
        return jnp.sum(jnp.where(diagonal, full, 0.0), 1, keepdims=True)

    narrow[...] = jnp.zeros_like(narrow)
    narrow[:8, :CM] = wct[...].astype(F32)
    narrow[8 : 8 + SHARE, :CM] = u1t[...].astype(F32)
    narrow[32 : 32 + SHARE, :CM] = u2t[...].astype(F32)
    biases = jnp.where(lane == CM, column(gb), jnp.where(lane == CM + 1, column(ob), 0.0))
    lines[BIG:, :] = fold(narrow[:8, :] + biases, narrow[8 : 8 + SHARE, :], narrow[32 : 32 + SHARE, :])
    block = lines[...].astype(BF16)
    for k in range(out.shape[0]):
        out[k] = block


def spread(wd, wot, wct, u1t, u2t, gb, ob):
    return pl.pallas_call(
        spread_kernel,
        out_shape=jax.ShapeDtypeStruct((64, LINES, LANES), BF16),
        scratch_shapes=[pltpu.VMEM((LINES, LANES), F32), pltpu.VMEM((56, LANES), F32)],
    )(wd, wot, wct, u1t, u2t, gb, ob)


def masked_past(before, audio, column):
    tile, half = audio.shape
    moved = jnp.concatenate([before, audio[: tile - STEP, :]], 0)
    return moved * jnp.concatenate([column] * (half // LANES), 1)


def roomy(shape, dtype):
    rows = 16 * 1024 * 1024 // (shape[1] * jnp.dtype(dtype).itemsize)
    return jax.ShapeDtypeStruct((rows, shape[1]), dtype)


def keep_columns(starts, seq_at, resets):
    tile = resets.shape[1]
    span = seq_at[0] * pl.num_programs(0) + pl.program_id(0)
    position = span * tile + lax.broadcasted_iota(jnp.int32, (1, tile), 1)
    blocked = position < STEP
    for k in range(starts.shape[1]):
        first = starts[0, k]
        blocked = blocked | ((first > position - STEP) & (first <= position))
    keep = jnp.where(blocked, 0, resets[...]).astype(F32)
    return jnp.broadcast_to(keep, (LANES, tile)).T.astype(BF16)


def turn_kernel(starts, seq_at, resets, audio_before, audio, g_res, g_skip, mask, xt, gt, g_sum):
    step = pl.program_id(0)
    tile, half = audio.shape
    column = keep_columns(starts, seq_at, resets)
    mask[...] = column
    before = jnp.where(step == 0, jnp.zeros_like(audio_before[...]), audio_before[...])
    xt[:half, :] = masked_past(before, audio[...], column).T
    xt[half:, :] = audio[...].T
    gt[:half, :] = g_res[...].T
    gt[half:, :] = g_skip[...].T

    @pl.when(step == 0)
    def _():
        g_sum[...] = jnp.zeros_like(g_sum)

    g_sum[:, :half] += jnp.sum(g_res[...].astype(F32).reshape(tile // 8, 8, half), 0)
    g_sum[:, half:] += jnp.sum(g_skip[...].astype(F32).reshape(tile // 8, 8, half), 0)


def turn(starts, seq_at, resets, audio, g_res, g_skip, tile):
    samples, width = audio.shape
    steps = tile // STEP
    rows = pl.BlockSpec((tile, width), lambda i: (i, 0))
    cols = pl.BlockSpec((2 * width, tile), lambda i: (0, i))
    scalars = pl.BlockSpec(memory_space=pltpu.SMEM)
    shape = jax.ShapeDtypeStruct((2 * width, samples), BF16)
    return pl.pallas_call(
        turn_kernel,
        grid=(samples // tile,),
        in_specs=[
            scalars,
            scalars,
            pl.BlockSpec((1, tile), lambda i: (0, i)),
            pl.BlockSpec((STEP, width), lambda i: (jnp.maximum(i * steps - 1, 0), 0)),
            rows,
            rows,
            rows,
        ],
        out_specs=[
            pl.BlockSpec((tile, LANES), lambda i: (i, 0)),
            cols,
            cols,
            pl.BlockSpec((8, 2 * width), lambda i: (0, 0)),
        ],
        out_shape=[
            jax.ShapeDtypeStruct((samples, LANES), BF16),
            shape,
            shape,
            roomy((8, 2 * width), F32),
        ],
        compiler_params=pltpu.CompilerParams(vmem_limit_bytes=SIDE_VMEM_BYTES),
        cost_estimate=pl.CostEstimate(flops=0, bytes_accessed=18 * samples * width, transcendentals=0),
    )(starts, seq_at, resets, audio, audio, g_res, g_skip)


def unpack_wide(ref, a, side, wd, wot):
    for b in range(0, 8, 2):
        rows = pl.ds(pl.multiple_of(a * 128 + side * 64 + b * 8, 16), 16)
        pair = [a * 8 + b, a * 8 + b + 1]
        for out, first, count in ((wd, 0, 4), (wot, 64, 2)):
            for m in range(count):
                two = [ref[k, pl.ds(first + 16 * m, 16), :].astype(F32) for k in pair]
                out[rows, pl.ds(256 * m, 128)] = jnp.concatenate([t[:8] for t in two], 0).astype(BF16)
                out[rows, pl.ds(256 * m + 128, 128)] = jnp.concatenate([t[8:] for t in two], 0).astype(BF16)


def unpack_head(ref, a, side, wct):
    for b in range(0, 8, 2):
        rows = pl.ds(pl.multiple_of(a * 128 + side * 64 + b * 8, 16), 16)
        two = [ref[a * 8 + b + k, pl.ds(BIG, 16), :].astype(F32) for k in range(2)]
        wct[rows, :] = jnp.concatenate([t[:8] for t in two], 0).astype(BF16)


def main_kernel(
    core, starts, seq_at, resets, mel_a, mel_b, tails, audio_all, g_res_all, g_skip_all, xt_all, gt_all, g_sum, own, other,
    dp_out, gated_out, stay, send, mel_here, halo,
    wd, wot, wct, u1t, u2t, wc, inter, cond_all, dcond_all, dinter, xg, owg, du, mine, theirs, mel_rows,
    audio, g_res, g_skip, xt, gt, in_sems, out_sems, mel_sem, tile_sems,
):
    step = pl.program_id(0)
    steps = pl.num_programs(0)
    tile, half = g_res.shape[1:]
    frames = cond_all.shape[0] // HALF_TAPS
    first_rows = mel_a.shape[0]
    slot = lax.rem(step, 2)

    def tile_copies(i, to, lead):
        at = pl.multiple_of(i * tile, tile)
        rows, cols = pl.ds(at, tile), pl.ds(at, tile)
        audio_from = pl.ds(pl.multiple_of(i * tile - lead, STEP), tile + lead)
        pairs = (
            (audio_all.at[audio_from], audio.at[to, pl.ds(STEP - lead, tile + lead)]),
            (g_res_all.at[rows], g_res.at[to]),
            (g_skip_all.at[rows], g_skip.at[to]),
            (xt_all.at[:, cols], xt.at[to]),
            (gt_all.at[:, cols], gt.at[to]),
        )
        return [pltpu.make_async_copy(a, b, tile_sems.at[to, k]) for k, (a, b) in enumerate(pairs)]

    give_mel = pltpu.make_async_copy(mel_rows, mel_here.at[pl.ds(0, mel_rows.shape[0])], mel_sem)

    @pl.when(step == 0)
    def _():
        fetched = ((own, mine), (other, theirs))
        fetch = [pltpu.make_async_copy(a, b, in_sems.at[k]) for k, (a, b) in enumerate(fetched)]
        for copy in fetch:
            copy.start()
        audio[0, :STEP, :] = tails[...]
        xg[...] = jnp.zeros_like(xg)
        owg[...] = jnp.zeros_like(owg)
        u1t[HALF_TAPS * CM :, :] = jnp.zeros_like(u1t[HALF_TAPS * CM :, :])
        u2t[HALF_TAPS * CM :, :] = jnp.zeros_like(u2t[HALF_TAPS * CM :, :])
        for copy, ref, side in ((fetch[0], mine, core[0]), (fetch[1], theirs, 1 - core[0])):
            copy.wait()
            if ref is theirs:
                for other_copy in tile_copies(0, 0, 0):
                    other_copy.start()

            def unpack(a, _, ref=ref, side=side):
                unpack_wide(ref, a, side, wd, wot)
                unpack_head(ref, a, side, wct)
                for b in range(0, 8, 4):
                    tap_row = pl.multiple_of((a % 4 * 16 + side * 8 + b) * SHARE, 16)
                    lanes = pl.ds(pl.multiple_of(a // 4 * LANES, LANES), LANES)
                    four = [unfold(ref[a * 8 + b + k, pl.ds(BIG, 32), :].astype(F32)) for k in range(4)]
                    for k, out in ((1, u1t), (2, u2t)):
                        out[pl.ds(tap_row, CM), lanes] = jnp.concatenate([t[k] for t in four], 0).astype(BF16)
                return _

            lax.fori_loop(0, 8, unpack, 0)
        wc[...] = wct[...].T
        keep = lane_mask(first_rows)
        mels = jnp.concatenate([mel_a[...], mel_b[...]], 1)
        for r in range(HALF_TAPS):
            both = dot_nt(mels, u1t[pl.ds(CM * r, LANES), :])
            rounded = jnp.where(keep, both, 0.0).astype(BF16).astype(F32)
            inter[pl.ds(r, first_rows, stride=HALF_TAPS), :] = rounded
        rows_a = inter[pl.ds(HALF_TAPS, frames), :].astype(BF16)
        rows_b = inter[pl.ds(HALF_TAPS - 1, frames), :].astype(BF16)
        lane = lax.broadcasted_iota(jnp.int32, (frames, LANES), 1)
        one = jnp.where(lane == CM, 1.0, 0.0)
        rows_ab = jnp.concatenate([rows_a, rows_b], 1)
        for r in range(HALF_TAPS):
            both = dot_nt(rows_ab, u2t[pl.ds(CM * r, LANES), :])
            cond_all[pl.ds(r, frames, stride=HALF_TAPS), :] = jnp.where(lane < CM, both, one)

        for copy in tile_copies(0, 0, 0):
            copy.wait()

    @pl.when(step + 1 < steps)
    def _():
        for copy in tile_copies(step + 1, 1 - slot, STEP):
            copy.start()

    @pl.when(step > 0)
    def _():
        for copy in tile_copies(step, slot, STEP):
            copy.wait()

    at = pl.multiple_of(step * tile, tile)
    cond = cond_all[pl.ds(at, tile), :].astype(BF16)
    column = keep_columns(starts, seq_at, resets)
    past = audio[slot, :tile, :] * jnp.concatenate([column] * (half // LANES), 1)
    pre = dot(past, wd[:half, :]) + dot(audio[slot, STEP:, :], wd[half:, :]) + dot(cond, wc[...])
    th = jnp.tanh(pre[:, :half])
    sg = 0.5 * jnp.tanh(0.5 * pre[:, half:]) + 0.5
    gated = (th * sg).astype(BF16)
    gated_out[...] = gated
    dg = dot(g_res[slot], wot[:half, :]) + dot(g_skip[slot], wot[half:, :])
    dgs = dg * sg
    dp = jnp.concatenate([dgs * (1.0 - th * th), dgs * th * (1.0 - sg)], 1).astype(BF16)
    dp_out[...] = dp
    dcond_all[pl.ds(at, tile), :] = dot(dp, wct[...])
    owg[...] += dot(gt[slot], gated)
    xg[...] += dot(jnp.concatenate([xt[slot], cond.T], 0), dp)

    @pl.when(step == 0)
    def _():
        xg[:half, :] += dot_tn(past[:STEP, :], dp[:STEP, :])
        halo[:STEP, :] = dp[:STEP, :] * jnp.concatenate([column[:STEP, :]] * (2 * half // LANES), 1)

    @pl.when(step == pl.num_programs(0) - 1)
    def _():
        def give(a, k, first, count):
            part, lines = pl.ds(pl.multiple_of(a * 8, 8), 8), pl.ds(first, count)
            src, dst = ((mine, stay), (theirs, send))[k]
            return pltpu.make_async_copy(src.at[part, lines], dst.at[part, lines], out_sems.at[first // BIG, k, a])

        def pack_big(a, _):
            for k, (out, side) in enumerate(((mine, core[0]), (theirs, 1 - core[0]))):
                for b in range(8):
                    rows = pl.ds(pl.multiple_of(a * 128 + side * 64 + b * 8, 8), 8)
                    place = a * 8 + b
                    for m in range(4):
                        two = [xg[rows, pl.ds(256 * m, 128)], xg[rows, pl.ds(256 * m + 128, 128)]]
                        out[place, pl.ds(16 * m, 16), :] = jnp.concatenate(two, 0).astype(BF16)
                    for m in range(2):
                        two = [owg[rows, pl.ds(256 * m, 128)], owg[rows, pl.ds(256 * m + 128, 128)]]
                        out[place, pl.ds(64 + 16 * m, 16), :] = jnp.concatenate(two, 0).astype(BF16)
                give(a, k, 0, BIG).start()
            return _

        lax.fori_loop(0, 8, pack_big, 0)
        rows_a = inter[pl.ds(HALF_TAPS, frames), :].astype(BF16)
        rows_b = inter[pl.ds(HALF_TAPS - 1, frames), :].astype(BF16)
        both = jnp.concatenate([rows_a, rows_b], 1)
        keep = lane_mask(frames)
        sums = jnp.zeros((frames, 2 * LANES), F32)

        def put(grads, tap, first):
            for q in range(CM // SHARE):
                du[pl.ds((CM // SHARE * tap + q) * 2 * SHARE + first, SHARE), :] = grads[SHARE * q : SHARE * (q + 1)]

        for r in range(HALF_TAPS):
            e = jnp.where(keep, dcond_all[pl.ds(r, frames, stride=HALF_TAPS), :], 0.0).astype(BF16)
            grads = dot_tn(e, both)
            put(grads[:, :LANES], r, SHARE)
            put(grads[:, LANES:], r + HALF_TAPS, SHARE)
            sums += dot(e, u2t[pl.ds(CM * r, LANES), :])
        dinter[...] = jnp.zeros_like(dinter)
        dinter[pl.ds(HALF_TAPS, frames), :] = sums[:, :LANES]
        dinter[pl.ds(HALF_TAPS - 1, frames), :] += sums[:, LANES:]
        mels = jnp.concatenate([mel_a[...], mel_b[...]], 1)
        keep = lane_mask(first_rows)
        mel_sums = jnp.zeros((first_rows, 2 * LANES), F32)
        for r in range(HALF_TAPS):
            f = jnp.where(keep, dinter[pl.ds(r, first_rows, stride=HALF_TAPS), :], 0.0).astype(BF16)
            grads = dot_tn(f, mels)
            put(grads[:, :LANES], r, 0)
            put(grads[:, LANES:], r + HALF_TAPS, 0)
            mel_sums += dot(f, u1t[pl.ds(CM * r, LANES), :])
        zero = jnp.zeros((1, LANES), F32)
        mel_sum = jnp.concatenate([zero, mel_sums[:, :LANES]], 0) + jnp.concatenate([mel_sums[:, LANES:], zero], 0)
        real = mel_rows.shape[0]
        mel_rows[...] = mel_sum[2 : 2 + real]
        give_mel.start()
        halo[STEP:, :] = jnp.zeros_like(halo[STEP:, :])
        halo[STEP:, :LANES] = jnp.concatenate([mel_sum[:2], jnp.zeros((14, LANES), F32)], 0).astype(BF16)
        xg[2 * half + CM + 1 : 2 * half + CM + 2, :] = jnp.sum(g_sum[...], 0, keepdims=True)
        cwgt = xg[2 * half :, :].T
        dcond_all[: cwgt.shape[0], :] = cwgt

        def pack_small(a, _):
            for k, (out, side) in enumerate(((mine, core[0]), (theirs, 1 - core[0]))):
                for b in range(8):
                    at_row = pl.multiple_of(a * 128 + side * 64 + b * 8, 8)
                    narrow = du[pl.ds(pl.multiple_of(at_row * 5, 8), 2 * SHARE), :]
                    folded = fold(dcond_all[pl.ds(at_row, 8), :], narrow[:SHARE], narrow[SHARE:])
                    out[a * 8 + b, pl.ds(BIG, LINES - BIG), :] = folded.astype(BF16)
                give(a, k, BIG, LINES - BIG).start()
            return _

        lax.fori_loop(0, 8, pack_small, 0)

        def finish(a, _):
            for k in range(2):
                give(a, k, 0, BIG).wait()
                give(a, k, BIG, LINES - BIG).wait()
            return _

        lax.fori_loop(0, 8, finish, 0)
        give_mel.wait()


def main_pass(core, starts, seq_at, resets, mel_a, mel_b, tails, audio, g_res, g_skip, xt, gt, g_sum, own, other, tile):
    samples, width = audio.shape
    first_rows = mel_a.shape[0]

    def whole(shape):
        return pl.BlockSpec(shape, lambda i: (0,) * len(shape))

    anywhere = pl.BlockSpec(memory_space=pl.ANY)
    hbm = pl.BlockSpec(memory_space=pltpu.HBM)
    packed = (64, LINES, LANES)
    outs = [
        ((samples, 2 * width), BF16),
        ((samples, width), BF16),
        (packed, BF16),
        (packed, BF16),
        ((samples // (HALF_TAPS * HALF_TAPS), LANES), F32),
        ((STEP + 16, 2 * width), BF16),
    ]
    return pl.pallas_call(
        main_kernel,
        grid=(samples // tile,),
        in_specs=[pl.BlockSpec(memory_space=pltpu.SMEM)] * 3
        + [pl.BlockSpec((1, tile), lambda i: (0, i))]
        + [whole(mel_a.shape), whole(mel_b.shape), whole((STEP, width))]
        + [anywhere] * 5
        + [whole((8, 2 * width)), anywhere, anywhere],
        out_specs=[
            pl.BlockSpec((tile, 2 * width), lambda i: (i, 0)),
            pl.BlockSpec((tile, width), lambda i: (i, 0)),
        ]
        + [hbm] * 3
        + [whole(s) for s, _ in outs[5:]],
        out_shape=[roomy(s, d) if s == outs[4][0] else jax.ShapeDtypeStruct(s, d) for s, d in outs],
        scratch_shapes=[
            pltpu.VMEM((2 * width, 2 * width), BF16),
            pltpu.VMEM((2 * width, width), BF16),
            pltpu.VMEM((2 * width, LANES), BF16),
            pltpu.VMEM((HALF_TAPS * CM + 48, 2 * LANES), BF16),
            pltpu.VMEM((HALF_TAPS * CM + 48, 2 * LANES), BF16),
            pltpu.VMEM((LANES, 2 * width), BF16),
            pltpu.VMEM((first_rows * HALF_TAPS, LANES), F32),
            pltpu.VMEM((samples, LANES), F32),
            pltpu.VMEM((samples, LANES), F32),
            pltpu.VMEM((first_rows * HALF_TAPS, LANES), F32),
            pltpu.VMEM((2 * width + LANES, 2 * width), F32),
            pltpu.VMEM((2 * width, width), F32),
            pltpu.VMEM((2 * TAPS * CM, LANES), F32),
            pltpu.VMEM(packed, BF16),
            pltpu.VMEM(packed, BF16),
            pltpu.VMEM(outs[4][0], F32),
            pltpu.VMEM((2, tile + STEP, width), BF16),
            pltpu.VMEM((2, tile, width), BF16),
            pltpu.VMEM((2, tile, width), BF16),
            pltpu.VMEM((2, 2 * width, tile), BF16),
            pltpu.VMEM((2, 2 * width, tile), BF16),
            pltpu.SemaphoreType.DMA((2,)),
            pltpu.SemaphoreType.DMA((2, 2, 8)),
            pltpu.SemaphoreType.DMA,
            pltpu.SemaphoreType.DMA((2, 5)),
        ],
        compiler_params=pltpu.CompilerParams(vmem_limit_bytes=VMEM_BYTES),
        cost_estimate=pl.CostEstimate(
            flops=28_000_000_000, bytes_accessed=48 * samples * width, transcendentals=0
        ),
    )(core, starts, seq_at, resets, mel_a, mel_b, tails, audio, g_res, g_skip, xt, gt, g_sum, own, other)


def tail_kernel(
    core, dp, dp_next, gated, audio, g_res, mask, mask_next, own, other, pair,
    res_out, skip_out, res_grad, rest, wd_past,
    wd, wot, wct, ob, wdt, wo, mine, theirs, in_sems,
):
    step = pl.program_id(0)
    tile, half = audio.shape

    @pl.when(step == 0)
    def _():
        fetch = [pltpu.make_async_copy(a, b, in_sems.at[k]) for k, (a, b) in enumerate(((own, mine), (other, theirs)))]
        for copy in fetch:
            copy.start()
        for copy in fetch:
            copy.wait()

        def unpack(a, _):
            for ref, side in ((mine, core[0]), (theirs, 1 - core[0])):
                unpack_wide(ref, a, side, wd, wot)
                unpack_head(ref, a, side, wct)
            return _

        lax.fori_loop(0, 8, unpack, 0)
        ob[...] = wct[...].T[CM + 1 : CM + 2, :].astype(F32)
        wdt[...] = wd[...].T
        wo[...] = wot[...].T
        wd_past[...] = wdt[:, :half]

    out = dot(gated[...], wo[...]) + ob[...]
    res_out[...] = (audio[...].astype(F32) + out[:, :half]).astype(BF16)
    skip_out[...] = out[:, half:].astype(BF16)
    last = step == pl.num_programs(0) - 1
    after = jnp.where(last, jnp.zeros_like(dp_next[...]), dp_next[...])
    ahead = jnp.concatenate([dp[STEP:, :], after], 0)
    d_past = dot(ahead, wdt[:, :half]).astype(BF16)
    kept = jnp.concatenate([mask[STEP:, :], mask_next[...]], 0)
    d_past = (d_past * jnp.concatenate([kept] * (half // LANES), 1)).astype(F32)
    here = g_res[...].astype(F32) + dot(dp[...], wdt[:, half:])
    rest[...] = here[tile - STEP :, :]
    res_grad[...] = (here + d_past).astype(BF16)


def tail_pass(core, dp, gated, audio, g_res, mask, own, other, pair, tile):
    samples, width = audio.shape
    rows = pl.BlockSpec((tile, width), lambda i: (i, 0))
    anywhere = pl.BlockSpec(memory_space=pl.ANY)
    step_blocks = tile // STEP
    final = samples // STEP - 1

    def whole(shape):
        return pl.BlockSpec(shape, lambda i: (0,) * len(shape))

    shape = jax.ShapeDtypeStruct((samples, width), BF16)
    return pl.pallas_call(
        tail_kernel,
        grid=(samples // tile,),
        in_specs=[
            pl.BlockSpec(memory_space=pltpu.SMEM),
            pl.BlockSpec((tile, 2 * width), lambda i: (i, 0)),
            pl.BlockSpec((STEP, 2 * width), lambda i: (jnp.minimum((i + 1) * step_blocks, final), 0)),
            rows,
            rows,
            rows,
            pl.BlockSpec((tile, LANES), lambda i: (i, 0)),
            pl.BlockSpec((STEP, LANES), lambda i: (jnp.minimum((i + 1) * step_blocks, final), 0)),
            anywhere,
            anywhere,
            anywhere,
        ],
        out_specs=[rows] * 3 + [whole((STEP, width)), whole((2 * width, width))],
        out_shape=[shape] * 3
        + [roomy((STEP, width), F32), roomy((2 * width, width), BF16)],
        scratch_shapes=[
            pltpu.VMEM((2 * width, 2 * width), BF16),
            pltpu.VMEM((2 * width, width), BF16),
            pltpu.VMEM((2 * width, LANES), BF16),
            pltpu.VMEM((1, 2 * width), F32),
            pltpu.VMEM((2 * width, 2 * width), BF16),
            pltpu.VMEM((width, 2 * width), BF16),
            pltpu.VMEM(own.shape, BF16),
            pltpu.VMEM(own.shape, BF16),
            pltpu.SemaphoreType.DMA((2,)),
        ],
        compiler_params=pltpu.CompilerParams(vmem_limit_bytes=TAIL_VMEM_BYTES),
        cost_estimate=pl.CostEstimate(
            flops=13_000_000_000, bytes_accessed=20 * samples * width, transcendentals=0
        ),
    )(core, dp, dp, gated, audio, g_res, mask, mask, own, other, pair)


def end_kernel(
    grad, rest, halo, wd_past, mel_here, parts,
    out, mel_out, wd, wot, wct, u1t, u2t, gb, ob,
    total,
):
    step = pl.program_id(0)

    @pl.when(step == 0)
    def _():
        total[...] = jnp.zeros_like(total)
        out[...] = (rest[...] + dot(halo[:STEP, :], wd_past[...]).astype(BF16).astype(F32)).astype(BF16)
        frames = mel_here.shape[0]
        back = halo[STEP:, :LANES].astype(F32)[:2]
        mel = mel_here[...] + jnp.concatenate([jnp.zeros((frames - 2, LANES), F32), back], 0)
        mel_out[...] = mel[:, :CM].astype(BF16)

    total[...] += jnp.sum(parts[...].astype(F32), 0)

    @pl.when(step == pl.num_programs(0) - 1)
    def _():
        for j in range(8):
            wd[:, LANES * j : LANES * (j + 1)] = total[8 * j : 8 * j + 8, :]
        for j in range(4):
            wot[:, LANES * j : LANES * (j + 1)] = total[64 + 8 * j : 72 + 8 * j, :]
        head, u1, u2 = unfold(total[BIG:, :])
        wct[...] = head[:, :CM]
        u1t[...] = u1[:, :CM]
        u2t[...] = u2[:, :CM]
        diagonal = lax.broadcasted_iota(jnp.int32, (8, 8), 0) == lax.broadcasted_iota(jnp.int32, (8, 8), 1)
        for lane, row in ((CM, gb), (CM + 1, ob)):
            column = jnp.broadcast_to(head[:, lane : lane + 1], (8, 8))
            row[...] = jnp.sum(jnp.where(diagonal, column, 0.0), 0, keepdims=True)


def end_pass(grad, rest, halo, wd_past, mel_here, parts, frames):
    samples, width = grad.shape
    steps = 4
    shapes = [(8, 1024), (8, 512), (8, CM), (SHARE, CM), (SHARE, CM), (1, 8), (1, 8)]

    def whole(shape):
        return pl.BlockSpec(shape, lambda i: (0,) * len(shape))

    return pl.pallas_call(
        end_kernel,
        grid=(steps,),
        in_specs=[pl.BlockSpec(memory_space=pl.ANY)]
        + [whole(s) for s in ((STEP, width), halo.shape, (2 * width, width), (frames, LANES))]
        + [pl.BlockSpec((64 // steps, LINES, LANES), lambda i: (i, 0, 0))],
        out_specs=[pl.BlockSpec((STEP, width), lambda i: (samples // STEP - 1, 0))]
        + [whole(s) for s in [(frames, CM)] + shapes],
        out_shape=[jax.ShapeDtypeStruct(grad.shape, BF16), jax.ShapeDtypeStruct((frames, CM), BF16)]
        + [jax.ShapeDtypeStruct(s, F32) for s in shapes],
        scratch_shapes=[pltpu.VMEM((LINES, LANES), F32)],
        input_output_aliases={0: 0},
        compiler_params=pltpu.CompilerParams(vmem_limit_bytes=END_VMEM_BYTES),
    )(grad, rest, halo, wd_past, mel_here, parts)


def shifted(value, steps, count=8):
    first, last = max(0, -steps), min(count, count - steps)
    return lax.ppermute(value, SEQ, [(s, s + steps) for s in range(first, last)])


def no_change(value):
    return jnp.minimum(jnp.abs(value), 0)


def swap(value):
    return lax.ppermute(value, "c", [(0, 1), (1, 0)])


def on_device(
    residual_input, mel_input_frames, starts, resets, residual_gradient, skip_gradient,
    first_upsample_weight, second_upsample_weight, conditioning_weight, dilated_weight,
    gate_bias_vector, output_weight, output_bias_vector,
):
    core = lax.axis_index("c")
    audio, mel = residual_input[0], mel_input_frames[0]
    g_res, g_skip = residual_gradient[0], skip_gradient[0]
    samples, width = audio.shape
    frames = mel.shape[0]

    tails = jnp.concatenate([audio[-STEP:], jnp.pad(mel[-2:], ((0, 14), (0, width - CM)))], 0)
    tails = shifted(tails, 1)

    shares = spread(
        dilated_weight,
        output_weight.T,
        conditioning_weight.T,
        first_upsample_weight.T,
        second_upsample_weight.T,
        gate_bias_vector[None],
        output_bias_vector[None],
    )
    own = lax.all_to_all(shares, CHIPS, 0, 0)

    mel_tail = tails[STEP : STEP + 2, :CM]
    mel_ext = jnp.concatenate([mel_tail, mel, jnp.zeros((14, CM), BF16)], 0)
    mel_ext = jnp.pad(mel_ext, ((0, 0), (0, LANES - CM)))
    mel_b, mel_a = mel_ext[: 2 * frames - 8], mel_ext[1 : 2 * frames - 7]
    seq_at = lax.axis_index(SEQ).astype(jnp.int32)[None]
    mask, xt, gt, g_sum = turn(starts, seq_at, resets, audio, g_res, g_skip, 512)

    zero = no_change(jnp.abs(gt[0, 0]) + jnp.abs(mel_a[0, 0]))
    own = lax.dynamic_update_slice(own, own[:1, :16] + zero, (0, 0, 0))
    other = swap(own)

    core = core.astype(jnp.int32)[None]
    dp, gated, stay, send, mel_here, halo = main_pass(
        core, starts, seq_at, resets, mel_a, mel_b, tails, audio, g_res, g_skip, xt, gt, g_sum, own, other, 512
    )

    came = swap(send)
    pair = stay + came
    all_parts = lax.all_to_all(pair, CHIPS, 0, 0)

    halo_next = shifted(halo, -1)
    res_out, skip_out, res_grad, rest, wd_past = tail_pass(
        core, dp, gated, audio, g_res, mask, own, other, pair, 512
    )
    res_grad, mel_grad, d_wd, d_wot, d_wct, d_u1t, d_u2t, d_gb, d_ob = end_pass(
        res_grad, rest, halo_next, wd_past, mel_here, all_parts, frames
    )
    return (
        res_out[None],
        skip_out[None],
        res_grad[None],
        mel_grad[None],
        d_u1t.T,
        d_u2t.T,
        d_wct.T,
        d_wd,
        d_gb[0],
        d_wot.T,
        d_ob[0],
    )


def solution(mesh):
    fine = Mesh(mesh.devices.reshape(4, 2, 2, 2, 4), ("y", "xh", "c", "xl", "z"))
    dp, seq = ("y", "xh", "c"), ("xl", "z")
    every = dp + seq
    return jax.shard_map(
        on_device,
        mesh=fine,
        in_specs=(
            P(dp, seq, None),
            P(dp, seq, None),
            P(dp, None),
            P(dp, seq),
            P(dp, seq, None),
            P(dp, seq, None),
            P(None, every),
            P(None, every),
            P(None, every),
            P(every, None),
            P(every),
            P(None, every),
            P(every),
        ),
        out_specs=(
            P(dp, seq, None),
            P(dp, seq, None),
            P(dp, seq, None),
            P(dp, seq, None),
            P(None, every),
            P(None, every),
            P(None, every),
            P(every, None),
            P(every),
            P(None, every),
            P(every),
        ),
        check_vma=False,
    )
```

```python
import jax
import jax.numpy as jnp
from jax import lax
from jax.experimental import pallas as pl
from jax.experimental.pallas import tpu as pltpu
from jax.sharding import Mesh, PartitionSpec as P

STEP = 64
SEQ = ("xl", "z")
CHIPS = ("y", "xh", "xl", "z")
BF16 = jnp.bfloat16
F32 = jnp.float32
LANES = 128
TAPS = 32
HALF_TAPS = 16
CM = 80
SHARE = 20
LINES = 128
BIG = 96
VMEM_BYTES = 46 * 1024 * 1024
SIDE_VMEM_BYTES = 60 * 1024 * 1024
END_VMEM_BYTES = 50 * 1024 * 1024
TAIL_VMEM_BYTES = 58 * 1024 * 1024


def dot(a, b):
    return jnp.dot(a, b, preferred_element_type=F32)


def dot_nt(a, b):
    return lax.dot_general(a, b, (((1,), (1,)), ((), ())), preferred_element_type=F32)


def dot_tn(a, b):
    return lax.dot_general(a, b, (((0,), (0,)), ((), ())), preferred_element_type=F32)


def lane_mask(rows):
    return lax.broadcasted_iota(jnp.int32, (rows, LANES), 1) < CM


SPLIT = LANES - CM
PIECE = CM - SPLIT


def fold(head, u1, u2):
    u2 = jnp.concatenate([u2, jnp.zeros((4, LANES), F32)], 0)
    lane = lax.broadcasted_iota(jnp.int32, (24, LANES), 1)
    top = jnp.where(lane[:8] < LANES - PIECE, head, pltpu.roll(u2[:8], LANES - PIECE - SPLIT, 1))
    middle = jnp.where(lane[:SHARE] < CM, u1, pltpu.roll(u2, CM, 1)[:SHARE])
    last = jnp.zeros((3, LANES), F32)
    for g in range(4):
        moved = pltpu.roll(u2, (PIECE * g - SPLIT) % LANES, 1)[8 + 3 * g : 11 + 3 * g]
        last = jnp.where(lane[:3] // PIECE == g, moved, last)
    return jnp.concatenate([top, middle, last, jnp.zeros((1, LANES), F32)], 0)


def unfold(rows):
    lane = lax.broadcasted_iota(jnp.int32, (SHARE, LANES), 1)
    low = pltpu.roll(rows[8:], LANES - CM, 1)[:SHARE]
    high = [pltpu.roll(rows[:8], (SPLIT - LANES + PIECE) % LANES, 1)]
    for g in range(4):
        high.append(pltpu.roll(rows[24:], (SPLIT - PIECE * g) % LANES, 1)[4:7])
    u2 = jnp.where(lane < SPLIT, low, jnp.concatenate(high, 0))
    return rows[:8], rows[8 : 8 + SHARE], u2


def spread_kernel(wd, wot, wct, u1t, u2t, gb, ob, out, lines, narrow):
    for j in range(8):
        lines[8 * j : 8 * j + 8, :] = wd[:, LANES * j : LANES * (j + 1)].astype(F32)
    for j in range(4):
        lines[64 + 8 * j : 72 + 8 * j, :] = wot[:, LANES * j : LANES * (j + 1)].astype(F32)
    lane = lax.broadcasted_iota(jnp.int32, (8, LANES), 1)
    diagonal = lax.broadcasted_iota(jnp.int32, (8, 8), 0) == lax.broadcasted_iota(jnp.int32, (8, 8), 1)

    def column(row):
        full = jnp.broadcast_to(row[...].astype(F32), (8, 8))
        return jnp.sum(jnp.where(diagonal, full, 0.0), 1, keepdims=True)

    narrow[...] = jnp.zeros_like(narrow)
    narrow[:8, :CM] = wct[...].astype(F32)
    narrow[8 : 8 + SHARE, :CM] = u1t[...].astype(F32)
    narrow[32 : 32 + SHARE, :CM] = u2t[...].astype(F32)
    biases = jnp.where(lane == CM, column(gb), jnp.where(lane == CM + 1, column(ob), 0.0))
    lines[BIG:, :] = fold(narrow[:8, :] + biases, narrow[8 : 8 + SHARE, :], narrow[32 : 32 + SHARE, :])
    block = lines[...].astype(BF16)
    for k in range(out.shape[0]):
        out[k] = block


def spread(wd, wot, wct, u1t, u2t, gb, ob):
    return pl.pallas_call(
        spread_kernel,
        out_shape=jax.ShapeDtypeStruct((64, LINES, LANES), BF16),
        scratch_shapes=[pltpu.VMEM((LINES, LANES), F32), pltpu.VMEM((56, LANES), F32)],
    )(wd, wot, wct, u1t, u2t, gb, ob)


def masked_past(before, audio, column):
    tile, half = audio.shape
    moved = jnp.concatenate([before, audio[: tile - STEP, :]], 0)
    return moved * jnp.concatenate([column] * (half // LANES), 1)


def roomy(shape, dtype):
    rows = 16 * 1024 * 1024 // (shape[1] * jnp.dtype(dtype).itemsize)
    return jax.ShapeDtypeStruct((rows, shape[1]), dtype)


def keep_columns(starts, seq_at, resets):
    tile = resets.shape[1]
    span = seq_at[0] * pl.num_programs(0) + pl.program_id(0)
    position = span * tile + lax.broadcasted_iota(jnp.int32, (1, tile), 1)
    blocked = position < STEP
    for k in range(starts.shape[1]):
        first = starts[0, k]
        blocked = blocked | ((first > position - STEP) & (first <= position))
    keep = jnp.where(blocked, 0, resets[...]).astype(F32)
    return jnp.broadcast_to(keep, (LANES, tile)).T.astype(BF16)


def turn_kernel(starts, seq_at, resets, audio_before, audio, g_res, g_skip, mask, xt, gt, g_sum):
    step = pl.program_id(0)
    tile, half = audio.shape
    column = keep_columns(starts, seq_at, resets)
    mask[...] = column
    before = jnp.where(step == 0, jnp.zeros_like(audio_before[...]), audio_before[...])
    xt[:half, :] = masked_past(before, audio[...], column).T
    xt[half:, :] = audio[...].T
    gt[:half, :] = g_res[...].T
    gt[half:, :] = g_skip[...].T

    @pl.when(step == 0)
    def _():
        g_sum[...] = jnp.zeros_like(g_sum)

    g_sum[:, :half] += jnp.sum(g_res[...].astype(F32).reshape(tile // 8, 8, half), 0)
    g_sum[:, half:] += jnp.sum(g_skip[...].astype(F32).reshape(tile // 8, 8, half), 0)


def turn(starts, seq_at, resets, audio, g_res, g_skip, tile):
    samples, width = audio.shape
    steps = tile // STEP
    rows = pl.BlockSpec((tile, width), lambda i: (i, 0))
    cols = pl.BlockSpec((2 * width, tile), lambda i: (0, i))
    scalars = pl.BlockSpec(memory_space=pltpu.SMEM)
    shape = jax.ShapeDtypeStruct((2 * width, samples), BF16)
    return pl.pallas_call(
        turn_kernel,
        grid=(samples // tile,),
        in_specs=[
            scalars,
            scalars,
            pl.BlockSpec((1, tile), lambda i: (0, i)),
            pl.BlockSpec((STEP, width), lambda i: (jnp.maximum(i * steps - 1, 0), 0)),
            rows,
            rows,
            rows,
        ],
        out_specs=[
            pl.BlockSpec((tile, LANES), lambda i: (i, 0)),
            cols,
            cols,
            pl.BlockSpec((8, 2 * width), lambda i: (0, 0)),
        ],
        out_shape=[
            jax.ShapeDtypeStruct((samples, LANES), BF16),
            shape,
            shape,
            roomy((8, 2 * width), F32),
        ],
        compiler_params=pltpu.CompilerParams(vmem_limit_bytes=SIDE_VMEM_BYTES),
        cost_estimate=pl.CostEstimate(flops=0, bytes_accessed=18 * samples * width, transcendentals=0),
    )(starts, seq_at, resets, audio, audio, g_res, g_skip)


def unpack_wide(ref, a, side, wd, wot):
    for b in range(0, 8, 2):
        rows = pl.ds(pl.multiple_of(a * 128 + side * 64 + b * 8, 16), 16)
        pair = [a * 8 + b, a * 8 + b + 1]
        for out, first, count in ((wd, 0, 4), (wot, 64, 2)):
            for m in range(count):
                two = [ref[k, pl.ds(first + 16 * m, 16), :].astype(F32) for k in pair]
                out[rows, pl.ds(256 * m, 128)] = jnp.concatenate([t[:8] for t in two], 0).astype(BF16)
                out[rows, pl.ds(256 * m + 128, 128)] = jnp.concatenate([t[8:] for t in two], 0).astype(BF16)


def unpack_head(ref, a, side, wct):
    for b in range(0, 8, 2):
        rows = pl.ds(pl.multiple_of(a * 128 + side * 64 + b * 8, 16), 16)
        two = [ref[a * 8 + b + k, pl.ds(BIG, 16), :].astype(F32) for k in range(2)]
        wct[rows, :] = jnp.concatenate([t[:8] for t in two], 0).astype(BF16)


def main_kernel(
    core, starts, seq_at, resets, mel_a, mel_b, tails, audio_all, g_res_all, g_skip_all, xt_all, gt_all, g_sum, own, other,
    dp_out, gated_out, stay, send, mel_here, halo,
    wd, wot, wct, u1t, u2t, wc, inter, cond_all, dcond_all, dinter, xg, owg, du, mine, theirs, mel_rows,
    audio, g_res, g_skip, xt, gt, in_sems, out_sems, mel_sem, tile_sems,
):
    step = pl.program_id(0)
    steps = pl.num_programs(0)
    tile, half = g_res.shape[1:]
    frames = cond_all.shape[0] // HALF_TAPS
    first_rows = mel_a.shape[0]
    slot = lax.rem(step, 2)

    def tile_copies(i, to, lead):
        at = pl.multiple_of(i * tile, tile)
        rows, cols = pl.ds(at, tile), pl.ds(at, tile)
        audio_from = pl.ds(pl.multiple_of(i * tile - lead, STEP), tile + lead)
        pairs = (
            (audio_all.at[audio_from], audio.at[to, pl.ds(STEP - lead, tile + lead)]),
            (g_res_all.at[rows], g_res.at[to]),
            (g_skip_all.at[rows], g_skip.at[to]),
            (xt_all.at[:, cols], xt.at[to]),
            (gt_all.at[:, cols], gt.at[to]),
        )
        return [pltpu.make_async_copy(a, b, tile_sems.at[to, k]) for k, (a, b) in enumerate(pairs)]

    give_mel = pltpu.make_async_copy(mel_rows, mel_here.at[pl.ds(0, mel_rows.shape[0])], mel_sem)

    @pl.when(step == 0)
    def _():
        fetched = ((own, mine), (other, theirs))
        fetch = [pltpu.make_async_copy(a, b, in_sems.at[k]) for k, (a, b) in enumerate(fetched)]
        for copy in fetch:
            copy.start()
        audio[0, :STEP, :] = tails[...]
        xg[...] = jnp.zeros_like(xg)
        owg[...] = jnp.zeros_like(owg)
        u1t[HALF_TAPS * CM :, :] = jnp.zeros_like(u1t[HALF_TAPS * CM :, :])
        u2t[HALF_TAPS * CM :, :] = jnp.zeros_like(u2t[HALF_TAPS * CM :, :])
        for copy, ref, side in ((fetch[0], mine, core[0]), (fetch[1], theirs, 1 - core[0])):
            copy.wait()
            if ref is theirs:
                for other_copy in tile_copies(0, 0, 0):
                    other_copy.start()

            def unpack(a, _, ref=ref, side=side):
                unpack_wide(ref, a, side, wd, wot)
                unpack_head(ref, a, side, wct)
                for b in range(0, 8, 4):
                    tap_row = pl.multiple_of((a % 4 * 16 + side * 8 + b) * SHARE, 16)
                    lanes = pl.ds(pl.multiple_of(a // 4 * LANES, LANES), LANES)
                    four = [unfold(ref[a * 8 + b + k, pl.ds(BIG, 32), :].astype(F32)) for k in range(4)]
                    for k, out in ((1, u1t), (2, u2t)):
                        out[pl.ds(tap_row, CM), lanes] = jnp.concatenate([t[k] for t in four], 0).astype(BF16)
                return _

            lax.fori_loop(0, 8, unpack, 0)
        wc[...] = wct[...].T
        keep = lane_mask(first_rows)
        mels = jnp.concatenate([mel_a[...], mel_b[...]], 1)
        for r in range(HALF_TAPS):
            both = dot_nt(mels, u1t[pl.ds(CM * r, LANES), :])
            rounded = jnp.where(keep, both, 0.0).astype(BF16).astype(F32)
            inter[pl.ds(r, first_rows, stride=HALF_TAPS), :] = rounded
        rows_a = inter[pl.ds(HALF_TAPS, frames), :].astype(BF16)
        rows_b = inter[pl.ds(HALF_TAPS - 1, frames), :].astype(BF16)
        lane = lax.broadcasted_iota(jnp.int32, (frames, LANES), 1)
        one = jnp.where(lane == CM, 1.0, 0.0)
        rows_ab = jnp.concatenate([rows_a, rows_b], 1)
        for r in range(HALF_TAPS):
            both = dot_nt(rows_ab, u2t[pl.ds(CM * r, LANES), :])
            cond_all[pl.ds(r, frames, stride=HALF_TAPS), :] = jnp.where(lane < CM, both, one)

        for copy in tile_copies(0, 0, 0):
            copy.wait()

    @pl.when(step + 1 < steps)
    def _():
        for copy in tile_copies(step + 1, 1 - slot, STEP):
            copy.start()

    @pl.when(step > 0)
    def _():
        for copy in tile_copies(step, slot, STEP):
            copy.wait()

    at = pl.multiple_of(step * tile, tile)
    cond = cond_all[pl.ds(at, tile), :].astype(BF16)
    column = keep_columns(starts, seq_at, resets)
    past = audio[slot, :tile, :] * jnp.concatenate([column] * (half // LANES), 1)
    pre = dot(past, wd[:half, :]) + dot(audio[slot, STEP:, :], wd[half:, :]) + dot(cond, wc[...])
    th = jnp.tanh(pre[:, :half])
    sg = 0.5 * jnp.tanh(0.5 * pre[:, half:]) + 0.5
    gated = (th * sg).astype(BF16)
    gated_out[...] = gated
    dg = dot(g_res[slot], wot[:half, :]) + dot(g_skip[slot], wot[half:, :])
    dgs = dg * sg
    dp = jnp.concatenate([dgs * (1.0 - th * th), dgs * th * (1.0 - sg)], 1).astype(BF16)
    dp_out[...] = dp
    dcond_all[pl.ds(at, tile), :] = dot(dp, wct[...])
    owg[...] += dot(gt[slot], gated)
    xg[...] += dot(jnp.concatenate([xt[slot], cond.T], 0), dp)

    @pl.when(step == 0)
    def _():
        xg[:half, :] += dot_tn(past[:STEP, :], dp[:STEP, :])
        halo[:STEP, :] = dp[:STEP, :] * jnp.concatenate([column[:STEP, :]] * (2 * half // LANES), 1)

    @pl.when(step == pl.num_programs(0) - 1)
    def _():
        def give(a, k, first, count):
            part, lines = pl.ds(pl.multiple_of(a * 8, 8), 8), pl.ds(first, count)
            src, dst = ((mine, stay), (theirs, send))[k]
            return pltpu.make_async_copy(src.at[part, lines], dst.at[part, lines], out_sems.at[first // BIG, k, a])

        def pack_big(a, _):
            for k, (out, side) in enumerate(((mine, core[0]), (theirs, 1 - core[0]))):
                for b in range(8):
                    rows = pl.ds(pl.multiple_of(a * 128 + side * 64 + b * 8, 8), 8)
                    place = a * 8 + b
                    for m in range(4):
                        two = [xg[rows, pl.ds(256 * m, 128)], xg[rows, pl.ds(256 * m + 128, 128)]]
                        out[place, pl.ds(16 * m, 16), :] = jnp.concatenate(two, 0).astype(BF16)
                    for m in range(2):
                        two = [owg[rows, pl.ds(256 * m, 128)], owg[rows, pl.ds(256 * m + 128, 128)]]
                        out[place, pl.ds(64 + 16 * m, 16), :] = jnp.concatenate(two, 0).astype(BF16)
                give(a, k, 0, BIG).start()
            return _

        lax.fori_loop(0, 8, pack_big, 0)
        rows_a = inter[pl.ds(HALF_TAPS, frames), :].astype(BF16)
        rows_b = inter[pl.ds(HALF_TAPS - 1, frames), :].astype(BF16)
        both = jnp.concatenate([rows_a, rows_b], 1)
        keep = lane_mask(frames)
        sums = jnp.zeros((frames, 2 * LANES), F32)

        def put(grads, tap, first):
            for q in range(CM // SHARE):
                du[pl.ds((CM // SHARE * tap + q) * 2 * SHARE + first, SHARE), :] = grads[SHARE * q : SHARE * (q + 1)]

        for r in range(HALF_TAPS):
            e = jnp.where(keep, dcond_all[pl.ds(r, frames, stride=HALF_TAPS), :], 0.0).astype(BF16)
            grads = dot_tn(e, both)
            put(grads[:, :LANES], r, SHARE)
            put(grads[:, LANES:], r + HALF_TAPS, SHARE)
            sums += dot(e, u2t[pl.ds(CM * r, LANES), :])
        dinter[...] = jnp.zeros_like(dinter)
        dinter[pl.ds(HALF_TAPS, frames), :] = sums[:, :LANES]
        dinter[pl.ds(HALF_TAPS - 1, frames), :] += sums[:, LANES:]
        mels = jnp.concatenate([mel_a[...], mel_b[...]], 1)
        keep = lane_mask(first_rows)
        mel_sums = jnp.zeros((first_rows, 2 * LANES), F32)
        for r in range(HALF_TAPS):
            f = jnp.where(keep, dinter[pl.ds(r, first_rows, stride=HALF_TAPS), :], 0.0).astype(BF16)
            grads = dot_tn(f, mels)
            put(grads[:, :LANES], r, 0)
            put(grads[:, LANES:], r + HALF_TAPS, 0)
            mel_sums += dot(f, u1t[pl.ds(CM * r, LANES), :])
        zero = jnp.zeros((1, LANES), F32)
        mel_sum = jnp.concatenate([zero, mel_sums[:, :LANES]], 0) + jnp.concatenate([mel_sums[:, LANES:], zero], 0)
        real = mel_rows.shape[0]
        mel_rows[...] = mel_sum[2 : 2 + real]
        give_mel.start()
        halo[STEP:, :] = jnp.zeros_like(halo[STEP:, :])
        halo[STEP:, :LANES] = jnp.concatenate([mel_sum[:2], jnp.zeros((14, LANES), F32)], 0).astype(BF16)
        xg[2 * half + CM + 1 : 2 * half + CM + 2, :] = jnp.sum(g_sum[...], 0, keepdims=True)
        cwgt = xg[2 * half :, :].T
        dcond_all[: cwgt.shape[0], :] = cwgt

        def pack_small(a, _):
            for k, (out, side) in enumerate(((mine, core[0]), (theirs, 1 - core[0]))):
                for b in range(8):
                    at_row = pl.multiple_of(a * 128 + side * 64 + b * 8, 8)
                    narrow = du[pl.ds(pl.multiple_of(at_row * 5, 8), 2 * SHARE), :]
                    folded = fold(dcond_all[pl.ds(at_row, 8), :], narrow[:SHARE], narrow[SHARE:])
                    out[a * 8 + b, pl.ds(BIG, LINES - BIG), :] = folded.astype(BF16)
                give(a, k, BIG, LINES - BIG).start()
            return _

        lax.fori_loop(0, 8, pack_small, 0)

        def finish(a, _):
            for k in range(2):
                give(a, k, 0, BIG).wait()
                give(a, k, BIG, LINES - BIG).wait()
            return _

        lax.fori_loop(0, 8, finish, 0)
        give_mel.wait()


def main_pass(core, starts, seq_at, resets, mel_a, mel_b, tails, audio, g_res, g_skip, xt, gt, g_sum, own, other, tile):
    samples, width = audio.shape
    first_rows = mel_a.shape[0]

    def whole(shape):
        return pl.BlockSpec(shape, lambda i: (0,) * len(shape))

    anywhere = pl.BlockSpec(memory_space=pl.ANY)
    hbm = pl.BlockSpec(memory_space=pltpu.HBM)
    packed = (64, LINES, LANES)
    outs = [
        ((samples, 2 * width), BF16),
        ((samples, width), BF16),
        (packed, BF16),
        (packed, BF16),
        ((samples // (HALF_TAPS * HALF_TAPS), LANES), F32),
        ((STEP + 16, 2 * width), BF16),
    ]
    return pl.pallas_call(
        main_kernel,
        grid=(samples // tile,),
        in_specs=[pl.BlockSpec(memory_space=pltpu.SMEM)] * 3
        + [pl.BlockSpec((1, tile), lambda i: (0, i))]
        + [whole(mel_a.shape), whole(mel_b.shape), whole((STEP, width))]
        + [anywhere] * 5
        + [whole((8, 2 * width)), anywhere, anywhere],
        out_specs=[
            pl.BlockSpec((tile, 2 * width), lambda i: (i, 0)),
            pl.BlockSpec((tile, width), lambda i: (i, 0)),
        ]
        + [hbm] * 3
        + [whole(s) for s, _ in outs[5:]],
        out_shape=[roomy(s, d) if s == outs[4][0] else jax.ShapeDtypeStruct(s, d) for s, d in outs],
        scratch_shapes=[
            pltpu.VMEM((2 * width, 2 * width), BF16),
            pltpu.VMEM((2 * width, width), BF16),
            pltpu.VMEM((2 * width, LANES), BF16),
            pltpu.VMEM((HALF_TAPS * CM + 48, 2 * LANES), BF16),
            pltpu.VMEM((HALF_TAPS * CM + 48, 2 * LANES), BF16),
            pltpu.VMEM((LANES, 2 * width), BF16),
            pltpu.VMEM((first_rows * HALF_TAPS, LANES), F32),
            pltpu.VMEM((samples, LANES), F32),
            pltpu.VMEM((samples, LANES), F32),
            pltpu.VMEM((first_rows * HALF_TAPS, LANES), F32),
            pltpu.VMEM((2 * width + LANES, 2 * width), F32),
            pltpu.VMEM((2 * width, width), F32),
            pltpu.VMEM((2 * TAPS * CM, LANES), F32),
            pltpu.VMEM(packed, BF16),
            pltpu.VMEM(packed, BF16),
            pltpu.VMEM(outs[4][0], F32),
            pltpu.VMEM((2, tile + STEP, width), BF16),
            pltpu.VMEM((2, tile, width), BF16),
            pltpu.VMEM((2, tile, width), BF16),
            pltpu.VMEM((2, 2 * width, tile), BF16),
            pltpu.VMEM((2, 2 * width, tile), BF16),
            pltpu.SemaphoreType.DMA((2,)),
            pltpu.SemaphoreType.DMA((2, 2, 8)),
            pltpu.SemaphoreType.DMA,
            pltpu.SemaphoreType.DMA((2, 5)),
        ],
        compiler_params=pltpu.CompilerParams(vmem_limit_bytes=VMEM_BYTES),
        cost_estimate=pl.CostEstimate(
            flops=28_000_000_000, bytes_accessed=48 * samples * width, transcendentals=0
        ),
    )(core, starts, seq_at, resets, mel_a, mel_b, tails, audio, g_res, g_skip, xt, gt, g_sum, own, other)


def tail_kernel(
    core, dp, dp_next, gated, audio, g_res, mask, mask_next, own, other, pair,
    res_out, skip_out, res_grad, rest, wd_past,
    wd, wot, wct, ob, wdt, wo, mine, theirs, in_sems,
):
    step = pl.program_id(0)
    tile, half = audio.shape

    @pl.when(step == 0)
    def _():
        fetch = [pltpu.make_async_copy(a, b, in_sems.at[k]) for k, (a, b) in enumerate(((own, mine), (other, theirs)))]
        for copy in fetch:
            copy.start()
        for copy in fetch:
            copy.wait()

        def unpack(a, _):
            for ref, side in ((mine, core[0]), (theirs, 1 - core[0])):
                unpack_wide(ref, a, side, wd, wot)
                unpack_head(ref, a, side, wct)
            return _

        lax.fori_loop(0, 8, unpack, 0)
        ob[...] = wct[...].T[CM + 1 : CM + 2, :].astype(F32)
        wdt[...] = wd[...].T
        wo[...] = wot[...].T
        wd_past[...] = wdt[:, :half]

    out = dot(gated[...], wo[...]) + ob[...]
    res_out[...] = (audio[...].astype(F32) + out[:, :half]).astype(BF16)
    skip_out[...] = out[:, half:].astype(BF16)
    last = step == pl.num_programs(0) - 1
    after = jnp.where(last, jnp.zeros_like(dp_next[...]), dp_next[...])
    ahead = jnp.concatenate([dp[STEP:, :], after], 0)
    d_past = dot(ahead, wdt[:, :half]).astype(BF16)
    kept = jnp.concatenate([mask[STEP:, :], mask_next[...]], 0)
    d_past = (d_past * jnp.concatenate([kept] * (half // LANES), 1)).astype(F32)
    here = g_res[...].astype(F32) + dot(dp[...], wdt[:, half:])
    rest[...] = here[tile - STEP :, :]
    res_grad[...] = (here + d_past).astype(BF16)


def tail_pass(core, dp, gated, audio, g_res, mask, own, other, pair, tile):
    samples, width = audio.shape
    rows = pl.BlockSpec((tile, width), lambda i: (i, 0))
    anywhere = pl.BlockSpec(memory_space=pl.ANY)
    step_blocks = tile // STEP
    final = samples // STEP - 1

    def whole(shape):
        return pl.BlockSpec(shape, lambda i: (0,) * len(shape))

    shape = jax.ShapeDtypeStruct((samples, width), BF16)
    return pl.pallas_call(
        tail_kernel,
        grid=(samples // tile,),
        in_specs=[
            pl.BlockSpec(memory_space=pltpu.SMEM),
            pl.BlockSpec((tile, 2 * width), lambda i: (i, 0)),
            pl.BlockSpec((STEP, 2 * width), lambda i: (jnp.minimum((i + 1) * step_blocks, final), 0)),
            rows,
            rows,
            rows,
            pl.BlockSpec((tile, LANES), lambda i: (i, 0)),
            pl.BlockSpec((STEP, LANES), lambda i: (jnp.minimum((i + 1) * step_blocks, final), 0)),
            anywhere,
            anywhere,
            anywhere,
        ],
        out_specs=[rows] * 3 + [whole((STEP, width)), whole((2 * width, width))],
        out_shape=[shape] * 3
        + [roomy((STEP, width), F32), roomy((2 * width, width), BF16)],
        scratch_shapes=[
            pltpu.VMEM((2 * width, 2 * width), BF16),
            pltpu.VMEM((2 * width, width), BF16),
            pltpu.VMEM((2 * width, LANES), BF16),
            pltpu.VMEM((1, 2 * width), F32),
            pltpu.VMEM((2 * width, 2 * width), BF16),
            pltpu.VMEM((width, 2 * width), BF16),
            pltpu.VMEM(own.shape, BF16),
            pltpu.VMEM(own.shape, BF16),
            pltpu.SemaphoreType.DMA((2,)),
        ],
        compiler_params=pltpu.CompilerParams(vmem_limit_bytes=TAIL_VMEM_BYTES),
        cost_estimate=pl.CostEstimate(
            flops=13_000_000_000, bytes_accessed=20 * samples * width, transcendentals=0
        ),
    )(core, dp, dp, gated, audio, g_res, mask, mask, own, other, pair)


def end_kernel(
    grad, rest, halo, wd_past, mel_here, parts,
    out, mel_out, wd, wot, wct, u1t, u2t, gb, ob,
    total,
):
    step = pl.program_id(0)

    @pl.when(step == 0)
    def _():
        total[...] = jnp.zeros_like(total)
        out[...] = (rest[...] + dot(halo[:STEP, :], wd_past[...]).astype(BF16).astype(F32)).astype(BF16)
        frames = mel_here.shape[0]
        back = halo[STEP:, :LANES].astype(F32)[:2]
        mel = mel_here[...] + jnp.concatenate([jnp.zeros((frames - 2, LANES), F32), back], 0)
        mel_out[...] = mel[:, :CM].astype(BF16)

    total[...] += jnp.sum(parts[...].astype(F32), 0)

    @pl.when(step == pl.num_programs(0) - 1)
    def _():
        for j in range(8):
            wd[:, LANES * j : LANES * (j + 1)] = total[8 * j : 8 * j + 8, :]
        for j in range(4):
            wot[:, LANES * j : LANES * (j + 1)] = total[64 + 8 * j : 72 + 8 * j, :]
        head, u1, u2 = unfold(total[BIG:, :])
        wct[...] = head[:, :CM]
        u1t[...] = u1[:, :CM]
        u2t[...] = u2[:, :CM]
        diagonal = lax.broadcasted_iota(jnp.int32, (8, 8), 0) == lax.broadcasted_iota(jnp.int32, (8, 8), 1)
        for lane, row in ((CM, gb), (CM + 1, ob)):
            column = jnp.broadcast_to(head[:, lane : lane + 1], (8, 8))
            row[...] = jnp.sum(jnp.where(diagonal, column, 0.0), 0, keepdims=True)


def end_pass(grad, rest, halo, wd_past, mel_here, parts, frames):
    samples, width = grad.shape
    steps = 4
    shapes = [(8, 1024), (8, 512), (8, CM), (SHARE, CM), (SHARE, CM), (1, 8), (1, 8)]

    def whole(shape):
        return pl.BlockSpec(shape, lambda i: (0,) * len(shape))

    return pl.pallas_call(
        end_kernel,
        grid=(steps,),
        in_specs=[pl.BlockSpec(memory_space=pl.ANY)]
        + [whole(s) for s in ((STEP, width), halo.shape, (2 * width, width), (frames, LANES))]
        + [pl.BlockSpec((64 // steps, LINES, LANES), lambda i: (i, 0, 0))],
        out_specs=[pl.BlockSpec((STEP, width), lambda i: (samples // STEP - 1, 0))]
        + [whole(s) for s in [(frames, CM)] + shapes],
        out_shape=[jax.ShapeDtypeStruct(grad.shape, BF16), jax.ShapeDtypeStruct((frames, CM), BF16)]
        + [jax.ShapeDtypeStruct(s, F32) for s in shapes],
        scratch_shapes=[pltpu.VMEM((LINES, LANES), F32)],
        input_output_aliases={0: 0},
        compiler_params=pltpu.CompilerParams(vmem_limit_bytes=END_VMEM_BYTES),
    )(grad, rest, halo, wd_past, mel_here, parts)


def shifted(value, steps, count=8):
    first, last = max(0, -steps), min(count, count - steps)
    return lax.ppermute(value, SEQ, [(s, s + steps) for s in range(first, last)])


def no_change(value):
    return jnp.minimum(jnp.abs(value), 0)


def swap(value):
    return lax.ppermute(value, "c", [(0, 1), (1, 0)])


def on_device(
    residual_input, mel_input_frames, starts, resets, residual_gradient, skip_gradient,
    first_upsample_weight, second_upsample_weight, conditioning_weight, dilated_weight,
    gate_bias_vector, output_weight, output_bias_vector,
):
    core = lax.axis_index("c")
    audio, mel = residual_input[0], mel_input_frames[0]
    g_res, g_skip = residual_gradient[0], skip_gradient[0]
    samples, width = audio.shape
    frames = mel.shape[0]

    tails = jnp.concatenate([audio[-STEP:], jnp.pad(mel[-2:], ((0, 14), (0, width - CM)))], 0)
    tails = shifted(tails, 1)

    shares = spread(
        dilated_weight,
        output_weight.T,
        conditioning_weight.T,
        first_upsample_weight.T,
        second_upsample_weight.T,
        gate_bias_vector[None],
        output_bias_vector[None],
    )
    own = lax.all_to_all(shares, CHIPS, 0, 0)

    mel_tail = tails[STEP : STEP + 2, :CM]
    mel_ext = jnp.concatenate([mel_tail, mel, jnp.zeros((14, CM), BF16)], 0)
    mel_ext = jnp.pad(mel_ext, ((0, 0), (0, LANES - CM)))
    mel_b, mel_a = mel_ext[: 2 * frames - 8], mel_ext[1 : 2 * frames - 7]
    seq_at = lax.axis_index(SEQ).astype(jnp.int32)[None]
    mask, xt, gt, g_sum = turn(starts, seq_at, resets, audio, g_res, g_skip, 512)

    zeros = no_change(tails[STEP : STEP + 16, :LANES]) + no_change(gt[0, 0])
    own = lax.dynamic_update_slice(own, own[:1, :16] + zeros[None], (0, 0, 0))
    other = swap(own)

    core = core.astype(jnp.int32)[None]
    dp, gated, stay, send, mel_here, halo = main_pass(
        core, starts, seq_at, resets, mel_a, mel_b, tails, audio, g_res, g_skip, xt, gt, g_sum, own, other, 512
    )

    came = swap(send)
    pair = stay + came
    all_parts = lax.all_to_all(pair, CHIPS, 0, 0)

    halo_next = shifted(halo, -1)
    res_out, skip_out, res_grad, rest, wd_past = tail_pass(
        core, dp, gated, audio, g_res, mask, own, other, pair, 512
    )
    res_grad, mel_grad, d_wd, d_wot, d_wct, d_u1t, d_u2t, d_gb, d_ob = end_pass(
        res_grad, rest, halo_next, wd_past, mel_here, all_parts, frames
    )
    return (
        res_out[None],
        skip_out[None],
        res_grad[None],
        mel_grad[None],
        d_u1t.T,
        d_u2t.T,
        d_wct.T,
        d_wd,
        d_gb[0],
        d_wot.T,
        d_ob[0],
    )


def solution(mesh):
    fine = Mesh(mesh.devices.reshape(4, 2, 2, 2, 4), ("y", "xh", "c", "xl", "z"))
    dp, seq = ("y", "xh", "c"), ("xl", "z")
    every = dp + seq
    return jax.shard_map(
        on_device,
        mesh=fine,
        in_specs=(
            P(dp, seq, None),
            P(dp, seq, None),
            P(dp, None),
            P(dp, seq),
            P(dp, seq, None),
            P(dp, seq, None),
            P(None, every),
            P(None, every),
            P(None, every),
            P(every, None),
            P(every),
            P(None, every),
            P(every),
        ),
        out_specs=(
            P(dp, seq, None),
            P(dp, seq, None),
            P(dp, seq, None),
            P(dp, seq, None),
            P(None, every),
            P(None, every),
            P(None, every),
            P(every, None),
            P(every),
            P(None, every),
            P(every),
        ),
        check_vma=False,
    )
```

```python
import jax
import jax.numpy as jnp
from jax import lax
from jax.experimental import pallas as pl
from jax.experimental.pallas import tpu as pltpu
from jax.sharding import Mesh, PartitionSpec as P

STEP = 64
SEQ = ("xl", "z")
CHIPS = ("y", "xh", "xl", "z")
BF16 = jnp.bfloat16
F32 = jnp.float32
LANES = 128
TAPS = 32
HALF_TAPS = 16
CM = 80
SHARE = 20
LINES = 128
BIG = 96
VMEM_BYTES = 46 * 1024 * 1024
SIDE_VMEM_BYTES = 60 * 1024 * 1024
END_VMEM_BYTES = 50 * 1024 * 1024
TAIL_VMEM_BYTES = 58 * 1024 * 1024


def dot(a, b):
    return jnp.dot(a, b, preferred_element_type=F32)


def dot_nt(a, b):
    return lax.dot_general(a, b, (((1,), (1,)), ((), ())), preferred_element_type=F32)


def dot_tn(a, b):
    return lax.dot_general(a, b, (((0,), (0,)), ((), ())), preferred_element_type=F32)


def lane_mask(rows):
    return lax.broadcasted_iota(jnp.int32, (rows, LANES), 1) < CM


SPLIT = LANES - CM
PIECE = CM - SPLIT


def fold(head, u1, u2):
    u2 = jnp.concatenate([u2, jnp.zeros((4, LANES), F32)], 0)
    lane = lax.broadcasted_iota(jnp.int32, (24, LANES), 1)
    top = jnp.where(lane[:8] < LANES - PIECE, head, pltpu.roll(u2[:8], LANES - PIECE - SPLIT, 1))
    middle = jnp.where(lane[:SHARE] < CM, u1, pltpu.roll(u2, CM, 1)[:SHARE])
    last = jnp.zeros((3, LANES), F32)
    for g in range(4):
        moved = pltpu.roll(u2, (PIECE * g - SPLIT) % LANES, 1)[8 + 3 * g : 11 + 3 * g]
        last = jnp.where(lane[:3] // PIECE == g, moved, last)
    return jnp.concatenate([top, middle, last, jnp.zeros((1, LANES), F32)], 0)


def unfold(rows):
    lane = lax.broadcasted_iota(jnp.int32, (SHARE, LANES), 1)
    low = pltpu.roll(rows[8:], LANES - CM, 1)[:SHARE]
    high = [pltpu.roll(rows[:8], (SPLIT - LANES + PIECE) % LANES, 1)]
    for g in range(4):
        high.append(pltpu.roll(rows[24:], (SPLIT - PIECE * g) % LANES, 1)[4:7])
    u2 = jnp.where(lane < SPLIT, low, jnp.concatenate(high, 0))
    return rows[:8], rows[8 : 8 + SHARE], u2


def spread_kernel(wd, wot, wct, u1t, u2t, gb, ob, out, lines, narrow):
    for j in range(8):
        lines[8 * j : 8 * j + 8, :] = wd[:, LANES * j : LANES * (j + 1)].astype(F32)
    for j in range(4):
        lines[64 + 8 * j : 72 + 8 * j, :] = wot[:, LANES * j : LANES * (j + 1)].astype(F32)
    lane = lax.broadcasted_iota(jnp.int32, (8, LANES), 1)
    diagonal = lax.broadcasted_iota(jnp.int32, (8, 8), 0) == lax.broadcasted_iota(jnp.int32, (8, 8), 1)

    def column(row):
        full = jnp.broadcast_to(row[...].astype(F32), (8, 8))
        return jnp.sum(jnp.where(diagonal, full, 0.0), 1, keepdims=True)

    narrow[...] = jnp.zeros_like(narrow)
    narrow[:8, :CM] = wct[...].astype(F32)
    narrow[8 : 8 + SHARE, :CM] = u1t[...].astype(F32)
    narrow[32 : 32 + SHARE, :CM] = u2t[...].astype(F32)
    biases = jnp.where(lane == CM, column(gb), jnp.where(lane == CM + 1, column(ob), 0.0))
    lines[BIG:, :] = fold(narrow[:8, :] + biases, narrow[8 : 8 + SHARE, :], narrow[32 : 32 + SHARE, :])
    block = lines[...].astype(BF16)
    for k in range(out.shape[0]):
        out[k] = block


def spread(wd, wot, wct, u1t, u2t, gb, ob):
    return pl.pallas_call(
        spread_kernel,
        out_shape=jax.ShapeDtypeStruct((64, LINES, LANES), BF16),
        scratch_shapes=[pltpu.VMEM((LINES, LANES), F32), pltpu.VMEM((56, LANES), F32)],
    )(wd, wot, wct, u1t, u2t, gb, ob)


def masked_past(before, audio, column):
    tile, half = audio.shape
    moved = jnp.concatenate([before, audio[: tile - STEP, :]], 0)
    return moved * jnp.concatenate([column] * (half // LANES), 1)


def roomy(shape, dtype):
    rows = 16 * 1024 * 1024 // (shape[1] * jnp.dtype(dtype).itemsize)
    return jax.ShapeDtypeStruct((rows, shape[1]), dtype)


def keep_columns(starts, seq_at, resets):
    tile = resets.shape[1]
    span = seq_at[0] * pl.num_programs(0) + pl.program_id(0)
    position = span * tile + lax.broadcasted_iota(jnp.int32, (1, tile), 1)
    blocked = position < STEP
    for k in range(starts.shape[1]):
        first = starts[0, k]
        blocked = blocked | ((first > position - STEP) & (first <= position))
    keep = jnp.where(blocked, 0, resets[...]).astype(F32)
    return jnp.broadcast_to(keep, (LANES, tile)).T.astype(BF16)


def turn_kernel(starts, seq_at, resets, audio_before, audio, g_res, g_skip, mask, xt, gt, g_sum):
    step = pl.program_id(0)
    tile, half = audio.shape
    column = keep_columns(starts, seq_at, resets)
    mask[...] = column
    before = jnp.where(step == 0, jnp.zeros_like(audio_before[...]), audio_before[...])
    xt[:half, :] = masked_past(before, audio[...], column).T
    xt[half:, :] = audio[...].T
    gt[:half, :] = g_res[...].T
    gt[half:, :] = g_skip[...].T

    @pl.when(step == 0)
    def _():
        g_sum[...] = jnp.zeros_like(g_sum)

    g_sum[:, :half] += jnp.sum(g_res[...].astype(F32).reshape(tile // 8, 8, half), 0)
    g_sum[:, half:] += jnp.sum(g_skip[...].astype(F32).reshape(tile // 8, 8, half), 0)


def turn(starts, seq_at, resets, audio, g_res, g_skip, tile):
    samples, width = audio.shape
    steps = tile // STEP
    rows = pl.BlockSpec((tile, width), lambda i: (i, 0))
    cols = pl.BlockSpec((2 * width, tile), lambda i: (0, i))
    scalars = pl.BlockSpec(memory_space=pltpu.SMEM)
    shape = jax.ShapeDtypeStruct((2 * width, samples), BF16)
    return pl.pallas_call(
        turn_kernel,
        grid=(samples // tile,),
        in_specs=[
            scalars,
            scalars,
            pl.BlockSpec((1, tile), lambda i: (0, i)),
            pl.BlockSpec((STEP, width), lambda i: (jnp.maximum(i * steps - 1, 0), 0)),
            rows,
            rows,
            rows,
        ],
        out_specs=[
            pl.BlockSpec((tile, LANES), lambda i: (i, 0)),
            cols,
            cols,
            pl.BlockSpec((8, 2 * width), lambda i: (0, 0)),
        ],
        out_shape=[
            jax.ShapeDtypeStruct((samples, LANES), BF16),
            shape,
            shape,
            roomy((8, 2 * width), F32),
        ],
        compiler_params=pltpu.CompilerParams(vmem_limit_bytes=SIDE_VMEM_BYTES),
        cost_estimate=pl.CostEstimate(flops=0, bytes_accessed=18 * samples * width, transcendentals=0),
    )(starts, seq_at, resets, audio, audio, g_res, g_skip)


def unpack_wide(ref, a, side, wd, wot):
    for b in range(0, 8, 2):
        rows = pl.ds(pl.multiple_of(a * 128 + side * 64 + b * 8, 16), 16)
        pair = [a * 8 + b, a * 8 + b + 1]
        for out, first, count in ((wd, 0, 4), (wot, 64, 2)):
            for m in range(count):
                two = [ref[k, pl.ds(first + 16 * m, 16), :].astype(F32) for k in pair]
                out[rows, pl.ds(256 * m, 128)] = jnp.concatenate([t[:8] for t in two], 0).astype(BF16)
                out[rows, pl.ds(256 * m + 128, 128)] = jnp.concatenate([t[8:] for t in two], 0).astype(BF16)


def unpack_head(ref, a, side, wct):
    for b in range(0, 8, 2):
        rows = pl.ds(pl.multiple_of(a * 128 + side * 64 + b * 8, 16), 16)
        two = [ref[a * 8 + b + k, pl.ds(BIG, 16), :].astype(F32) for k in range(2)]
        wct[rows, :] = jnp.concatenate([t[:8] for t in two], 0).astype(BF16)


def main_kernel(
    core, starts, seq_at, resets, mel_a, mel_b, tails, audio_all, g_res_all, g_skip_all, xt_all, gt_all, g_sum, own, other,
    dp_out, gated_out, stay, send, mel_here, halo,
    wd, wot, wct, u1t, u2t, wc, inter, cond_all, dcond_all, dinter, xg, owg, du, mine, theirs, mel_rows,
    audio, g_res, g_skip, xt, gt, in_sems, out_sems, mel_sem, tile_sems,
):
    step = pl.program_id(0)
    steps = pl.num_programs(0)
    tile, half = g_res.shape[1:]
    frames = cond_all.shape[0] // HALF_TAPS
    first_rows = mel_a.shape[0]
    slot = lax.rem(step, 2)

    def tile_copies(i, to, lead):
        at = pl.multiple_of(i * tile, tile)
        rows, cols = pl.ds(at, tile), pl.ds(at, tile)
        audio_from = pl.ds(pl.multiple_of(i * tile - lead, STEP), tile + lead)
        pairs = (
            (audio_all.at[audio_from], audio.at[to, pl.ds(STEP - lead, tile + lead)]),
            (g_res_all.at[rows], g_res.at[to]),
            (g_skip_all.at[rows], g_skip.at[to]),
            (xt_all.at[:, cols], xt.at[to]),
            (gt_all.at[:, cols], gt.at[to]),
        )
        return [pltpu.make_async_copy(a, b, tile_sems.at[to, k]) for k, (a, b) in enumerate(pairs)]

    give_mel = pltpu.make_async_copy(mel_rows, mel_here.at[pl.ds(0, mel_rows.shape[0])], mel_sem)

    @pl.when(step == 0)
    def _():
        fetched = ((own, mine), (other, theirs))
        fetch = [pltpu.make_async_copy(a, b, in_sems.at[k]) for k, (a, b) in enumerate(fetched)]
        for copy in fetch:
            copy.start()
        audio[0, :STEP, :] = tails[...]
        xg[...] = jnp.zeros_like(xg)
        owg[...] = jnp.zeros_like(owg)
        u1t[HALF_TAPS * CM :, :] = jnp.zeros_like(u1t[HALF_TAPS * CM :, :])
        u2t[HALF_TAPS * CM :, :] = jnp.zeros_like(u2t[HALF_TAPS * CM :, :])
        for copy, ref, side in ((fetch[0], mine, core[0]), (fetch[1], theirs, 1 - core[0])):
            copy.wait()
            if ref is theirs:
                for other_copy in tile_copies(0, 0, 0):
                    other_copy.start()

            def unpack(a, _, ref=ref, side=side):
                unpack_wide(ref, a, side, wd, wot)
                unpack_head(ref, a, side, wct)
                for b in range(0, 8, 4):
                    tap_row = pl.multiple_of((a % 4 * 16 + side * 8 + b) * SHARE, 16)
                    lanes = pl.ds(pl.multiple_of(a // 4 * LANES, LANES), LANES)
                    four = [unfold(ref[a * 8 + b + k, pl.ds(BIG, 32), :].astype(F32)) for k in range(4)]
                    for k, out in ((1, u1t), (2, u2t)):
                        out[pl.ds(tap_row, CM), lanes] = jnp.concatenate([t[k] for t in four], 0).astype(BF16)
                return _

            lax.fori_loop(0, 8, unpack, 0)
        wc[...] = wct[...].T
        keep = lane_mask(first_rows)
        mels = jnp.concatenate([mel_a[...], mel_b[...]], 1)
        for r in range(HALF_TAPS):
            both = dot_nt(mels, u1t[pl.ds(CM * r, LANES), :])
            rounded = jnp.where(keep, both, 0.0).astype(BF16).astype(F32)
            inter[pl.ds(r, first_rows, stride=HALF_TAPS), :] = rounded
        rows_a = inter[pl.ds(HALF_TAPS, frames), :].astype(BF16)
        rows_b = inter[pl.ds(HALF_TAPS - 1, frames), :].astype(BF16)
        lane = lax.broadcasted_iota(jnp.int32, (frames, LANES), 1)
        one = jnp.where(lane == CM, 1.0, 0.0)
        rows_ab = jnp.concatenate([rows_a, rows_b], 1)
        for r in range(HALF_TAPS):
            both = dot_nt(rows_ab, u2t[pl.ds(CM * r, LANES), :])
            cond_all[pl.ds(r, frames, stride=HALF_TAPS), :] = jnp.where(lane < CM, both, one)

        for copy in tile_copies(0, 0, 0):
            copy.wait()

    @pl.when(step + 1 < steps)
    def _():
        for copy in tile_copies(step + 1, 1 - slot, STEP):
            copy.start()

    @pl.when(step > 0)
    def _():
        for copy in tile_copies(step, slot, STEP):
            copy.wait()

    at = pl.multiple_of(step * tile, tile)
    cond = cond_all[pl.ds(at, tile), :].astype(BF16)
    column = keep_columns(starts, seq_at, resets)
    past = audio[slot, :tile, :] * jnp.concatenate([column] * (half // LANES), 1)
    pre = dot(past, wd[:half, :]) + dot(audio[slot, STEP:, :], wd[half:, :]) + dot(cond, wc[...])
    th = jnp.tanh(pre[:, :half])
    sg = 0.5 * jnp.tanh(0.5 * pre[:, half:]) + 0.5
    gated = (th * sg).astype(BF16)
    gated_out[...] = gated
    dg = dot(g_res[slot], wot[:half, :]) + dot(g_skip[slot], wot[half:, :])
    dgs = dg * sg
    dp = jnp.concatenate([dgs * (1.0 - th * th), dgs * th * (1.0 - sg)], 1).astype(BF16)
    dp_out[...] = dp
    dcond_all[pl.ds(at, tile), :] = dot(dp, wct[...])
    owg[...] += dot(gt[slot], gated)
    xg[: 2 * half + 96, :] += dot(jnp.concatenate([xt[slot], cond.T[:96]], 0), dp)

    @pl.when(step == 0)
    def _():
        xg[:half, :] += dot_tn(past[:STEP, :], dp[:STEP, :])
        halo[:STEP, :] = dp[:STEP, :] * jnp.concatenate([column[:STEP, :]] * (2 * half // LANES), 1)

    @pl.when(step == pl.num_programs(0) - 1)
    def _():
        def give(a, k, first, count):
            part, lines = pl.ds(pl.multiple_of(a * 8, 8), 8), pl.ds(first, count)
            src, dst = ((mine, stay), (theirs, send))[k]
            return pltpu.make_async_copy(src.at[part, lines], dst.at[part, lines], out_sems.at[first // BIG, k, a])

        def pack_big(a, _):
            for k, (out, side) in enumerate(((mine, core[0]), (theirs, 1 - core[0]))):
                for b in range(8):
                    rows = pl.ds(pl.multiple_of(a * 128 + side * 64 + b * 8, 8), 8)
                    place = a * 8 + b
                    for m in range(4):
                        two = [xg[rows, pl.ds(256 * m, 128)], xg[rows, pl.ds(256 * m + 128, 128)]]
                        out[place, pl.ds(16 * m, 16), :] = jnp.concatenate(two, 0).astype(BF16)
                    for m in range(2):
                        two = [owg[rows, pl.ds(256 * m, 128)], owg[rows, pl.ds(256 * m + 128, 128)]]
                        out[place, pl.ds(64 + 16 * m, 16), :] = jnp.concatenate(two, 0).astype(BF16)
                give(a, k, 0, BIG).start()
            return _

        lax.fori_loop(0, 8, pack_big, 0)
        rows_a = inter[pl.ds(HALF_TAPS, frames), :].astype(BF16)
        rows_b = inter[pl.ds(HALF_TAPS - 1, frames), :].astype(BF16)
        both = jnp.concatenate([rows_a, rows_b], 1)
        keep = lane_mask(frames)
        sums = jnp.zeros((frames, 2 * LANES), F32)

        def put(grads, tap, first):
            for q in range(CM // SHARE):
                du[pl.ds((CM // SHARE * tap + q) * 2 * SHARE + first, SHARE), :] = grads[SHARE * q : SHARE * (q + 1)]

        for r in range(HALF_TAPS):
            e = jnp.where(keep, dcond_all[pl.ds(r, frames, stride=HALF_TAPS), :], 0.0).astype(BF16)
            grads = dot_tn(e, both)
            put(grads[:, :LANES], r, SHARE)
            put(grads[:, LANES:], r + HALF_TAPS, SHARE)
            sums += dot(e, u2t[pl.ds(CM * r, LANES), :])
        dinter[...] = jnp.zeros_like(dinter)
        dinter[pl.ds(HALF_TAPS, frames), :] = sums[:, :LANES]
        dinter[pl.ds(HALF_TAPS - 1, frames), :] += sums[:, LANES:]
        mels = jnp.concatenate([mel_a[...], mel_b[...]], 1)
        keep = lane_mask(first_rows)
        mel_sums = jnp.zeros((first_rows, 2 * LANES), F32)
        for r in range(HALF_TAPS):
            f = jnp.where(keep, dinter[pl.ds(r, first_rows, stride=HALF_TAPS), :], 0.0).astype(BF16)
            grads = dot_tn(f, mels)
            put(grads[:, :LANES], r, 0)
            put(grads[:, LANES:], r + HALF_TAPS, 0)
            mel_sums += dot(f, u1t[pl.ds(CM * r, LANES), :])
        zero = jnp.zeros((1, LANES), F32)
        mel_sum = jnp.concatenate([zero, mel_sums[:, :LANES]], 0) + jnp.concatenate([mel_sums[:, LANES:], zero], 0)
        real = mel_rows.shape[0]
        mel_rows[...] = mel_sum[2 : 2 + real]
        give_mel.start()
        halo[STEP:, :] = jnp.zeros_like(halo[STEP:, :])
        halo[STEP:, :LANES] = jnp.concatenate([mel_sum[:2], jnp.zeros((14, LANES), F32)], 0).astype(BF16)
        xg[2 * half + CM + 1 : 2 * half + CM + 2, :] = jnp.sum(g_sum[...], 0, keepdims=True)
        cwgt = xg[2 * half :, :].T
        dcond_all[: cwgt.shape[0], :] = cwgt

        def pack_small(a, _):
            for k, (out, side) in enumerate(((mine, core[0]), (theirs, 1 - core[0]))):
                for b in range(8):
                    at_row = pl.multiple_of(a * 128 + side * 64 + b * 8, 8)
                    narrow = du[pl.ds(pl.multiple_of(at_row * 5, 8), 2 * SHARE), :]
                    folded = fold(dcond_all[pl.ds(at_row, 8), :], narrow[:SHARE], narrow[SHARE:])
                    out[a * 8 + b, pl.ds(BIG, LINES - BIG), :] = folded.astype(BF16)
                give(a, k, BIG, LINES - BIG).start()
            return _

        lax.fori_loop(0, 8, pack_small, 0)

        def finish(a, _):
            for k in range(2):
                give(a, k, 0, BIG).wait()
                give(a, k, BIG, LINES - BIG).wait()
            return _

        lax.fori_loop(0, 8, finish, 0)
        give_mel.wait()


def main_pass(core, starts, seq_at, resets, mel_a, mel_b, tails, audio, g_res, g_skip, xt, gt, g_sum, own, other, tile):
    samples, width = audio.shape
    first_rows = mel_a.shape[0]

    def whole(shape):
        return pl.BlockSpec(shape, lambda i: (0,) * len(shape))

    anywhere = pl.BlockSpec(memory_space=pl.ANY)
    hbm = pl.BlockSpec(memory_space=pltpu.HBM)
    packed = (64, LINES, LANES)
    outs = [
        ((samples, 2 * width), BF16),
        ((samples, width), BF16),
        (packed, BF16),
        (packed, BF16),
        ((samples // (HALF_TAPS * HALF_TAPS), LANES), F32),
        ((STEP + 16, 2 * width), BF16),
    ]
    return pl.pallas_call(
        main_kernel,
        grid=(samples // tile,),
        in_specs=[pl.BlockSpec(memory_space=pltpu.SMEM)] * 3
        + [pl.BlockSpec((1, tile), lambda i: (0, i))]
        + [whole(mel_a.shape), whole(mel_b.shape), whole((STEP, width))]
        + [anywhere] * 5
        + [whole((8, 2 * width)), anywhere, anywhere],
        out_specs=[
            pl.BlockSpec((tile, 2 * width), lambda i: (i, 0)),
            pl.BlockSpec((tile, width), lambda i: (i, 0)),
        ]
        + [hbm] * 3
        + [whole(s) for s, _ in outs[5:]],
        out_shape=[roomy(s, d) if s == outs[4][0] else jax.ShapeDtypeStruct(s, d) for s, d in outs],
        scratch_shapes=[
            pltpu.VMEM((2 * width, 2 * width), BF16),
            pltpu.VMEM((2 * width, width), BF16),
            pltpu.VMEM((2 * width, LANES), BF16),
            pltpu.VMEM((HALF_TAPS * CM + 48, 2 * LANES), BF16),
            pltpu.VMEM((HALF_TAPS * CM + 48, 2 * LANES), BF16),
            pltpu.VMEM((LANES, 2 * width), BF16),
            pltpu.VMEM((first_rows * HALF_TAPS, LANES), F32),
            pltpu.VMEM((samples, LANES), F32),
            pltpu.VMEM((samples, LANES), F32),
            pltpu.VMEM((first_rows * HALF_TAPS, LANES), F32),
            pltpu.VMEM((2 * width + LANES, 2 * width), F32),
            pltpu.VMEM((2 * width, width), F32),
            pltpu.VMEM((2 * TAPS * CM, LANES), F32),
            pltpu.VMEM(packed, BF16),
            pltpu.VMEM(packed, BF16),
            pltpu.VMEM(outs[4][0], F32),
            pltpu.VMEM((2, tile + STEP, width), BF16),
            pltpu.VMEM((2, tile, width), BF16),
            pltpu.VMEM((2, tile, width), BF16),
            pltpu.VMEM((2, 2 * width, tile), BF16),
            pltpu.VMEM((2, 2 * width, tile), BF16),
            pltpu.SemaphoreType.DMA((2,)),
            pltpu.SemaphoreType.DMA((2, 2, 8)),
            pltpu.SemaphoreType.DMA,
            pltpu.SemaphoreType.DMA((2, 5)),
        ],
        compiler_params=pltpu.CompilerParams(vmem_limit_bytes=VMEM_BYTES),
        cost_estimate=pl.CostEstimate(
            flops=28_000_000_000, bytes_accessed=48 * samples * width, transcendentals=0
        ),
    )(core, starts, seq_at, resets, mel_a, mel_b, tails, audio, g_res, g_skip, xt, gt, g_sum, own, other)


def tail_kernel(
    core, dp, dp_next, gated, audio, g_res, mask, mask_next, own, other, pair,
    res_out, skip_out, res_grad, rest, wd_past,
    wd, wot, wct, ob, wdt, wo, mine, theirs, in_sems,
):
    step = pl.program_id(0)
    tile, half = audio.shape

    @pl.when(step == 0)
    def _():
        fetch = [pltpu.make_async_copy(a, b, in_sems.at[k]) for k, (a, b) in enumerate(((own, mine), (other, theirs)))]
        for copy in fetch:
            copy.start()
        for copy in fetch:
            copy.wait()

        def unpack(a, _):
            for ref, side in ((mine, core[0]), (theirs, 1 - core[0])):
                unpack_wide(ref, a, side, wd, wot)
                unpack_head(ref, a, side, wct)
            return _

        lax.fori_loop(0, 8, unpack, 0)
        ob[...] = wct[...].T[CM + 1 : CM + 2, :].astype(F32)
        wdt[...] = wd[...].T
        wo[...] = wot[...].T
        wd_past[...] = wdt[:, :half]

    out = dot(gated[...], wo[...]) + ob[...]
    res_out[...] = (audio[...].astype(F32) + out[:, :half]).astype(BF16)
    skip_out[...] = out[:, half:].astype(BF16)
    last = step == pl.num_programs(0) - 1
    after = jnp.where(last, jnp.zeros_like(dp_next[...]), dp_next[...])
    ahead = jnp.concatenate([dp[STEP:, :], after], 0)
    d_past = dot(ahead, wdt[:, :half]).astype(BF16)
    kept = jnp.concatenate([mask[STEP:, :], mask_next[...]], 0)
    d_past = (d_past * jnp.concatenate([kept] * (half // LANES), 1)).astype(F32)
    here = g_res[...].astype(F32) + dot(dp[...], wdt[:, half:])
    rest[...] = here[tile - STEP :, :]
    res_grad[...] = (here + d_past).astype(BF16)


def tail_pass(core, dp, gated, audio, g_res, mask, own, other, pair, tile):
    samples, width = audio.shape
    rows = pl.BlockSpec((tile, width), lambda i: (i, 0))
    anywhere = pl.BlockSpec(memory_space=pl.ANY)
    step_blocks = tile // STEP
    final = samples // STEP - 1

    def whole(shape):
        return pl.BlockSpec(shape, lambda i: (0,) * len(shape))

    shape = jax.ShapeDtypeStruct((samples, width), BF16)
    return pl.pallas_call(
        tail_kernel,
        grid=(samples // tile,),
        in_specs=[
            pl.BlockSpec(memory_space=pltpu.SMEM),
            pl.BlockSpec((tile, 2 * width), lambda i: (i, 0)),
            pl.BlockSpec((STEP, 2 * width), lambda i: (jnp.minimum((i + 1) * step_blocks, final), 0)),
            rows,
            rows,
            rows,
            pl.BlockSpec((tile, LANES), lambda i: (i, 0)),
            pl.BlockSpec((STEP, LANES), lambda i: (jnp.minimum((i + 1) * step_blocks, final), 0)),
            anywhere,
            anywhere,
            anywhere,
        ],
        out_specs=[rows] * 3 + [whole((STEP, width)), whole((2 * width, width))],
        out_shape=[shape] * 3
        + [roomy((STEP, width), F32), roomy((2 * width, width), BF16)],
        scratch_shapes=[
            pltpu.VMEM((2 * width, 2 * width), BF16),
            pltpu.VMEM((2 * width, width), BF16),
            pltpu.VMEM((2 * width, LANES), BF16),
            pltpu.VMEM((1, 2 * width), F32),
            pltpu.VMEM((2 * width, 2 * width), BF16),
            pltpu.VMEM((width, 2 * width), BF16),
            pltpu.VMEM(own.shape, BF16),
            pltpu.VMEM(own.shape, BF16),
            pltpu.SemaphoreType.DMA((2,)),
        ],
        compiler_params=pltpu.CompilerParams(vmem_limit_bytes=TAIL_VMEM_BYTES),
        cost_estimate=pl.CostEstimate(
            flops=13_000_000_000, bytes_accessed=20 * samples * width, transcendentals=0
        ),
    )(core, dp, dp, gated, audio, g_res, mask, mask, own, other, pair)


def end_kernel(
    grad, rest, halo, wd_past, mel_here, parts,
    out, mel_out, wd, wot, wct, u1t, u2t, gb, ob,
    total,
):
    step = pl.program_id(0)

    @pl.when(step == 0)
    def _():
        total[...] = jnp.zeros_like(total)
        out[...] = (rest[...] + dot(halo[:STEP, :], wd_past[...]).astype(BF16).astype(F32)).astype(BF16)
        frames = mel_here.shape[0]
        back = halo[STEP:, :LANES].astype(F32)[:2]
        mel = mel_here[...] + jnp.concatenate([jnp.zeros((frames - 2, LANES), F32), back], 0)
        mel_out[...] = mel[:, :CM].astype(BF16)

    total[...] += jnp.sum(parts[...].astype(F32), 0)

    @pl.when(step == pl.num_programs(0) - 1)
    def _():
        for j in range(8):
            wd[:, LANES * j : LANES * (j + 1)] = total[8 * j : 8 * j + 8, :]
        for j in range(4):
            wot[:, LANES * j : LANES * (j + 1)] = total[64 + 8 * j : 72 + 8 * j, :]
        head, u1, u2 = unfold(total[BIG:, :])
        wct[...] = head[:, :CM]
        u1t[...] = u1[:, :CM]
        u2t[...] = u2[:, :CM]
        diagonal = lax.broadcasted_iota(jnp.int32, (8, 8), 0) == lax.broadcasted_iota(jnp.int32, (8, 8), 1)
        for lane, row in ((CM, gb), (CM + 1, ob)):
            column = jnp.broadcast_to(head[:, lane : lane + 1], (8, 8))
            row[...] = jnp.sum(jnp.where(diagonal, column, 0.0), 0, keepdims=True)


def end_pass(grad, rest, halo, wd_past, mel_here, parts, frames):
    samples, width = grad.shape
    steps = 2
    shapes = [(8, 1024), (8, 512), (8, CM), (SHARE, CM), (SHARE, CM), (1, 8), (1, 8)]

    def whole(shape):
        return pl.BlockSpec(shape, lambda i: (0,) * len(shape))

    return pl.pallas_call(
        end_kernel,
        grid=(steps,),
        in_specs=[pl.BlockSpec(memory_space=pl.ANY)]
        + [whole(s) for s in ((STEP, width), halo.shape, (2 * width, width), (frames, LANES))]
        + [pl.BlockSpec((64 // steps, LINES, LANES), lambda i: (i, 0, 0))],
        out_specs=[pl.BlockSpec((STEP, width), lambda i: (samples // STEP - 1, 0))]
        + [whole(s) for s in [(frames, CM)] + shapes],
        out_shape=[jax.ShapeDtypeStruct(grad.shape, BF16), jax.ShapeDtypeStruct((frames, CM), BF16)]
        + [jax.ShapeDtypeStruct(s, F32) for s in shapes],
        scratch_shapes=[pltpu.VMEM((LINES, LANES), F32)],
        input_output_aliases={0: 0},
        compiler_params=pltpu.CompilerParams(vmem_limit_bytes=END_VMEM_BYTES),
    )(grad, rest, halo, wd_past, mel_here, parts)


def shifted(value, steps, count=8):
    first, last = max(0, -steps), min(count, count - steps)
    return lax.ppermute(value, SEQ, [(s, s + steps) for s in range(first, last)])


def no_change(value):
    return jnp.minimum(jnp.abs(value), 0)


def swap(value):
    return lax.ppermute(value, "c", [(0, 1), (1, 0)])


def on_device(
    residual_input, mel_input_frames, starts, resets, residual_gradient, skip_gradient,
    first_upsample_weight, second_upsample_weight, conditioning_weight, dilated_weight,
    gate_bias_vector, output_weight, output_bias_vector,
):
    core = lax.axis_index("c")
    audio, mel = residual_input[0], mel_input_frames[0]
    g_res, g_skip = residual_gradient[0], skip_gradient[0]
    samples, width = audio.shape
    frames = mel.shape[0]

    tails = jnp.concatenate([audio[-STEP:], jnp.pad(mel[-2:], ((0, 14), (0, width - CM)))], 0)
    tails = shifted(tails, 1)

    shares = spread(
        dilated_weight,
        output_weight.T,
        conditioning_weight.T,
        first_upsample_weight.T,
        second_upsample_weight.T,
        gate_bias_vector[None],
        output_bias_vector[None],
    )
    own = lax.all_to_all(shares, CHIPS, 0, 0)

    mel_tail = tails[STEP : STEP + 2, :CM]
    mel_ext = jnp.concatenate([mel_tail, mel, jnp.zeros((14, CM), BF16)], 0)
    mel_ext = jnp.pad(mel_ext, ((0, 0), (0, LANES - CM)))
    mel_b, mel_a = mel_ext[: 2 * frames - 8], mel_ext[1 : 2 * frames - 7]
    seq_at = lax.axis_index(SEQ).astype(jnp.int32)[None]
    mask, xt, gt, g_sum = turn(starts, seq_at, resets, audio, g_res, g_skip, 512)

    zeros = no_change(tails[STEP : STEP + 16, :LANES]) + no_change(gt[0, 0])
    own = lax.dynamic_update_slice(own, own[:1, :16] + zeros[None], (0, 0, 0))
    other = swap(own)

    core = core.astype(jnp.int32)[None]
    dp, gated, stay, send, mel_here, halo = main_pass(
        core, starts, seq_at, resets, mel_a, mel_b, tails, audio, g_res, g_skip, xt, gt, g_sum, own, other, 512
    )

    came = swap(send)
    pair = stay + came
    all_parts = lax.all_to_all(pair, CHIPS, 0, 0)

    halo_next = shifted(halo, -1)
    res_out, skip_out, res_grad, rest, wd_past = tail_pass(
        core, dp, gated, audio, g_res, mask, own, other, pair, 512
    )
    res_grad, mel_grad, d_wd, d_wot, d_wct, d_u1t, d_u2t, d_gb, d_ob = end_pass(
        res_grad, rest, halo_next, wd_past, mel_here, all_parts, frames
    )
    return (
        res_out[None],
        skip_out[None],
        res_grad[None],
        mel_grad[None],
        d_u1t.T,
        d_u2t.T,
        d_wct.T,
        d_wd,
        d_gb[0],
        d_wot.T,
        d_ob[0],
    )


def solution(mesh):
    fine = Mesh(mesh.devices.reshape(4, 2, 2, 2, 4), ("y", "xh", "c", "xl", "z"))
    dp, seq = ("y", "xh", "c"), ("xl", "z")
    every = dp + seq
    return jax.shard_map(
        on_device,
        mesh=fine,
        in_specs=(
            P(dp, seq, None),
            P(dp, seq, None),
            P(dp, None),
            P(dp, seq),
            P(dp, seq, None),
            P(dp, seq, None),
            P(None, every),
            P(None, every),
            P(None, every),
            P(every, None),
            P(every),
            P(None, every),
            P(every),
        ),
        out_specs=(
            P(dp, seq, None),
            P(dp, seq, None),
            P(dp, seq, None),
            P(dp, seq, None),
            P(None, every),
            P(None, every),
            P(None, every),
            P(every, None),
            P(every),
            P(None, every),
            P(every),
        ),
        check_vma=False,
    )
```
